32 devices in a mesh: rows: 4 (over z), cols: 8 (over y, x, core).
Axes of the slice: x: 2, y: 2, z: 4, core: 2. Of those that a mesh axis runs over, the one named last changes fastest.
Arguments:
- features: bfloat16 [16384, 256], P(('rows', 'cols')), may hold values from -6 to 6
- coords: float32 [3, 16384], P(None, ('rows', 'cols')), may hold values from -6 to 6
- valid_mask: int32 [16384], P(('rows', 'cols')), may hold values from 0 to 1, as said below
- neighbors: int32 [16, 16384], P(None, ('rows', 'cols')), may hold values from 0 to 511, as said below
- cotangent: bfloat16 [16384, 256], P(('rows', 'cols')), may hold values from -6 to 6
- weights: bfloat16 [338784], replicated
- master: float32 [338784], P(('rows', 'cols'))
- first_moment: float32 [338784], P(('rows', 'cols'))
- second_moment: float32 [338784], P(('rows', 'cols')), as said below
Outputs:
- block_out: bfloat16 [16384, 256], P(('rows', 'cols'))
- grad_features: bfloat16 [16384, 256], P(('rows', 'cols'))
- grad_norm: float32 [], replicated
- new_master: float32 [338784], P(('rows', 'cols'))
- new_first: float32 [338784], P(('rows', 'cols'))
- new_second: float32 [338784], P(('rows', 'cols'))
- new_weights: bfloat16 [338784], replicated
The draws below stay inside these ranges and needn't reach their ends.
Inputs may be any that keep to these rules, and one draw needn't show every extreme that they name: `valid_mask`: the real points of each device are its first slots; each device has at least 64 of them, and some device has all 512. `neighbors`: indices of rows of the point's own device; the first neighbour of each point is the point itself, and every neighbour lies within 48 rows of it. `second_moment`: Positive.
All inputs are finite; a program needn't handle non-finite values.
Results may differ from the reference program's by a relative error of at most 0.0097.
Values may be sent and summed in bfloat16 or wider, within the bound.
A program may use at most 192 MiB of HBM per device.

```python
import math
import jax
import jax.numpy as jnp
from jax import lax

WIDTH = 256
GROUPS = 32
NEAREST = 16
POINTS_DEV = 512
POINTS = 16384
NORM_PARAMS = 547
PARAMS = 338767
PARAMS_PAD = 338784


clip_level = 0.01


def block_count():
    return POINTS // POINTS_DEV


def draw_valid_mask(key, part):
    blocks = block_count()
    lengths = jax.random.randint(jax.random.fold_in(key, 17), (blocks,), max(POINTS_DEV // 8, 1), POINTS_DEV + 1)
    lengths = lengths.at[0].set(POINTS_DEV)
    rows_local = jnp.arange(POINTS_DEV, dtype=jnp.int32)
    return (rows_local[None, :] < lengths[:, None]).astype(jnp.int32).reshape(POINTS)


def draw_neighbors(key, part):
    blocks = block_count()
    reach = min(48, POINTS_DEV)
    offsets = jax.random.randint(jax.random.fold_in(key, 29), (NEAREST, blocks, POINTS_DEV), -reach, reach + 1)
    rows_local = jnp.arange(POINTS_DEV, dtype=jnp.int32)
    chosen = jnp.clip(rows_local[None, None, :] + offsets, 0, POINTS_DEV - 1)
    chosen = chosen.at[0].set(jnp.broadcast_to(rows_local[None, :], (blocks, POINTS_DEV)))
    return chosen.reshape(NEAREST, POINTS).astype(jnp.int32)


def param_law(key):
    keys_all = jax.random.split(key, 8)
    square_part = jax.random.normal(keys_all[0], (5 * WIDTH * WIDTH,)) / math.sqrt(WIDTH)
    att_in_part = jax.random.normal(keys_all[1], (WIDTH * GROUPS,)) / math.sqrt(WIDTH)
    att_out_part = jax.random.normal(keys_all[2], (GROUPS * GROUPS,)) * (2.5 / math.sqrt(GROUPS))
    pos_in_part = jax.random.normal(keys_all[3], (9,)) / math.sqrt(3.0)
    pos_out_part = jax.random.normal(keys_all[4], (3 * WIDTH,)) / math.sqrt(3.0)
    gain_part = jax.random.uniform(keys_all[5], (NORM_PARAMS,), minval=0.6, maxval=1.4)
    shift_part = 0.3 * jax.random.normal(keys_all[6], (NORM_PARAMS,))
    padding = 0.05 * jax.random.normal(keys_all[7], (PARAMS_PAD - PARAMS,))
    return jnp.concatenate([square_part, att_in_part, att_out_part, pos_in_part, pos_out_part, gain_part, shift_part, padding]).astype(jnp.float32)


def draw_weights(key, part):
    return param_law(jax.random.fold_in(key, 41)).astype(jnp.bfloat16)


def draw_master(key, part):
    return param_law(jax.random.fold_in(key, 43))


def draw_first_moment(key, part):
    grad_scale = clip_level / math.sqrt(PARAMS)
    return (jax.random.normal(jax.random.fold_in(key, 47), (PARAMS_PAD,)) * (0.1 / 0.9) * grad_scale).astype(jnp.float32)


def draw_second_moment(key, part):
    grad_scale = clip_level / math.sqrt(PARAMS)
    first_factor = jax.random.uniform(jax.random.fold_in(key, 53), (PARAMS_PAD,), minval=1.0, maxval=4.0)
    second_factor = jnp.exp(jax.random.uniform(jax.random.fold_in(key, 59), (PARAMS_PAD,), minval=math.log(0.5), maxval=math.log(2.0)))
    return (first_factor * second_factor * (0.001 / 0.999) * grad_scale * grad_scale).astype(jnp.float32)


def levels(key, dims, cuts, smallest, largest):
    loudness = 1.0
    for axis_at, blocks in cuts:
        steps = jax.random.uniform(jax.random.fold_in(jax.random.fold_in(key, 6), axis_at), (blocks,), jnp.float32, smallest / len(cuts), largest / len(cuts))
        loudness = loudness * jnp.repeat(jnp.exp(steps), dims[axis_at] // blocks).reshape((-1,) + (1,) * (len(dims) - 1 - axis_at))
    return loudness


def gaussian(own_key, extent, deviation, most, pieces=(), held_as=jnp.bfloat16):
    loudness = levels(own_key, extent, pieces, -0.22, 0.18) if pieces else 1.0
    array = jax.random.normal(own_key, extent, jnp.float32) * deviation * loudness
    return jnp.minimum(jnp.maximum(array, -most), most).astype(held_as)


def setup_inputs(seed: int = 0) -> dict:
    keys = jax.random.split(jax.random.key(seed), 10)
    return {
        "features": gaussian(keys[0], (POINTS, WIDTH), 1.0, 6.0, ((0, 32),)),
        "coords": gaussian(keys[1], (3, POINTS), 1.0, 6.0, ((1, 32),), jnp.float32),
        "valid_mask": draw_valid_mask(jax.random.fold_in(keys[9], 71), 0),
        "neighbors": draw_neighbors(jax.random.fold_in(keys[9], 71), 0),
        "cotangent": gaussian(keys[4], (POINTS, WIDTH), 1.0, 6.0, ((0, 32),)),
        "weights": draw_weights(jax.random.fold_in(keys[9], 71), 0),
        "master": draw_master(jax.random.fold_in(keys[9], 71), 0),
        "first_moment": draw_first_moment(jax.random.fold_in(keys[9], 71), 0),
        "second_moment": draw_second_moment(jax.random.fold_in(keys[9], 71), 0),
    }


@jax.custom_vjp
def low(v):
    return lax.optimization_barrier(v.astype(jnp.bfloat16)).astype(jnp.float32)

@jax.custom_vjp
def low_back(v):
    return v

def low_keep(v):
    return (low(v), None)

def low_pass(kept, grad):
    return (grad,)

def back_keep(v):
    return (v, None)

def back_low(kept, grad):
    return (low(grad),)
low.defvjp(low_keep, low_pass)
low_back.defvjp(back_keep, back_low)
bn_eps = 1e-05
clip_norm = 0.01
learn_rate = 0.05
beta_one = 0.9
beta_two = 0.999
adam_eps = 1e-08
decay_rate = 0.01
step_count = 10
masked_logit = -1000000000.0
highest = lax.Precision.HIGHEST

def split_params(packed):
    square_size = WIDTH * WIDTH
    norm_size = 2 * WIDTH + 3 + GROUPS
    squares = packed[0:5 * square_size].reshape(5, WIDTH, WIDTH)
    offset = 5 * square_size
    att_in = packed[offset:offset + WIDTH * GROUPS].reshape(WIDTH, GROUPS)
    offset = offset + WIDTH * GROUPS
    att_out = packed[offset:offset + GROUPS * GROUPS].reshape(GROUPS, GROUPS)
    offset = offset + GROUPS * GROUPS
    pos_in = packed[offset:offset + 9].reshape(3, 3)
    offset = offset + 9
    pos_out = packed[offset:offset + 3 * WIDTH].reshape(3, WIDTH)
    offset = offset + 3 * WIDTH
    scales = packed[offset:offset + norm_size]
    offset = offset + norm_size
    shifts = packed[offset:offset + norm_size]
    return (squares, att_in, att_out, pos_in, pos_out, scales, shifts)

def norm_parts(vector):
    return (vector[0:WIDTH], vector[WIDTH:WIDTH + 3], vector[WIDTH + 3:WIDTH + 3 + GROUPS], vector[WIDTH + 3 + GROUPS:2 * WIDTH + 3 + GROUPS])

def normalize(sample, sum_one, sum_two, members, factor, offset):
    center = sum_one / members
    spread = sum_two / members - center * center
    return factor * (sample - center) * lax.rsqrt(spread + bn_eps) + offset

def gather_rows(source_table, indices):
    return source_table[indices]

def adam_update(param, moment, second, grad):
    moment_new = beta_one * moment + (1.0 - beta_one) * grad
    second_new = beta_two * second + (1.0 - beta_two) * grad * grad
    moment_hat = moment_new / (1.0 - beta_one ** step_count)
    second_hat = second_new / (1.0 - beta_two ** step_count)
    param_new = param - learn_rate * (moment_hat / (jnp.sqrt(second_hat) + adam_eps) + decay_rate * param)
    return (param_new, moment_new, second_new)

def reference(features, coords, valid_mask, neighbors, cotangent, weights, master, first_moment, second_moment):
    blocks = POINTS // POINTS_DEV
    feature_blocks = features.astype(jnp.float32).reshape(blocks, POINTS_DEV, WIDTH)
    coord_blocks = coords.reshape(3, blocks, POINTS_DEV).transpose(1, 0, 2)
    valid_blocks = valid_mask.astype(jnp.float32).reshape(blocks, POINTS_DEV)
    neighbor_blocks = neighbors.reshape(NEAREST, blocks, POINTS_DEV).transpose(1, 2, 0).astype(jnp.int32)
    neighbor_valid = jax.vmap(gather_rows)(valid_blocks, neighbor_blocks)
    pair_valid = valid_blocks[:, :, None] * neighbor_valid
    first_slot = (lax.broadcasted_iota(jnp.int32, (POINTS_DEV, NEAREST), 1) == 0).astype(jnp.float32)
    allowed_blocks = jnp.maximum(neighbor_valid, first_slot[None])
    point_count = jnp.sum(valid_blocks)
    pair_count = jnp.sum(pair_valid)
    point_mask = valid_blocks[:, :, None]

    def forward(packed, inputs_all):
        squares, att_in, att_out, pos_in, pos_out, scales, shifts = split_params(packed)
        gain_one, gain_pos, gain_att, gain_out = norm_parts(scales)
        shift_one, shift_pos, shift_att, shift_out = norm_parts(shifts)

        def first_section(items):
            source, coord_block, neighbor_rows = items
            pre_one = low_back(jnp.dot(source, squares[0], precision=highest))
            rel_pos = coord_block[:, neighbor_rows] - coord_block[:, :, None]
            pos_pre = jnp.einsum('cpk,cd->dpk', rel_pos, pos_in, precision=highest)
            return (pre_one, pos_pre)
        pre_ones, pos_pres = lax.map(jax.checkpoint(first_section), (inputs_all, coord_blocks, neighbor_blocks))
        sum_a = lax.optimization_barrier(jnp.sum(point_mask * pre_ones, axis=(0, 1)))
        sqr_a = lax.optimization_barrier(jnp.sum(point_mask * pre_ones * pre_ones, axis=(0, 1)))
        sum_p = lax.optimization_barrier(jnp.sum(pair_valid[:, None] * pos_pres, axis=(0, 2, 3)))
        sqr_p = lax.optimization_barrier(jnp.sum(pair_valid[:, None] * pos_pres * pos_pres, axis=(0, 2, 3)))

        def hidden_of(pre_one):
            return low(jax.nn.silu(normalize(pre_one, sum_a, sqr_a, point_count, gain_one, shift_one)))

        def encode(pos_pre):
            pos_act = jax.nn.silu(normalize(pos_pre, sum_p[:, None, None], sqr_p[:, None, None], pair_count, gain_pos[:, None, None], shift_pos[:, None, None]))
            return jnp.einsum('cpk,cd->pkd', pos_act, pos_out, precision=highest)

        def second_section(items):
            pre_one, pos_pre, neighbor_rows = items
            hidden = hidden_of(pre_one)
            queries = low(low_back(jnp.dot(hidden, squares[1], precision=highest)))
            key_rows = low(low_back(jnp.dot(hidden, squares[2], precision=highest)))
            relation = queries[:, None, :] - key_rows[neighbor_rows] + encode(pos_pre)
            return low_back(jnp.einsum('pkc,cg->pkg', low(relation), att_in, precision=highest))
        pre_atts = lax.map(jax.checkpoint(second_section), (pre_ones, pos_pres, neighbor_blocks))
        sum_w = lax.optimization_barrier(jnp.sum(pair_valid[..., None] * pre_atts, axis=(0, 1, 2)))
        sqr_w = lax.optimization_barrier(jnp.sum(pair_valid[..., None] * pre_atts * pre_atts, axis=(0, 1, 2)))

        def third_section(items):
            pre_one, pos_pre, pre_att, allowed, neighbor_rows = items
            hidden = hidden_of(pre_one)
            values = low(low_back(jnp.dot(hidden, squares[3], precision=highest)))
            encoding = encode(pos_pre)
            activ = low(jax.nn.silu(normalize(pre_att, sum_w, sqr_w, pair_count, gain_att, shift_att)))
            logits = low_back(jnp.einsum('pkg,gh->pkh', activ, att_out, precision=highest))
            masked = jnp.where(allowed[:, :, None] > 0.5, logits, masked_logit)
            top_val = lax.optimization_barrier(jnp.max(masked, axis=1, keepdims=True))
            expon = jnp.exp(masked - top_val)
            attention = expon / lax.optimization_barrier(jnp.sum(expon, axis=1, keepdims=True))
            mixed = (values[neighbor_rows] + encoding).reshape(POINTS_DEV, NEAREST, GROUPS, WIDTH // GROUPS)
            attended = jnp.einsum('pkg,pkgc->pgc', attention, mixed, precision=highest).reshape(POINTS_DEV, WIDTH)
            return low_back(jnp.dot(low(attended), squares[4], precision=highest))
        pre_outs = lax.map(jax.checkpoint(third_section), (pre_ones, pos_pres, pre_atts, allowed_blocks, neighbor_blocks))
        sum_o = lax.optimization_barrier(jnp.sum(point_mask * pre_outs, axis=(0, 1)))
        sqr_o = lax.optimization_barrier(jnp.sum(point_mask * pre_outs * pre_outs, axis=(0, 1)))
        return point_mask * jax.nn.silu(inputs_all + normalize(pre_outs, sum_o, sqr_o, point_count, gain_out, shift_out))
    outputs, pullback = jax.vjp(forward, weights.astype(jnp.float32), feature_blocks)
    grad_weights, grad_inputs = pullback(cotangent.astype(jnp.float32).reshape(blocks, POINTS_DEV, WIDTH))
    norm_value = jnp.sqrt(jnp.sum(grad_weights * grad_weights))
    clipped = grad_weights * jnp.minimum(1.0, clip_norm / norm_value)
    new_master, new_first, new_second = adam_update(master, first_moment, second_moment, clipped)
    return (outputs.reshape(POINTS, WIDTH).astype(jnp.bfloat16), grad_inputs.reshape(POINTS, WIDTH).astype(jnp.bfloat16), norm_value, new_master, new_first, new_second, new_master.astype(jnp.bfloat16))
```

```python
import functools

import jax
import jax.numpy as jnp
from jax import lax
from jax.experimental import pallas as pl
from jax.experimental.pallas import tpu as pltpu
from jax.sharding import PartitionSpec as P

WIDTH = 256
GROUPS = 32
NEAREST = 16
PER_GROUP = WIDTH // GROUPS
LANES = 128
WINDOW = 256
PAIRS = NEAREST * LANES

SQUARE = WIDTH * WIDTH
OFF_ATT_IN = 5 * SQUARE
OFF_ATT_OUT = OFF_ATT_IN + WIDTH * GROUPS
OFF_TAIL = OFF_ATT_OUT + GROUPS * GROUPS
NORMS = 2 * WIDTH + 3 + GROUPS
TAIL_POS_OUT = 9
TAIL_GAINS = TAIL_POS_OUT + 3 * WIDTH
TAIL_SHIFTS = TAIL_GAINS + NORMS
TAIL_USED = TAIL_SHIFTS + NORMS
TAIL_PAD = 2048
SLICE = 2048
SLICE_ROWS = SLICE // LANES
CHUNK = 1024

bn_eps = 1e-05
clip_norm = 0.01
learn_rate = 0.05
beta_one = 0.9
beta_two = 0.999
adam_eps = 1e-08
decay_rate = 0.01
step_count = 10
masked_logit = -1000000000.0

f32 = jnp.float32
bf16 = jnp.bfloat16
MESH = pl.DeviceIdType.MESH


def contract(a, b, left, right):
    return lax.dot_general(a, b, (((left,), (right,)), ((), ())), preferred_element_type=f32)


def nn(a, b):
    return contract(a, b, 1, 0)


def nt(a, b):
    return contract(a, b, 1, 1)


def tn(a, b):
    return contract(a, b, 0, 0)


def split(value, parts):
    pieces = []
    for _ in range(parts):
        piece = value.astype(bf16)
        pieces.append(piece)
        value = value - piece.astype(f32)
    return pieces


def silu_parts(value):
    gate = 0.5 * jnp.tanh(0.5 * value) + 0.5
    return value * gate, gate


def silu_slope(value, gate):
    return gate * (1.0 + value * (1.0 - gate))


def iota(shape, dim):
    return lax.broadcasted_iota(jnp.int32, shape, dim)


def row_to_col(row, count):
    wide = jnp.broadcast_to(row, (count, row.shape[1]))
    same = iota(wide.shape, 0) == iota(wide.shape, 1)
    return jnp.sum(jnp.where(same, wide, 0.0), axis=1, keepdims=True)


def col_to_row(col, offset):
    wide = jnp.broadcast_to(col, (col.shape[0], LANES))
    same = iota(wide.shape, 0) + offset == iota(wide.shape, 1)
    return jnp.sum(jnp.where(same, wide, 0.0), axis=0, keepdims=True)


def row_sum(value):
    return jnp.sum(value, axis=0, keepdims=True)


def lane_fold(value):
    total = value[:, 0:LANES]
    for k in range(1, value.shape[1] // LANES):
        total = total + value[:, k * LANES : (k + 1) * LANES]
    return total


def lane_sum(value):
    return jnp.sum(lane_fold(value), axis=1, keepdims=True)


def tiles(value):
    return jnp.concatenate([value] * NEAREST, axis=1)


def adam(param, moment, second, grad):
    moment_new = beta_one * moment + (1.0 - beta_one) * grad
    second_new = beta_two * second + (1.0 - beta_two) * grad * grad
    moment_hat = moment_new / (1.0 - beta_one**step_count)
    second_hat = second_new / (1.0 - beta_two**step_count)
    param_new = param - learn_rate * (
        moment_hat / (jnp.sqrt(second_hat) + adam_eps) + decay_rate * param
    )
    return param_new, moment_new, second_new


def peer(me, step, count):
    if count & (count - 1) == 0:
        return me ^ (count - step)
    return lax.rem(me + step, count)


def block_kernel(
    n_rows, n_cols,
    feat_h, coords_h, valid_h, nbrs_h, cot_h, weights_h, master_h, first_h, second_h,
    out_h, gfeat_h, gnorm_h, new_master_h, new_first_h, new_second_h, slabs_h,
    feat, coords, valid, nbrs, cot, w_first, pos_first, weights, state, news, outs, norm_s, in_sem, out_sem,
    stat_send, stat_buf, stat_ssem, stat_rsem,
    tail1d, mats, onehot, vgat, att, wpre, uact, dyw, rel, pos, act, pmask, allow, dmix,
    a1_s, z_s, h_s, q_s, k_s, o_s, do_s, dv_s, sk_s, bd_s, xs, dz_s, dz16,
    flat, pair_got, part16, got16, sums, owned, tail_g, slab_f, shard_w, all_w,
    pair_ssem, pair_rsem, rs_ssem, rs_rsem, own_ssem, own_rsem, ag_ssem, ag_rsem, fw_ssem, fw_rsem,
):
    n = n_rows * n_cols
    half = n // 2
    row_id, col_id = lax.axis_index("rows"), lax.axis_index("cols")
    me = row_id * n_cols + col_id
    core = lax.rem(col_id, 2)
    chip = me // 2
    points = feat.shape[0]
    blocks = points // LANES
    starts = [min(max(LANES * b - (WINDOW - LANES) // 2, 0), points - WINDOW) for b in range(blocks)]
    total_len = weights.shape[0]
    shard_len = master_h.shape[0]
    shard_rows = -(-tail_g.shape[0] // LANES)
    sliced = flat.shape[0]
    slots = got16.shape[0]
    sides = own_ssem.shape[1]
    span = own_rsem.shape[0]

    def place(device):
        return (device // n_cols, lax.rem(device, n_cols))

    loads = []

    def load(source, target):
        copy = pltpu.make_async_copy(source, target, in_sem.at[len(loads)])
        copy.start()
        loads.append(copy)
        return copy

    stores = []

    def store(source, target):
        copy = pltpu.make_async_copy(source, target, out_sem.at[len(stores)])
        copy.start()
        stores.append(copy)

    early = [
        load(feat_h, feat),
        load(weights_h.at[pl.ds(0, SQUARE)], w_first),
        load(weights_h.at[pl.ds(OFF_TAIL, 1024)], pos_first),
        load(nbrs_h, nbrs),
        load(coords_h, coords),
        load(valid_h, valid),
    ]

    barrier = pltpu.get_barrier_semaphore()

    def greet(k, carry):
        pl.semaphore_signal(barrier, inc=1, device_id=place(peer(me, k, n)), device_id_type=MESH)
        return carry

    lax.fori_loop(1, n, greet, 0)
    late = [load(weights_h, weights), load(cot_h, cot)]
    for source, target in ((master_h, 0), (first_h, 1), (second_h, 2)):
        late.append(load(source, state[target]))
    owned[...] = jnp.zeros(owned.shape, f32)
    for copy in early:
        copy.wait()

    sent = []

    def all_sum(index, message):
        rows = message.shape[0]
        stat_send[index, 0:rows] = message
        stat_buf[index, me, 0:rows] = message

        def post(k, carry):
            pltpu.make_async_remote_copy(
                src_ref=stat_send.at[index, pl.ds(0, rows)],
                dst_ref=stat_buf.at[index, me, pl.ds(0, rows)],
                send_sem=stat_ssem.at[index],
                recv_sem=stat_rsem.at[index],
                device_id=place(peer(me, k, n)),
                device_id_type=MESH,
            ).start()
            return carry

        lax.fori_loop(1, n, post, 0)
        sent.append((index, rows))

        def collect():
            span = stat_buf.at[index, pl.ds(0, n - 1), pl.ds(0, rows)]
            pltpu.make_async_copy(span, span, stat_rsem.at[index]).wait()
            return jnp.sum(stat_buf[index, :, 0:rows], axis=0)

        return collect

    sibling = (row_id, col_id + 1 - 2 * core)
    per_matrix = SQUARE // SLICE // 2

    def put_matrix(m, grad):
        flat[m * per_matrix : (m + 1) * per_matrix] = grad.reshape(per_matrix, 2, SLICE_ROWS, LANES)

    def exchange(group, begin, count):
        copy = pltpu.make_async_remote_copy(
            src_ref=flat.at[pl.ds(begin, count), 1 - core],
            dst_ref=pair_got.at[pl.ds(begin, count)],
            send_sem=pair_ssem.at[group],
            recv_sem=pair_rsem.at[group],
            device_id=sibling,
            device_id_type=MESH,
        )
        copy.start()
        return copy, begin, count

    def send_slice(index, slot, other):
        pltpu.make_async_remote_copy(
            src_ref=part16.at[index],
            dst_ref=got16.at[slot, chip],
            send_sem=rs_ssem.at[slot],
            recv_sem=rs_rsem.at[slot],
            device_id=place(2 * other + core),
            device_id_type=MESH,
        ).start()

    def send_group(pair):
        copy, begin, count = pair
        copy.wait()
        part16[pl.ds(begin, count)] = (
            flat[pl.ds(begin, count), core] + pair_got[pl.ds(begin, count)]
        ).astype(bf16)
        if count % half == 0 and begin % half == 0:
            for slot in range(begin // half, (begin + count) // half):

                def post(k, carry, slot=slot):
                    other = peer(chip, k, half)
                    send_slice(slot * half + other, slot, other)
                    return carry

                lax.fori_loop(1, half, post, 0)
        else:

            def post_any(k, carry):
                index = begin + k
                slot, other = index // half, lax.rem(index, half)

                @pl.when(other != chip)
                def _():
                    send_slice(index, slot, other)

                return carry

            lax.fori_loop(0, count, post_any, 0)

    def drain_stats(index, rows):
        span = stat_buf.at[index, pl.ds(0, n - 1), pl.ds(0, rows)]
        pltpu.make_async_copy(span, span, stat_ssem.at[index]).wait()

    w_in = w_first[...].reshape(WIDTH, WIDTH)
    mats[0] = w_in
    w_in = mats[0]
    pos_in = pos_first[...].reshape(1024 // LANES, LANES)[0:1].astype(f32)
    lane8 = iota((8, 1), 0)

    def pos_in_col(c):
        return jnp.where(lane8 < 3, row_to_col(pos_in[:, 3 * c : 3 * c + 8], 8), 0.0)

    valid_rows = valid[...].reshape(points // LANES, LANES).astype(f32)
    n_valid = jnp.sum(jnp.sum(valid_rows, axis=0, keepdims=True), axis=1, keepdims=True)
    point_mask = (iota((points, 1), 0).astype(f32) < n_valid).astype(f32)
    lane_mask = (iota((1, points), 1).astype(f32) < n_valid).astype(f32)

    a1 = nn(feat[...], w_in)
    a1_s[...] = a1
    masked = point_mask * a1
    sum_a, sqr_a = row_sum(masked), row_sum(masked * a1)

    window_row = iota((WINDOW, LANES), 0)
    for b in range(blocks):
        for j in range(NEAREST):
            index = nbrs[j : j + 1, b * LANES : (b + 1) * LANES] - starts[b]
            onehot[b, :, j * LANES : (j + 1) * LANES] = jnp.where(
                window_row == index, 1.0, 0.0
            ).astype(bf16)

    coords8 = jnp.concatenate([coords[...], jnp.zeros((5, points), f32)], axis=0)
    table = jnp.concatenate(
        split(coords8, 3) + [jnp.broadcast_to(lane_mask, (8, points)).astype(bf16)], axis=0
    )
    slot0 = (iota((1, PAIRS), 1) < LANES).astype(f32)
    pos_in_cols = [pos_in_col(c) for c in range(3)]
    sum_p = jnp.zeros((8, 1), f32)
    sqr_p = jnp.zeros((8, 1), f32)
    pairs_local = jnp.zeros((1, 1), f32)
    for b in range(blocks):
        here = slice(b * LANES, (b + 1) * LANES)
        fetched = nn(table[:, starts[b] : starts[b] + WINDOW], onehot[b])
        place_n = fetched[0:8] + fetched[8:16] + fetched[16:24]
        mask_n = fetched[24:32]
        r = place_n - tiles(coords8[:, here])
        pm = mask_n * tiles(lane_mask[:, here])
        p = pos_in_cols[0] * r[0:1] + pos_in_cols[1] * r[1:2] + pos_in_cols[2] * r[2:3]
        rel[b] = r
        pos[b] = p
        pmask[b] = pm
        allow[b] = jnp.maximum(mask_n, slot0)
        sum_p = sum_p + lane_sum(pm * p)
        sqr_p = sqr_p + lane_sum(pm * p * p)
        pairs_local = pairs_local + lane_sum(pm[0:1])

    lane = iota((1, LANES), 1)
    last = (
        col_to_row(sum_p, 0)
        + col_to_row(sqr_p, 8)
        + jnp.where(lane == 16, n_valid, 0.0)
        + jnp.where(lane == 17, pairs_local, 0.0)
    )

    def fold(row):
        return jnp.concatenate([row[:, 0:LANES], row[:, LANES:WIDTH]], axis=0)

    def unfold(rows):
        return jnp.concatenate([rows[0:1], rows[1:2]], axis=1)

    pl.semaphore_wait(barrier, n - 1)
    collect_first = all_sum(0, jnp.concatenate([fold(sum_a), fold(sqr_a), last], axis=0))
    for copy in late:
        copy.wait()
    for m in range(1, 5):
        mats[m] = weights[pl.ds(m * SQUARE, SQUARE)].reshape(WIDTH, WIDTH)
    w_q, w_k, w_v, w_o = (mats[m] for m in range(1, 5))
    att_in = weights[pl.ds(OFF_ATT_IN, WIDTH * GROUPS)].reshape(WIDTH * GROUPS // LANES, LANES)
    att_in_f = att_in.astype(f32).reshape(WIDTH, GROUPS)
    att_in_t = att_in_f.T.astype(bf16)
    att_out_f = (
        weights[pl.ds(OFF_ATT_OUT, GROUPS * GROUPS)]
        .reshape(GROUPS * GROUPS // LANES, LANES)
        .astype(f32)
        .reshape(GROUPS, GROUPS)
    )
    att_out = att_out_f.astype(bf16)
    att_out_t = att_out_f.T.astype(bf16)
    tail1d[pl.ds(0, 1024)] = weights[pl.ds(OFF_TAIL, 1024)]
    rest = total_len - OFF_TAIL - 1024
    tail1d[pl.ds(1024, rest)] = weights[pl.ds(OFF_TAIL + 1024, rest)]
    tail = tail1d[pl.ds(0, TAIL_PAD)].reshape(TAIL_PAD // LANES, LANES).astype(f32)
    tail = jnp.concatenate([tail[k : k + 1] for k in range(TAIL_PAD // LANES)], axis=1)
    pos_rows = [tail[:, TAIL_POS_OUT + WIDTH * d : TAIL_POS_OUT + WIDTH * (d + 1)] for d in range(3)]
    def norm_pieces(start):
        ends = [0, WIDTH, WIDTH + 3, WIDTH + 3 + GROUPS, NORMS]
        return [tail[:, start + ends[k] : start + ends[k + 1]] for k in range(4)]

    gain_a, gain_p, gain_w, gain_o = norm_pieces(TAIL_GAINS)
    shift_a, shift_p, shift_w, shift_o = norm_pieces(TAIL_SHIFTS)

    def pad_col(row):
        wide = jnp.concatenate([row, jnp.zeros((1, 5), f32)], axis=1)
        return row_to_col(wide, 8)

    gain_p, shift_p = pad_col(gain_p), pad_col(shift_p)
    gain_w, shift_w = row_to_col(gain_w, GROUPS), row_to_col(shift_w, GROUPS)

    stats = collect_first()

    def pick(row, at):
        return jnp.sum(jnp.where(lane == at, row, 0.0), axis=1, keepdims=True)

    point_count, pair_count = pick(stats[4:5], 16), pick(stats[4:5], 17)
    inv_points, inv_pairs = 1.0 / point_count, 1.0 / pair_count

    def moments(total, square, inv):
        mean = total * inv
        return mean, lax.rsqrt(square * inv - mean * mean + bn_eps)

    mean_a, rs_a = moments(unfold(stats[0:2]), unfold(stats[2:4]), inv_points)
    mean_p, rs_p = moments(
        row_to_col(stats[4:5, 0:8], 8), row_to_col(stats[4:5, 8:16], 8), inv_pairs
    )

    h = silu_parts((a1_s[...] - mean_a) * rs_a * gain_a + shift_a)[0].astype(bf16)
    h_s[...] = h
    q = nn(h, w_q).astype(bf16)
    k = nn(h, w_k).astype(bf16)
    q_s[...] = q
    k_s[...] = k
    q_att = nt(att_in_t, q)
    k_att = jnp.concatenate(split(nt(att_in_t, k), 3), axis=0)
    pos_mat = jnp.concatenate(pos_rows + [jnp.zeros((13, WIDTH), f32)], axis=0).astype(bf16)
    pos_att = nt(att_in_t, pos_mat)
    pos_att_cols = [pos_att[:, d : d + 1] for d in range(3)]

    sum_w = jnp.zeros((GROUPS, LANES), f32)
    sqr_w = jnp.zeros((GROUPS, LANES), f32)
    for b in range(blocks):
        here = slice(b * LANES, (b + 1) * LANES)
        active = silu_parts((pos[b] - mean_p) * rs_p * gain_p + shift_p)[0]
        act[b] = active
        fetched = nn(k_att[:, starts[b] : starts[b] + WINDOW], onehot[b])
        w = tiles(q_att[:, here]) - (
            fetched[0:GROUPS] + fetched[GROUPS : 2 * GROUPS] + fetched[2 * GROUPS : 3 * GROUPS]
        )
        for d in range(3):
            w = w + pos_att_cols[d] * active[d : d + 1]
        wpre[b] = w
        mw = w * pmask[b, 0:1]
        sum_w = sum_w + lane_fold(mw)
        sqr_w = sqr_w + lane_fold(mw * w)

    def pair_row(one, two):
        one = jnp.sum(one, axis=1, keepdims=True)
        two = jnp.sum(two, axis=1, keepdims=True)
        return col_to_row(one, 0) + col_to_row(two, GROUPS)

    collect_w = all_sum(1, pair_row(sum_w, sqr_w))
    v_t = nn(h, w_v).T.astype(bf16)
    for b in range(blocks):
        vgat[b] = nn(v_t[:, starts[b] : starts[b] + WINDOW], onehot[b])
    stats = collect_w()
    mean_w, rs_w = moments(
        row_to_col(stats[:, 0:GROUPS], GROUPS),
        row_to_col(stats[:, GROUPS : 2 * GROUPS], GROUPS),
        inv_pairs,
    )

    group_of = iota((WIDTH, 2 * GROUPS), 0) // PER_GROUP
    spread = jnp.where(group_of == iota((WIDTH, 2 * GROUPS), 1) % GROUPS, 1.0, 0.0).astype(bf16)
    own_group = iota((GROUPS, WIDTH), 1) // PER_GROUP == iota((GROUPS, WIDTH), 0)
    gather_groups = jnp.where(own_group, 1.0, 0.0).astype(bf16)
    pos_spread = jnp.concatenate(
        [jnp.where(own_group, jnp.broadcast_to(pos_rows[d], (GROUPS, WIDTH)), 0.0) for d in range(3)],
        axis=0,
    ).astype(bf16)

    def cols(j):
        return slice(j * LANES, (j + 1) * LANES)

    for b in range(blocks):
        here = slice(b * LANES, (b + 1) * LANES)
        u = silu_parts((wpre[b] - mean_w) * rs_w * gain_w + shift_w)[0].astype(bf16)
        uact[b] = u
        logit = jnp.where(allow[b, 0:1] > 0.5, nn(att_out_t, u), masked_logit)
        top = logit[:, cols(0)]
        for j in range(1, NEAREST):
            top = jnp.maximum(top, logit[:, cols(j)])
        weight = jnp.exp(logit - tiles(top))
        share = 1.0 / functools.reduce(jnp.add, [weight[:, cols(j)] for j in range(NEAREST)])
        att[b] = weight * tiles(share)
        mixed = jnp.zeros((WIDTH, LANES), f32)
        enc = [jnp.zeros((GROUPS, LANES), f32) for _ in range(3)]
        for j in range(NEAREST):
            a = att[b, :, cols(j)]
            wide = nn(spread, jnp.concatenate(split(a, 2), axis=0))
            mixed = mixed + wide * vgat[b, :, cols(j)]
            for d in range(3):
                enc[d] = enc[d] + a * act[b, d : d + 1, cols(j)]
        enc = jnp.concatenate(enc, axis=0)
        bd_s[:, here] = enc
        for piece in split(enc, 3):
            mixed = mixed + tn(pos_spread, piece)
        o_s[:, here] = mixed.astype(bf16)

    z = tn(o_s[...], w_o)
    z_s[...] = z
    masked = point_mask * z
    collect_o = all_sum(2, jnp.concatenate([fold(row_sum(masked)), fold(row_sum(masked * z))], axis=0))
    stats = collect_o()
    mean_o, rs_o = moments(unfold(stats[0:2]), unfold(stats[2:4]), inv_points)

    zhat = (z_s[...] - mean_o) * rs_o
    y = feat[...].astype(f32) + zhat * gain_o + shift_o
    value, gate = silu_parts(y)
    outs[0] = (point_mask * value).astype(bf16)
    store(outs.at[0], out_h)
    dy = point_mask * cot[...].astype(f32) * silu_slope(y, gate)
    dz_s[...] = dy
    shift_grad_o, gain_grad_o = row_sum(dy), row_sum(dy * zhat)
    stats = all_sum(3, jnp.concatenate([fold(shift_grad_o), fold(gain_grad_o)], axis=0))()
    one, two = unfold(stats[0:2]) * inv_points, unfold(stats[2:4]) * inv_points
    zhat = (z_s[...] - mean_o) * rs_o
    dz = (gain_o * rs_o * (dz_s[...] - point_mask * (one + zhat * two))).astype(bf16)
    dz16[...] = dz
    do_s[...] = nt(w_o, dz)
    dv_s[...] = jnp.zeros(dv_s.shape, f32)

    sum_w = jnp.zeros((GROUPS, LANES), f32)
    sqr_w = jnp.zeros((GROUPS, LANES), f32)
    d_att_out = jnp.zeros((GROUPS, GROUPS), f32)
    for b in range(blocks):
        here = slice(b * LANES, (b + 1) * LANES)
        do = do_s[:, here]
        do_pos = sum(nn(pos_spread, piece) for piece in split(do, 2))
        da, mix = [], []
        for j in range(NEAREST):
            a = att[b, :, cols(j)]
            wide = nn(spread, jnp.concatenate(split(a, 2), axis=0))
            xs[:, cols(j)] = (wide * do).astype(bf16)
            grad = nn(gather_groups, (vgat[b, :, cols(j)] * do).astype(bf16))
            back = []
            for d in range(3):
                part = do_pos[d * GROUPS : (d + 1) * GROUPS]
                grad = grad + part * act[b, d : d + 1, cols(j)]
                back.append(row_sum(part * a))
            da.append(grad)
            mix.append(jnp.concatenate(back + [jnp.zeros((5, LANES), f32)], axis=0))
        dmix[b] = jnp.concatenate(mix, axis=1)
        dv_s[pl.ds(starts[b], WINDOW)] += nt(onehot[b], xs[...])
        mean_da = functools.reduce(jnp.add, [da[j] * att[b, :, cols(j)] for j in range(NEAREST)])
        ds = jnp.concatenate(
            [att[b, :, cols(j)] * (da[j] - mean_da) for j in range(NEAREST)], axis=1
        ).astype(bf16)
        d_att_out = d_att_out + nt(uact[b], ds)
        what = (wpre[b] - mean_w) * rs_w
        y = what * gain_w + shift_w
        gate = silu_parts(y)[1]
        dy = nn(att_out, ds) * silu_slope(y, gate)
        dyw[b] = dy
        sum_w = sum_w + lane_fold(dy)
        sqr_w = sqr_w + lane_fold(dy * what)

    back_w = pair_row(sum_w, sqr_w)
    collect_w = all_sum(4, back_w)
    dv = dv_s[...].astype(bf16)
    put_matrix(4, nn(o_s[...], dz16[...]))
    put_matrix(3, tn(h_s[...], dv))
    late_pair = exchange(0, 3 * 16, 2 * 16)
    send_group(late_pair)
    stats = collect_w()
    one = row_to_col(stats[:, 0:GROUPS], GROUPS) * inv_pairs
    two = row_to_col(stats[:, GROUPS : 2 * GROUPS], GROUPS) * inv_pairs

    sk_s[...] = jnp.zeros(sk_s.shape, f32)
    pos_att_rows = split(pos_att[:, 0:8].T, 3)
    pos_att_rows = jnp.concatenate(pos_att_rows, axis=0)
    dw_sums = []
    d_pos_att = jnp.zeros((24, GROUPS), f32)
    sum_p = jnp.zeros((8, 1), f32)
    sqr_p = jnp.zeros((8, 1), f32)
    for b in range(blocks):
        what = (wpre[b] - mean_w) * rs_w
        dw_f = gain_w * rs_w * (dyw[b] - pmask[b, 0:1] * (one + what * two))
        dw = dw_f.astype(bf16)
        sk_s[pl.ds(starts[b], WINDOW)] += nt(onehot[b], dw)
        dw_sums.append(lane_slots(dw.astype(f32)))
        active = act[b]
        d_pos_att = d_pos_att + nt(jnp.concatenate(split(active, 3), axis=0), dw)
        back = nn(pos_att_rows, dw)
        d_act = dmix[b] + back[0:8] + back[8:16] + back[16:24]
        phat = (pos[b] - mean_p) * rs_p
        y = phat * gain_p + shift_p
        gate = silu_parts(y)[1]
        dy = d_act * silu_slope(y, gate)
        dmix[b] = dy
        sum_p = sum_p + lane_sum(dy)
        sqr_p = sqr_p + lane_sum(dy * phat)
    dq_att = jnp.concatenate(dw_sums, axis=1)
    dq_split = split(dq_att, 2)
    dk_split = split(-sk_s[...], 2)
    dq = sum(tn(piece, att_in_t) for piece in dq_split).astype(bf16)
    dk = sum(nn(piece, att_in_t) for piece in dk_split).astype(bf16)
    dh = nt(dq, w_q) + nt(dk, w_k) + nt(dv, w_v)
    ahat = (a1_s[...] - mean_a) * rs_a
    y = ahat * gain_a + shift_a
    gate = silu_parts(y)[1]
    dy = dh * silu_slope(y, gate)
    z_s[...] = dy
    shift_grad_a, gain_grad_a = row_sum(dy), row_sum(dy * ahat)
    last = col_to_row(sum_p, 0) + col_to_row(sqr_p, 8)
    collect_a = all_sum(
        5, jnp.concatenate([fold(shift_grad_a), fold(gain_grad_a), last], axis=0)
    )

    put_matrix(1, tn(h_s[...], dq))
    put_matrix(2, tn(h_s[...], dk))
    send_group(exchange(1, per_matrix, 2 * per_matrix))
    d_pos_att = d_pos_att[0:8] + d_pos_att[8:16] + d_pos_att[16:24]
    d_pos_split = split(d_pos_att, 3)
    d_att_in = sum(contract(q_s[...], piece, 0, 1) for piece in dq_split)
    d_att_in = d_att_in + sum(tn(k_s[...], piece) for piece in dk_split)
    d_att_in = d_att_in + sum(tn(pos_mat[0:8], piece) for piece in d_pos_split)
    d_pos_out = sum(nn(piece, att_in_t) for piece in d_pos_split)
    do_split = split(do_s[...], 2)
    bd_split = split(bd_s[...], 2)
    cross = nt(bd_split[0], do_split[0]) + nt(bd_split[0], do_split[1]) + nt(bd_split[1], do_split[0])
    d_pos_rows = [
        d_pos_out[d : d + 1]
        + row_sum(jnp.where(own_group, cross[d * GROUPS : (d + 1) * GROUPS], 0.0))
        for d in range(3)
    ]
    small = 5 * per_matrix
    pieces_rows = [
        d_att_in.reshape(WIDTH * GROUPS // LANES, LANES),
        d_att_out.reshape(GROUPS * GROUPS // LANES, LANES),
    ]
    along, along_hat, offsets = [], [], []
    for c in range(3):
        one = [jnp.zeros((8, 1), f32) for _ in range(3)]
        for b in range(blocks):
            masked = pmask[b] * rel[b, c : c + 1]
            one[0] = one[0] + lane_sum(dmix[b] * rel[b, c : c + 1])
            one[1] = one[1] + lane_sum(masked * ((pos[b] - mean_p) * rs_p))
            one[2] = one[2] + lane_sum(masked)
        along.append(one[0])
        along_hat.append(one[1])
        offsets.append(one[2])
    stats = collect_a()
    one, two = unfold(stats[0:2]) * inv_points, unfold(stats[2:4]) * inv_points
    ahat = (a1_s[...] - mean_a) * rs_a
    da1 = (gain_a * rs_a * (z_s[...] - point_mask * (one + ahat * two))).astype(bf16)
    put_matrix(0, tn(feat[...], da1))
    one = row_to_col(stats[4:5, 0:8], 8) * inv_pairs
    two = row_to_col(stats[4:5, 8:16], 8) * inv_pairs
    pieces = []
    for c in range(3):
        d_pos_in = gain_p * rs_p * (along[c] - one * offsets[c] - two * along_hat[c])
        pieces.append(col_to_row(d_pos_in, 0)[:, 0:3])
    pieces = pieces + d_pos_rows
    pieces = pieces + [
        gain_grad_a, col_to_row(sqr_p, 0)[:, 0:3], back_w[:, GROUPS : 2 * GROUPS], gain_grad_o,
        shift_grad_a, col_to_row(sum_p, 0)[:, 0:3], back_w[:, 0:GROUPS], shift_grad_o,
        jnp.zeros((1, TAIL_PAD - TAIL_USED), f32),
    ]
    pieces_rows.append(jnp.concatenate(pieces, axis=1).reshape(TAIL_PAD // LANES, LANES))
    used_rows = OFF_TAIL // LANES + TAIL_PAD // LANES - 5 * SQUARE // LANES
    spare_rows = (sliced - small) * 2 * SLICE_ROWS - used_rows
    pieces_rows.append(jnp.zeros((spare_rows, LANES), f32))
    flat[small:sliced] = jnp.concatenate(pieces_rows, axis=0).reshape(
        sliced - small, 2, SLICE_ROWS, LANES
    )
    first_pair, small_pair = exchange(2, 0, per_matrix), exchange(3, small, sliced - small)
    send_group(first_pair)
    send_group(small_pair)
    outs[1] = (dz_s[...] + nt(da1, w_in)).astype(bf16)
    store(outs.at[1], gfeat_h)

    squares = jnp.zeros((1, 1), f32)
    for slot in list(range(1, slots)) + [0]:
        index = slot * half + chip
        if (slot + 1) * half <= sliced:
            here = None
        else:
            here = index < sliced

        def take(slot=slot, index=index):
            got = got16.at[slot, pl.ds(0, half - 1)]
            pltpu.make_async_copy(got, got, rs_rsem.at[slot]).wait()
            total = flat[index, core] + pair_got[index]

            def add(k, total):
                return total + got16[slot, peer(chip, k, half)].astype(f32)

            sums[slot] = lax.fori_loop(1, half, add, total, unroll=half <= 16)

        if here is None:
            take()
        else:
            sums[slot] = jnp.zeros((SLICE_ROWS, LANES), f32)
            pl.when(here)(take)
        squares = squares + lane_sum(row_sum(sums[slot] * sums[slot]))

    collect_norm = all_sum(6, jnp.where(lane == 0, squares, 0.0))

    def slice_of(slot):
        return 2 * (slot * half + chip) + core

    def each_owner(slot, act_on):
        number = slice_of(slot)
        low = number * SLICE // shard_len
        high = jnp.minimum((number * SLICE + SLICE - 1) // shard_len, n - 1)
        for side in range(sides):
            owner = low + side

            @pl.when((number * SLICE < total_len) & (owner <= high))
            def _(owner=owner, side=side):
                act_on(owner, number - owner * shard_len // SLICE, side)

    def owned_rows(k):
        return owned.at[pl.ds(pl.multiple_of(k * SLICE_ROWS, SLICE_ROWS), SLICE_ROWS)]

    def own_copy(slot, owner, k, side):
        return pltpu.make_async_remote_copy(
            src_ref=sums.at[slot],
            dst_ref=owned_rows(k),
            send_sem=own_ssem.at[slot, side],
            recv_sem=own_rsem.at[k],
            device_id=place(owner),
            device_id_type=MESH,
        )

    for slot in range(slots):

        def hand_over(owner, k, side, slot=slot):
            @pl.when(owner != me)
            def _():
                own_copy(slot, owner, k, side).start()

            @pl.when(owner == me)
            def _():
                owned_rows(k)[...] = sums[slot]

        each_owner(slot, hand_over)

    begin = me * shard_len
    first_slice = begin // SLICE
    last_slice = (begin + shard_len - 1) // SLICE
    for k in range(span):
        number = first_slice + k

        @pl.when((number <= last_slice) & (lax.rem(number, n) != me))
        def _(k=k):
            rows = owned.at[pl.ds(k * SLICE_ROWS, SLICE_ROWS)]
            pltpu.make_async_copy(rows, rows, own_rsem.at[k]).wait()

    offset = begin - first_slice * SLICE
    skip = lax.rem(offset, LANES)
    lanes_all = iota((shard_rows, LANES), 1)
    rows = owned[pl.ds(offset // LANES, shard_rows), :]
    turned = pltpu.roll(rows, lax.rem(LANES - skip, LANES), 1)
    below = pltpu.roll(turned, shard_rows - 1, 0)
    grad = jnp.where(lanes_all < LANES - skip, turned, below)
    inside = iota(grad.shape, 0) * LANES + lanes_all < shard_len
    grad = jnp.where(inside, grad, 0.0)

    stats = collect_norm()
    norm = jnp.sqrt(pick(stats, 0))
    norm_s[...] = jnp.broadcast_to(norm, norm_s.shape)
    grad = grad * jnp.minimum(1.0, clip_norm / norm)

    main = shard_len // 1024 * 1024
    spare = shard_len - main
    tail_g[...] = grad.reshape(shard_rows * LANES)
    for start, size in ((0, main), (main, spare)):
        if size == 0:
            continue
        at = pl.ds(start, size)
        p_new, m_new, s_new = adam(state[0][at], state[1][at], state[2][at], tail_g[at])
        news[0][at] = p_new
        news[1][at] = m_new
        news[2][at] = s_new
        tail_g[at] = p_new
    moved = jnp.where(inside, tail_g[...].reshape(shard_rows, LANES), 0.0)
    turned = pltpu.roll(moved, skip, 1)
    above = pltpu.roll(turned, 1, 0)
    slab_f[...] = jnp.zeros(slab_f.shape, f32)
    slab_f[pl.ds(lax.rem(begin, CHUNK) // LANES, shard_rows), :] = jnp.where(
        lanes_all < skip, above, turned
    )
    shard_w[...] = slab_f[...].astype(bf16)
    all_w[core, chip] = slab_f[...].astype(bf16)

    def send_new(k, carry):
        pltpu.make_async_remote_copy(
            src_ref=shard_w,
            dst_ref=all_w.at[core, chip],
            send_sem=ag_ssem,
            recv_sem=ag_rsem.at[chip],
            device_id=place(2 * peer(chip, k, half) + core),
            device_id_type=MESH,
        ).start()
        return carry

    lax.fori_loop(1, half, send_new, 0)
    store(norm_s, gnorm_h)
    for source, target in ((0, new_master_h), (1, new_first_h), (2, new_second_h)):
        store(news[source], target)

    def forward(other):
        return pltpu.make_async_remote_copy(
            src_ref=all_w.at[core, other],
            dst_ref=all_w.at[core, other],
            send_sem=fw_ssem,
            recv_sem=fw_rsem,
            device_id=sibling,
            device_id_type=MESH,
        )

    forward(chip).start()

    def pass_on(k, carry):
        other = peer(chip, half - k, half)
        pltpu.make_async_copy(shard_w, shard_w, ag_rsem.at[other]).wait()
        forward(other).start()
        return carry

    lax.fori_loop(1, half, pass_on, 0)
    pltpu.make_async_copy(all_w.at[core], all_w.at[core], fw_rsem).wait()
    store(all_w, slabs_h)

    for index, rows in sent:
        drain_stats(index, rows)
    for copy in stores:
        copy.wait()
    pltpu.make_async_copy(all_w.at[core], all_w.at[core], fw_ssem).wait()
    rest = all_w.at[core, pl.ds(0, half - 1)]
    pltpu.make_async_copy(rest, rest, ag_ssem).wait()
    for slot in range(slots):
        count = min(sliced - slot * half, half)

        def drain(k, carry, slot=slot):
            pltpu.make_async_copy(part16.at[0], part16.at[0], rs_ssem.at[slot]).wait()
            return carry

        lax.fori_loop(0, count - (chip < count).astype(jnp.int32), drain, 0)

        def own_drain(owner, k, side, slot=slot):
            @pl.when(owner != me)
            def _():
                own_copy(slot, owner, k, side).wait_send()

        each_owner(slot, own_drain)


def finish_kernel(
    n, shard_len,
    out_t, gfeat_t, gnorm_t, master_t, first_t, second_t, slabs_t,
    out_h, gfeat_h, gnorm, master_h, first_h, second_h, weights_h,
    out, gfeat, norm_s, master, first, second, slabs, joined, in_sem, out_sem,
):
    loads = [
        pltpu.make_async_copy(source, target, in_sem.at[k])
        for k, (source, target) in enumerate(
            (
                (slabs_t, slabs),
                (out_t, out),
                (gfeat_t, gfeat),
                (master_t, master),
                (first_t, first),
                (second_t, second),
                (gnorm_t, norm_s),
            )
        )
    ]
    stores = [
        pltpu.make_async_copy(source, target, out_sem.at[k])
        for k, (source, target) in enumerate(
            (
                (joined, weights_h),
                (out, out_h),
                (gfeat, gfeat_h),
                (master, master_h),
                (first, first_h),
                (second, second_h),
            )
        )
    ]
    for copy in loads:
        copy.start()
    for k in range(1, 6):
        loads[k].wait()
        stores[k].start()
    loads[6].wait()
    gnorm[...] = norm_s[0:1, 0:1]
    loads[0].wait()
    total_len = joined.shape[0]
    rows = CHUNK // LANES

    def chunk(c):
        value = None
        for owner in range(c * CHUNK // shard_len, min((c * CHUNK + CHUNK - 1) // shard_len, n - 1) + 1):
            k = c - owner * shard_len // CHUNK
            part = slabs[owner % 2, owner // 2, rows * k : rows * (k + 1)].astype(f32)
            value = part if value is None else value + part
        return value

    whole = total_len // (2 * CHUNK)
    for c in range(whole):
        both = jnp.concatenate([chunk(2 * c), chunk(2 * c + 1)], axis=0)
        joined[pl.ds(2 * CHUNK * c, 2 * CHUNK)] = both.astype(bf16).reshape(2 * CHUNK)
    left = total_len - whole * 2 * CHUNK
    if left:
        parts = [chunk(2 * whole)]
        parts.append(chunk(2 * whole + 1) if left > CHUNK else jnp.zeros((rows, LANES), f32))
        both = jnp.concatenate(parts, axis=0).astype(bf16).reshape(2 * CHUNK)
        joined[pl.ds(2 * CHUNK * whole, left)] = both[0:left]
    stores[0].start()
    for copy in stores:
        copy.wait()


def lane_slots(value):
    return functools.reduce(
        jnp.add, [value[:, j * LANES : (j + 1) * LANES] for j in range(NEAREST)]
    )


def shards(
    n_rows, n_cols,
    features, coords, valid_mask, neighbors, cotangent, weights, master, first_moment, second_moment,
):
    n = n_rows * n_cols
    half = n // 2
    points = features.shape[0]
    blocks = points // LANES
    shard_len = master.shape[0]
    total_len = weights.shape[0]

    def up(value, unit):
        return -(-value // unit) * unit

    shard_rows = up(-(-shard_len // LANES) + 1, 8)
    slab_rows = up(shard_rows + CHUNK // LANES, 16)
    sliced = up(-(-total_len // SLICE), 2) // 2
    slots = -(-sliced // half)
    sides = (SLICE + shard_len - 2) // shard_len + 1
    span = (SLICE + shard_len - 2) // SLICE + 1
    hbm = pl.BlockSpec(memory_space=pltpu.HBM)
    vmem = pl.BlockSpec(memory_space=pltpu.VMEM)
    dma = pltpu.SemaphoreType.DMA
    shape = jax.ShapeDtypeStruct

    def pairs(rows, dtype=f32):
        return pltpu.VMEM((blocks, rows, PAIRS), dtype)

    def shard():
        return [pltpu.VMEM(master.shape, f32) for _ in range(3)]

    scratch = [
        pltpu.VMEM(features.shape, bf16),
        pltpu.VMEM(coords.shape, f32),
        pltpu.VMEM(valid_mask.shape, jnp.int32),
        pltpu.VMEM(neighbors.shape, jnp.int32),
        pltpu.VMEM(features.shape, bf16),
        pltpu.VMEM((SQUARE,), bf16),
        pltpu.VMEM((1024,), bf16),
        pltpu.VMEM(weights.shape, bf16),
        shard(),
        shard(),
        pltpu.VMEM((2, *features.shape), bf16),
        pltpu.VMEM((1, LANES), f32),
        dma((11,)),
        dma((7,)),
        pltpu.VMEM((7, 8, LANES), f32),
        pltpu.VMEM((7, n, 8, LANES), f32),
        dma((7,)),
        dma((7,)),
        pltpu.VMEM((TAIL_PAD,), bf16),
        pltpu.VMEM((5, WIDTH, WIDTH), bf16),
        pairs(WINDOW, bf16),
        pairs(WIDTH),
        pairs(GROUPS),
        pairs(GROUPS),
        pairs(GROUPS, bf16),
        pairs(GROUPS),
        pairs(8),
        pairs(8),
        pairs(8),
        pairs(8),
        pairs(8),
        pairs(8),
        pltpu.VMEM((points, WIDTH), f32),
        pltpu.VMEM((points, WIDTH), f32),
        pltpu.VMEM((points, WIDTH), bf16),
        pltpu.VMEM((points, WIDTH), bf16),
        pltpu.VMEM((points, WIDTH), bf16),
        pltpu.VMEM((WIDTH, points), bf16),
        pltpu.VMEM((WIDTH, points), f32),
        pltpu.VMEM((points, WIDTH), f32),
        pltpu.VMEM((points, GROUPS), f32),
        pltpu.VMEM((3 * GROUPS, points), f32),
        pltpu.VMEM((WIDTH, PAIRS), bf16),
        pltpu.VMEM((points, WIDTH), f32),
        pltpu.VMEM((points, WIDTH), bf16),
        pltpu.VMEM((sliced, 2, SLICE_ROWS, LANES), f32),
        pltpu.VMEM((sliced, SLICE_ROWS, LANES), f32),
        pltpu.VMEM((sliced, SLICE_ROWS, LANES), bf16),
        pltpu.VMEM((slots, half, SLICE_ROWS, LANES), bf16),
        pltpu.VMEM((slots, SLICE_ROWS, LANES), f32),
        pltpu.VMEM((up(max(span * SLICE_ROWS, SLICE_ROWS + shard_rows), SLICE_ROWS), LANES), f32),
        pltpu.VMEM((shard_rows * LANES,), f32),
        pltpu.VMEM((slab_rows, LANES), f32),
        pltpu.VMEM((slab_rows, LANES), bf16),
        pltpu.VMEM((2, half, slab_rows, LANES), bf16),
        dma((4,)),
        dma((4,)),
        dma((slots,)),
        dma((slots,)),
        dma((slots, sides)),
        dma((span,)),
        dma,
        dma((half,)),
        dma,
        dma,
    ]
    results = pl.pallas_call(
        functools.partial(block_kernel, n_rows, n_cols),
        out_shape=(
            shape(features.shape, bf16),
            shape(features.shape, bf16),
            shape((1, LANES), f32),
            shape(master.shape, f32),
            shape(master.shape, f32),
            shape(master.shape, f32),
            shape((2, half, slab_rows, LANES), bf16),
        ),
        in_specs=[hbm] * 9,
        out_specs=[hbm] * 7,
        scratch_shapes=scratch,
        compiler_params=pltpu.CompilerParams(
            collective_id=0, has_side_effects=True, vmem_limit_bytes=56 * 2**20
        ),
    )(features, coords, valid_mask, neighbors, cotangent, weights, master, first_moment, second_moment)
    results = pl.pallas_call(
        functools.partial(finish_kernel, n, shard_len),
        out_shape=(
            shape(features.shape, bf16),
            shape(features.shape, bf16),
            shape((1, 1), f32),
            shape(master.shape, f32),
            shape(master.shape, f32),
            shape(master.shape, f32),
            shape(weights.shape, bf16),
        ),
        in_specs=[hbm] * 7,
        out_specs=[hbm, hbm, vmem, hbm, hbm, hbm, hbm],
        scratch_shapes=[
            pltpu.VMEM(features.shape, bf16),
            pltpu.VMEM(features.shape, bf16),
            pltpu.VMEM((1, LANES), f32),
            pltpu.VMEM(master.shape, f32),
            pltpu.VMEM(master.shape, f32),
            pltpu.VMEM(master.shape, f32),
            pltpu.VMEM((2, half, slab_rows, LANES), bf16),
            pltpu.VMEM(weights.shape, bf16),
            dma((7,)),
            dma((6,)),
        ],
        compiler_params=pltpu.CompilerParams(vmem_limit_bytes=62 * 2**20),
    )(*results)
    return results[0], results[1], results[2].reshape(()), *results[3:]


def solution(mesh):
    both = ("rows", "cols")
    rows_split, cols_split, flat_split = P(both, None), P(None, both), P(both)
    return jax.shard_map(
        functools.partial(shards, mesh.shape["rows"], mesh.shape["cols"]),
        mesh=mesh,
        in_specs=(
            rows_split, cols_split, flat_split, cols_split, rows_split, P(),
            flat_split, flat_split, flat_split,
        ),
        out_specs=(rows_split, rows_split, P(), flat_split, flat_split, flat_split, P()),
        check_vma=False,
    )
```

```python
import functools

import jax
import jax.numpy as jnp
from jax import lax
from jax.experimental import pallas as pl
from jax.experimental.pallas import tpu as pltpu
from jax.sharding import PartitionSpec as P

WIDTH = 256
GROUPS = 32
NEAREST = 16
PER_GROUP = WIDTH // GROUPS
LANES = 128
WINDOW = 256
PAIRS = NEAREST * LANES

SQUARE = WIDTH * WIDTH
OFF_ATT_IN = 5 * SQUARE
OFF_ATT_OUT = OFF_ATT_IN + WIDTH * GROUPS
OFF_TAIL = OFF_ATT_OUT + GROUPS * GROUPS
NORMS = 2 * WIDTH + 3 + GROUPS
TAIL_POS_OUT = 9
TAIL_GAINS = TAIL_POS_OUT + 3 * WIDTH
TAIL_SHIFTS = TAIL_GAINS + NORMS
TAIL_USED = TAIL_SHIFTS + NORMS
TAIL_PAD = 2048
SLICE = 2048
SLICE_ROWS = SLICE // LANES
CHUNK = 1024

bn_eps = 1e-05
clip_norm = 0.01
learn_rate = 0.05
beta_one = 0.9
beta_two = 0.999
adam_eps = 1e-08
decay_rate = 0.01
step_count = 10
masked_logit = -1000000000.0

f32 = jnp.float32
bf16 = jnp.bfloat16
MESH = pl.DeviceIdType.MESH


def contract(a, b, left, right):
    return lax.dot_general(a, b, (((left,), (right,)), ((), ())), preferred_element_type=f32)


def nn(a, b):
    return contract(a, b, 1, 0)


def nt(a, b):
    return contract(a, b, 1, 1)


def tn(a, b):
    return contract(a, b, 0, 0)


def split(value, parts):
    pieces = []
    for _ in range(parts):
        piece = value.astype(bf16)
        pieces.append(piece)
        value = value - piece.astype(f32)
    return pieces


def silu_parts(value):
    gate = 0.5 * jnp.tanh(0.5 * value) + 0.5
    return value * gate, gate


def silu_slope(value, gate):
    return gate * (1.0 + value * (1.0 - gate))


def iota(shape, dim):
    return lax.broadcasted_iota(jnp.int32, shape, dim)


def row_to_col(row, count):
    wide = jnp.broadcast_to(row, (count, row.shape[1]))
    same = iota(wide.shape, 0) == iota(wide.shape, 1)
    return jnp.sum(jnp.where(same, wide, 0.0), axis=1, keepdims=True)


def col_to_row(col, offset):
    wide = jnp.broadcast_to(col, (col.shape[0], LANES))
    same = iota(wide.shape, 0) + offset == iota(wide.shape, 1)
    return jnp.sum(jnp.where(same, wide, 0.0), axis=0, keepdims=True)


def row_sum(value):
    return jnp.sum(value, axis=0, keepdims=True)


def lane_fold(value):
    total = value[:, 0:LANES]
    for k in range(1, value.shape[1] // LANES):
        total = total + value[:, k * LANES : (k + 1) * LANES]
    return total


def lane_sum(value):
    return jnp.sum(lane_fold(value), axis=1, keepdims=True)


def tiles(value):
    return jnp.concatenate([value] * NEAREST, axis=1)


def adam(param, moment, second, grad):
    moment_new = beta_one * moment + (1.0 - beta_one) * grad
    second_new = beta_two * second + (1.0 - beta_two) * grad * grad
    moment_hat = moment_new / (1.0 - beta_one**step_count)
    second_hat = second_new / (1.0 - beta_two**step_count)
    param_new = param - learn_rate * (
        moment_hat / (jnp.sqrt(second_hat) + adam_eps) + decay_rate * param
    )
    return param_new, moment_new, second_new


def peer(me, step, count):
    if count & (count - 1) == 0:
        return me ^ (count - step)
    return lax.rem(me + step, count)


def block_kernel(
    n_rows, n_cols,
    feat_h, coords_h, valid_h, nbrs_h, cot_h, weights_h, master_h, first_h, second_h,
    out_h, gfeat_h, gnorm_h, new_master_h, new_first_h, new_second_h, weights_out,
    feat, coords, valid, nbrs, cot, w_first, pos_first, weights, state, news, outs, norm_s, in_sem, out_sem,
    stat_send, stat_buf, stat_ssem, stat_rsem,
    tail1d, mats, onehot, vgat, att, wpre, uact, dyw, rel, pos, act, pmask, allow, dmix,
    a1_s, z_s, h_s, h_ts, q_s, k_s, ba_s, o_s, do_s, dv_s, sk_s, bd_s, dp_s, ds_s, xs, dz_s, dz16,
    flat, pair_got, part16, got16, sums, owned, tail_g, slab_f, shard_w, all_w,
    pair_ssem, pair_rsem, rs_ssem, rs_rsem, own_ssem, own_rsem, ag_ssem, ag_rsem, fw_ssem, fw_rsem,
):
    n = n_rows * n_cols
    half = n // 2
    row_id, col_id = lax.axis_index("rows"), lax.axis_index("cols")
    me = row_id * n_cols + col_id
    core = lax.rem(col_id, 2)
    chip = me // 2
    points = feat.shape[0]
    blocks = points // LANES
    starts = [min(max(LANES * b - (WINDOW - LANES) // 2, 0), points - WINDOW) for b in range(blocks)]
    total_len = weights.shape[0]
    shard_len = master_h.shape[0]
    shard_rows = -(-tail_g.shape[0] // LANES)
    sliced = flat.shape[0]
    slots = got16.shape[0]
    sides = own_ssem.shape[1]
    span = own_rsem.shape[0]

    def place(device):
        return (device // n_cols, lax.rem(device, n_cols))

    barrier = pltpu.get_barrier_semaphore()

    def greet(k, carry):
        pl.semaphore_signal(barrier, inc=1, device_id=place(peer(me, k, n)), device_id_type=MESH)
        return carry

    lax.fori_loop(1, n, greet, 0)
    loads = []

    def load(source, target):
        copy = pltpu.make_async_copy(source, target, in_sem.at[len(loads)])
        copy.start()
        loads.append(copy)
        return copy

    stores = []

    def store(source, target):
        copy = pltpu.make_async_copy(source, target, out_sem.at[len(stores)])
        copy.start()
        stores.append(copy)

    early = [
        load(feat_h, feat),
        load(weights_h.at[pl.ds(0, SQUARE)], w_first),
        load(weights_h.at[pl.ds(OFF_TAIL, 1024)], pos_first),
        load(nbrs_h, nbrs),
        load(coords_h, coords),
        load(valid_h, valid),
    ]

    late = [load(weights_h, weights), load(cot_h, cot)]
    for source, target in ((master_h, 0), (first_h, 1), (second_h, 2)):
        late.append(load(source, state[target]))
    owned[...] = jnp.zeros(owned.shape, f32)
    for copy in early:
        copy.wait()

    sent = []

    def all_sum(index, message):
        rows = message.shape[0]
        stat_send[index, 0:rows] = message
        stat_buf[index, me, 0:rows] = message

        def post(k, carry):
            pltpu.make_async_remote_copy(
                src_ref=stat_send.at[index, pl.ds(0, rows)],
                dst_ref=stat_buf.at[index, me, pl.ds(0, rows)],
                send_sem=stat_ssem.at[index],
                recv_sem=stat_rsem.at[index],
                device_id=place(peer(me, k, n)),
                device_id_type=MESH,
            ).start()
            return carry

        lax.fori_loop(1, n, post, 0)
        sent.append((index, rows))

        def collect():
            span = stat_buf.at[index, pl.ds(0, n - 1), pl.ds(0, rows)]
            pltpu.make_async_copy(span, span, stat_rsem.at[index]).wait()
            return jnp.sum(stat_buf[index, :, 0:rows], axis=0)

        return collect

    sibling = (row_id, col_id + 1 - 2 * core)
    per_matrix = SQUARE // SLICE // 2

    def put_matrix(m, grad):
        flat[m * per_matrix : (m + 1) * per_matrix] = grad.reshape(per_matrix, 2, SLICE_ROWS, LANES)

    def exchange(group, begin, count):
        copy = pltpu.make_async_remote_copy(
            src_ref=flat.at[pl.ds(begin, count), 1 - core],
            dst_ref=pair_got.at[pl.ds(begin, count)],
            send_sem=pair_ssem.at[group],
            recv_sem=pair_rsem.at[group],
            device_id=sibling,
            device_id_type=MESH,
        )
        copy.start()
        return copy, begin, count

    def send_slice(index, slot, other):
        pltpu.make_async_remote_copy(
            src_ref=part16.at[index],
            dst_ref=got16.at[slot, chip],
            send_sem=rs_ssem.at[slot],
            recv_sem=rs_rsem.at[slot],
            device_id=place(2 * other + core),
            device_id_type=MESH,
        ).start()

    def send_group(pair):
        copy, begin, count = pair
        copy.wait()
        part16[pl.ds(begin, count)] = (
            flat[pl.ds(begin, count), core] + pair_got[pl.ds(begin, count)]
        ).astype(bf16)
        if count % half == 0 and begin % half == 0:
            for slot in range(begin // half, (begin + count) // half):

                def post(k, carry, slot=slot):
                    other = peer(chip, k, half)
                    send_slice(slot * half + other, slot, other)
                    return carry

                lax.fori_loop(1, half, post, 0)
        else:

            def post_any(k, carry):
                index = begin + k
                slot, other = index // half, lax.rem(index, half)

                @pl.when(other != chip)
                def _():
                    send_slice(index, slot, other)

                return carry

            lax.fori_loop(0, count, post_any, 0)

    def drain_stats(index, rows):
        span = stat_buf.at[index, pl.ds(0, n - 1), pl.ds(0, rows)]
        pltpu.make_async_copy(span, span, stat_ssem.at[index]).wait()

    w_in = w_first[...].reshape(WIDTH, WIDTH)
    mats[0] = w_in
    w_in = mats[0]
    pos_in = pos_first[...].reshape(1024 // LANES, LANES)[0:1].astype(f32)
    lane8 = iota((8, 1), 0)

    def pos_in_col(c):
        return jnp.where(lane8 < 3, row_to_col(pos_in[:, 3 * c : 3 * c + 8], 8), 0.0)

    valid_rows = valid[...].reshape(points // LANES, LANES).astype(f32)
    n_valid = jnp.sum(jnp.sum(valid_rows, axis=0, keepdims=True), axis=1, keepdims=True)
    point_mask = (iota((points, 1), 0).astype(f32) < n_valid).astype(f32)
    lane_mask = (iota((1, points), 1).astype(f32) < n_valid).astype(f32)

    a1 = nn(feat[...], w_in)
    a1_s[...] = a1
    masked = point_mask * a1
    sum_a, sqr_a = row_sum(masked), row_sum(masked * a1)

    window_row = iota((WINDOW, LANES), 0)
    for b in range(blocks):
        for j in range(NEAREST):
            index = nbrs[j : j + 1, b * LANES : (b + 1) * LANES] - starts[b]
            onehot[b, :, j * LANES : (j + 1) * LANES] = jnp.where(
                window_row == index, 1.0, 0.0
            ).astype(bf16)

    coords8 = jnp.concatenate([coords[...], jnp.zeros((5, points), f32)], axis=0)
    table = jnp.concatenate(
        split(coords8, 3) + [jnp.broadcast_to(lane_mask, (8, points)).astype(bf16)], axis=0
    )
    slot0 = (iota((1, PAIRS), 1) < LANES).astype(f32)
    pos_in_cols = [pos_in_col(c) for c in range(3)]
    sum_p = jnp.zeros((8, 1), f32)
    sqr_p = jnp.zeros((8, 1), f32)
    pairs_local = jnp.zeros((1, 1), f32)
    for b in range(blocks):
        here = slice(b * LANES, (b + 1) * LANES)
        fetched = nn(table[:, starts[b] : starts[b] + WINDOW], onehot[b])
        place_n = fetched[0:8] + fetched[8:16] + fetched[16:24]
        mask_n = fetched[24:32]
        r = place_n - tiles(coords8[:, here])
        pm = mask_n * tiles(lane_mask[:, here])
        p = pos_in_cols[0] * r[0:1] + pos_in_cols[1] * r[1:2] + pos_in_cols[2] * r[2:3]
        rel[b] = r
        pos[b] = p
        pmask[b] = pm
        allow[b] = jnp.maximum(mask_n, slot0)
        sum_p = sum_p + lane_sum(pm * p)
        sqr_p = sqr_p + lane_sum(pm * p * p)
        pairs_local = pairs_local + lane_sum(pm[0:1])

    lane = iota((1, LANES), 1)
    last = (
        col_to_row(sum_p, 0)
        + col_to_row(sqr_p, 8)
        + jnp.where(lane == 16, n_valid, 0.0)
        + jnp.where(lane == 17, pairs_local, 0.0)
    )

    def fold(row):
        return jnp.concatenate([row[:, 0:LANES], row[:, LANES:WIDTH]], axis=0)

    def unfold(rows):
        return jnp.concatenate([rows[0:1], rows[1:2]], axis=1)

    pl.semaphore_wait(barrier, n - 1)
    collect_first = all_sum(0, jnp.concatenate([fold(sum_a), fold(sqr_a), last], axis=0))
    for copy in late:
        copy.wait()
    for m in range(1, 5):
        mats[m] = weights[pl.ds(m * SQUARE, SQUARE)].reshape(WIDTH, WIDTH)
    w_q, w_k, w_v, w_o = (mats[m] for m in range(1, 5))
    att_in = weights[pl.ds(OFF_ATT_IN, WIDTH * GROUPS)].reshape(WIDTH * GROUPS // LANES, LANES)
    att_in_f = att_in.astype(f32).reshape(WIDTH, GROUPS)
    att_in_t = att_in_f.T.astype(bf16)
    att_out_f = (
        weights[pl.ds(OFF_ATT_OUT, GROUPS * GROUPS)]
        .reshape(GROUPS * GROUPS // LANES, LANES)
        .astype(f32)
        .reshape(GROUPS, GROUPS)
    )
    att_out = att_out_f.astype(bf16)
    att_out_t = att_out_f.T.astype(bf16)
    tail1d[pl.ds(0, 1024)] = weights[pl.ds(OFF_TAIL, 1024)]
    rest = total_len - OFF_TAIL - 1024
    tail1d[pl.ds(1024, rest)] = weights[pl.ds(OFF_TAIL + 1024, rest)]
    tail = tail1d[pl.ds(0, TAIL_PAD)].reshape(TAIL_PAD // LANES, LANES).astype(f32)
    tail = jnp.concatenate([tail[k : k + 1] for k in range(TAIL_PAD // LANES)], axis=1)
    pos_rows = [tail[:, TAIL_POS_OUT + WIDTH * d : TAIL_POS_OUT + WIDTH * (d + 1)] for d in range(3)]
    def norm_pieces(start):
        ends = [0, WIDTH, WIDTH + 3, WIDTH + 3 + GROUPS, NORMS]
        return [tail[:, start + ends[k] : start + ends[k + 1]] for k in range(4)]

    gain_a, gain_p, gain_w, gain_o = norm_pieces(TAIL_GAINS)
    shift_a, shift_p, shift_w, shift_o = norm_pieces(TAIL_SHIFTS)

    def pad_col(row):
        wide = jnp.concatenate([row, jnp.zeros((1, 5), f32)], axis=1)
        return row_to_col(wide, 8)

    gain_p, shift_p = pad_col(gain_p), pad_col(shift_p)
    gain_w, shift_w = row_to_col(gain_w, GROUPS), row_to_col(shift_w, GROUPS)

    new_at = iota((WIDTH, WIDTH), 0)
    reorder = jnp.where(
        iota((WIDTH, WIDTH), 1) == new_at % GROUPS * PER_GROUP + new_at // GROUPS, 1.0, 0.0
    ).astype(bf16)
    w_o_new = nn(reorder, w_o)
    mats[4] = w_o_new.astype(bf16)
    mats[5] = w_o_new.T.astype(bf16)
    mats[6] = w_q.astype(f32).T.astype(bf16)
    mats[7] = w_k.astype(f32).T.astype(bf16)
    mats[8] = nt(reorder, w_v).astype(bf16)
    pos_mat = jnp.concatenate(pos_rows + [jnp.zeros((13, WIDTH), f32)], axis=0).astype(bf16)
    pos_cols = nt(reorder, pos_mat)
    pos_cols = [pos_cols[:, d : d + 1] for d in range(3)]
    stats = collect_first()

    def pick(row, at):
        return jnp.sum(jnp.where(lane == at, row, 0.0), axis=1, keepdims=True)

    point_count, pair_count = pick(stats[4:5], 16), pick(stats[4:5], 17)
    inv_points, inv_pairs = 1.0 / point_count, 1.0 / pair_count

    def moments(total, square, inv):
        mean = total * inv
        return mean, lax.rsqrt(square * inv - mean * mean + bn_eps)

    mean_a, rs_a = moments(unfold(stats[0:2]), unfold(stats[2:4]), inv_points)
    mean_p, rs_p = moments(
        row_to_col(stats[4:5, 0:8], 8), row_to_col(stats[4:5, 8:16], 8), inv_pairs
    )

    h = silu_parts((a1_s[...] - mean_a) * rs_a * gain_a + shift_a)[0]
    h_s[...] = h.astype(bf16)
    h_t = h.T.astype(bf16)
    q_t = nn(mats[6], h_t).astype(bf16)
    k_t = nn(mats[7], h_t).astype(bf16)
    q_s[...] = q_t
    k_s[...] = k_t
    h_ts[...] = h_t
    q_att = nn(att_in_t, q_t)
    k_att = jnp.concatenate(split(nn(att_in_t, k_t), 3), axis=0)
    pos_att = nt(att_in_t, pos_mat)
    pos_att_cols = [pos_att[:, d : d + 1] for d in range(3)]
    back_att = jnp.concatenate([nn(att_in_t, mats[6]), nn(att_in_t, mats[7])], axis=0)
    for k, piece in enumerate(split(back_att, 2)):
        ba_s[k] = piece

    sum_w = jnp.zeros((GROUPS, LANES), f32)
    sqr_w = jnp.zeros((GROUPS, LANES), f32)
    for b in range(blocks):
        here = slice(b * LANES, (b + 1) * LANES)
        active = silu_parts((pos[b] - mean_p) * rs_p * gain_p + shift_p)[0]
        act[b] = active
        fetched = nn(k_att[:, starts[b] : starts[b] + WINDOW], onehot[b])
        w = tiles(q_att[:, here]) - (
            fetched[0:GROUPS] + fetched[GROUPS : 2 * GROUPS] + fetched[2 * GROUPS : 3 * GROUPS]
        )
        for d in range(3):
            w = w + pos_att_cols[d] * active[d : d + 1]
        wpre[b] = w
        mw = w * pmask[b, 0:1]
        sum_w = sum_w + lane_fold(mw)
        sqr_w = sqr_w + lane_fold(mw * w)

    def pair_row(one, two):
        one = jnp.sum(one, axis=1, keepdims=True)
        two = jnp.sum(two, axis=1, keepdims=True)
        return col_to_row(one, 0) + col_to_row(two, GROUPS)

    collect_w = all_sum(1, pair_row(sum_w, sqr_w))
    v_t = nn(mats[8], h_ts[...]).astype(bf16)
    for b in range(blocks):
        vgat[b] = nn(v_t[:, starts[b] : starts[b] + WINDOW], onehot[b])
    stats = collect_w()
    mean_w, rs_w = moments(
        row_to_col(stats[:, 0:GROUPS], GROUPS),
        row_to_col(stats[:, GROUPS : 2 * GROUPS], GROUPS),
        inv_pairs,
    )

    def each_channel(value):
        return jnp.concatenate([value] * PER_GROUP, axis=0)

    def over_channels(value):
        return functools.reduce(
            jnp.add, [value[c * GROUPS : (c + 1) * GROUPS] for c in range(PER_GROUP)]
        )

    def cols(j):
        return slice(j * LANES, (j + 1) * LANES)

    for b in range(blocks):
        here = slice(b * LANES, (b + 1) * LANES)
        u = silu_parts((wpre[b] - mean_w) * rs_w * gain_w + shift_w)[0].astype(bf16)
        uact[b] = u
        logit = jnp.where(allow[b, 0:1] > 0.5, nn(att_out_t, u), masked_logit)
        top = logit[:, cols(0)]
        for j in range(1, NEAREST):
            top = jnp.maximum(top, logit[:, cols(j)])
        weight = jnp.exp(logit - tiles(top))
        share = 1.0 / functools.reduce(jnp.add, [weight[:, cols(j)] for j in range(NEAREST)])
        att[b] = weight * tiles(share)
        mixed = jnp.zeros((WIDTH, LANES), f32)
        enc = [jnp.zeros((GROUPS, LANES), f32) for _ in range(3)]
        for j in range(NEAREST):
            a = att[b, :, cols(j)]
            mixed = mixed + each_channel(a) * vgat[b, :, cols(j)]
            for d in range(3):
                enc[d] = enc[d] + a * act[b, d : d + 1, cols(j)]
        bd_s[:, here] = jnp.concatenate(enc, axis=0)
        for d in range(3):
            mixed = mixed + pos_cols[d] * each_channel(enc[d])
        o_s[here, :] = mixed.T.astype(bf16)

    z = nn(o_s[...], mats[4])
    z_s[...] = z
    masked = point_mask * z
    collect_o = all_sum(2, jnp.concatenate([fold(row_sum(masked)), fold(row_sum(masked * z))], axis=0))
    stats = collect_o()
    mean_o, rs_o = moments(unfold(stats[0:2]), unfold(stats[2:4]), inv_points)

    zhat = (z_s[...] - mean_o) * rs_o
    y = feat[...].astype(f32) + zhat * gain_o + shift_o
    value, gate = silu_parts(y)
    outs[0] = (point_mask * value).astype(bf16)
    store(outs.at[0], out_h)
    dy = point_mask * cot[...].astype(f32) * silu_slope(y, gate)
    dz_s[...] = dy
    shift_grad_o, gain_grad_o = row_sum(dy), row_sum(dy * zhat)
    stats = all_sum(3, jnp.concatenate([fold(shift_grad_o), fold(gain_grad_o)], axis=0))()
    one, two = unfold(stats[0:2]) * inv_points, unfold(stats[2:4]) * inv_points
    zhat = (z_s[...] - mean_o) * rs_o
    dz = (gain_o * rs_o * (dz_s[...] - point_mask * (one + zhat * two))).astype(bf16)
    dz16[...] = dz
    do_s[...] = nn(dz, mats[5]).T

    sum_w = jnp.zeros((GROUPS, LANES), f32)
    sqr_w = jnp.zeros((GROUPS, LANES), f32)
    for b in range(blocks):
        here = slice(b * LANES, (b + 1) * LANES)
        do = do_s[:, here]
        do_pos = [over_channels(do * pos_cols[d]) for d in range(3)]
        dp_s[:, here] = jnp.concatenate(do_pos, axis=0)
        da = []
        for j in range(NEAREST):
            grad = over_channels(do * vgat[b, :, cols(j)])
            for d in range(3):
                grad = grad + do_pos[d] * act[b, d : d + 1, cols(j)]
            da.append(grad)
        mean_da = functools.reduce(jnp.add, [da[j] * att[b, :, cols(j)] for j in range(NEAREST)])
        ds = jnp.concatenate(
            [att[b, :, cols(j)] * (da[j] - mean_da) for j in range(NEAREST)], axis=1
        ).astype(bf16)
        ds_s[b] = ds
        what = (wpre[b] - mean_w) * rs_w
        y = what * gain_w + shift_w
        gate = silu_parts(y)[1]
        dy = nn(att_out, ds) * silu_slope(y, gate)
        dyw[b] = dy
        sum_w = sum_w + lane_fold(dy)
        sqr_w = sqr_w + lane_fold(dy * what)

    back_w = pair_row(sum_w, sqr_w)
    collect_w = all_sum(4, back_w)
    put_matrix(4, tn(nn(o_s[...], reorder).astype(bf16), dz16[...]))
    dv_s[...] = jnp.zeros(dv_s.shape, f32)
    for b in range(blocks):
        here = slice(b * LANES, (b + 1) * LANES)
        do = do_s[:, here]
        for j in range(NEAREST):
            xs[:, cols(j)] = (each_channel(att[b, :, cols(j)]) * do).astype(bf16)
        dv_s[pl.ds(starts[b], WINDOW)] += nt(onehot[b], xs[...])
    dv = nn(dv_s[...].astype(bf16), reorder).astype(bf16)
    put_matrix(3, tn(h_s[...], dv))
    late_pair = exchange(0, 3 * per_matrix, 2 * per_matrix)
    dv_s[...] = nt(dv, w_v)
    d_att_out = jnp.zeros((GROUPS, GROUPS), f32)
    for b in range(blocks):
        here = slice(b * LANES, (b + 1) * LANES)
        d_att_out = d_att_out + nt(uact[b], ds_s[b])
        mix = []
        for j in range(NEAREST):
            a = att[b, :, cols(j)]
            back = [row_sum(dp_s[d * GROUPS : (d + 1) * GROUPS, here] * a) for d in range(3)]
            mix.append(jnp.concatenate(back + [jnp.zeros((5, LANES), f32)], axis=0))
        dmix[b] = jnp.concatenate(mix, axis=1)
    send_group(late_pair)
    stats = collect_w()
    one = row_to_col(stats[:, 0:GROUPS], GROUPS) * inv_pairs
    two = row_to_col(stats[:, GROUPS : 2 * GROUPS], GROUPS) * inv_pairs

    sk_s[...] = jnp.zeros(sk_s.shape, f32)
    pos_att_rows = split(pos_att[:, 0:8].T, 3)
    pos_att_rows = jnp.concatenate(pos_att_rows, axis=0)
    dw_sums = []
    sum_p = jnp.zeros((8, 1), f32)
    sqr_p = jnp.zeros((8, 1), f32)
    for b in range(blocks):
        what = (wpre[b] - mean_w) * rs_w
        dw_f = gain_w * rs_w * (dyw[b] - pmask[b, 0:1] * (one + what * two))
        dw = dw_f.astype(bf16)
        sk_s[pl.ds(starts[b], WINDOW)] += nt(onehot[b], dw)
        dw_sums.append(lane_slots(dw.astype(f32)))
        ds_s[b] = dw
        back = nn(pos_att_rows, dw)
        d_act = dmix[b] + back[0:8] + back[8:16] + back[16:24]
        phat = (pos[b] - mean_p) * rs_p
        y = phat * gain_p + shift_p
        gate = silu_parts(y)[1]
        dy = d_act * silu_slope(y, gate)
        dmix[b] = dy
        sum_p = sum_p + lane_sum(dy)
        sqr_p = sqr_p + lane_sum(dy * phat)
    dq_att = jnp.concatenate(dw_sums, axis=1)
    both_att = jnp.concatenate([dq_att.T, -sk_s[...]], axis=1)
    both_split = split(both_att, 2)
    dh = nn(both_split[0], ba_s[0]) + nn(both_split[1], ba_s[0]) + nn(both_split[0], ba_s[1])
    dh = dh + dv_s[...]
    ahat = (a1_s[...] - mean_a) * rs_a
    y = ahat * gain_a + shift_a
    gate = silu_parts(y)[1]
    dy = dh * silu_slope(y, gate)
    z_s[...] = dy
    shift_grad_a, gain_grad_a = row_sum(dy), row_sum(dy * ahat)
    last = col_to_row(sum_p, 0) + col_to_row(sqr_p, 8)
    collect_a = all_sum(
        5, jnp.concatenate([fold(shift_grad_a), fold(gain_grad_a), last], axis=0)
    )

    dq_split = split(dq_att, 2)
    dk_split = [piece[:, GROUPS : 2 * GROUPS] for piece in both_split]
    dq = sum(tn(piece, att_in_t) for piece in dq_split).astype(bf16)
    dk = sum(nn(piece, att_in_t) for piece in dk_split).astype(bf16)
    put_matrix(1, tn(h_s[...], dq))
    put_matrix(2, tn(h_s[...], dk))
    send_group(exchange(1, per_matrix, 2 * per_matrix))
    d_pos_att = sum(
        nt(jnp.concatenate(split(act[b], 3), axis=0), ds_s[b]) for b in range(blocks)
    )
    d_pos_att = d_pos_att[0:8] + d_pos_att[8:16] + d_pos_att[16:24]
    d_pos_split = split(d_pos_att, 3)
    d_att_in = sum(nt(q_s[...], piece) for piece in dq_split)
    d_att_in = d_att_in + sum(nn(k_s[...], piece) for piece in dk_split)
    d_att_in = d_att_in + sum(tn(pos_mat[0:8], piece) for piece in d_pos_split)
    d_pos_out = sum(nn(piece, att_in_t) for piece in d_pos_split)
    do_split = split(do_s[...], 2)
    bd_split = split(bd_s[...], 2)
    cross = nt(bd_split[0], do_split[0]) + nt(bd_split[0], do_split[1]) + nt(bd_split[1], do_split[0])
    own_group = iota((GROUPS, WIDTH), 1) % GROUPS == iota((GROUPS, WIDTH), 0)
    cross = [
        row_sum(jnp.where(own_group, cross[d * GROUPS : (d + 1) * GROUPS], 0.0)) for d in range(3)
    ]
    cross = jnp.concatenate(cross + [jnp.zeros((5, WIDTH), f32)], axis=0)
    d_pos_out = d_pos_out + sum(nn(piece, reorder) for piece in split(cross, 3))
    d_pos_rows = [d_pos_out[d : d + 1] for d in range(3)]
    small = 5 * per_matrix
    pieces_rows = [
        d_att_in.reshape(WIDTH * GROUPS // LANES, LANES),
        d_att_out.reshape(GROUPS * GROUPS // LANES, LANES),
    ]
    along, along_hat, offsets = [], [], []
    for c in range(3):
        one = [jnp.zeros((8, 1), f32) for _ in range(3)]
        for b in range(blocks):
            masked = pmask[b] * rel[b, c : c + 1]
            one[0] = one[0] + lane_sum(dmix[b] * rel[b, c : c + 1])
            one[1] = one[1] + lane_sum(masked * ((pos[b] - mean_p) * rs_p))
            one[2] = one[2] + lane_sum(masked)
        along.append(one[0])
        along_hat.append(one[1])
        offsets.append(one[2])
    stats = collect_a()
    one, two = unfold(stats[0:2]) * inv_points, unfold(stats[2:4]) * inv_points
    ahat = (a1_s[...] - mean_a) * rs_a
    da1 = (gain_a * rs_a * (z_s[...] - point_mask * (one + ahat * two))).astype(bf16)
    put_matrix(0, tn(feat[...], da1))
    first_pair = exchange(2, 0, per_matrix)
    one = row_to_col(stats[4:5, 0:8], 8) * inv_pairs
    two = row_to_col(stats[4:5, 8:16], 8) * inv_pairs
    pieces = []
    for c in range(3):
        d_pos_in = gain_p * rs_p * (along[c] - one * offsets[c] - two * along_hat[c])
        pieces.append(col_to_row(d_pos_in, 0)[:, 0:3])
    pieces = pieces + d_pos_rows
    pieces = pieces + [
        gain_grad_a, col_to_row(sqr_p, 0)[:, 0:3], back_w[:, GROUPS : 2 * GROUPS], gain_grad_o,
        shift_grad_a, col_to_row(sum_p, 0)[:, 0:3], back_w[:, 0:GROUPS], shift_grad_o,
        jnp.zeros((1, TAIL_PAD - TAIL_USED), f32),
    ]
    pieces_rows.append(jnp.concatenate(pieces, axis=1).reshape(TAIL_PAD // LANES, LANES))
    used_rows = OFF_TAIL // LANES + TAIL_PAD // LANES - 5 * SQUARE // LANES
    spare_rows = (sliced - small) * 2 * SLICE_ROWS - used_rows
    pieces_rows.append(jnp.zeros((spare_rows, LANES), f32))
    flat[small:sliced] = jnp.concatenate(pieces_rows, axis=0).reshape(
        sliced - small, 2, SLICE_ROWS, LANES
    )
    small_pair = exchange(3, small, sliced - small)
    send_group(first_pair)
    send_group(small_pair)
    outs[1] = (dz_s[...] + nt(da1, w_in)).astype(bf16)
    store(outs.at[1], gfeat_h)

    squares = jnp.zeros((1, 1), f32)
    for slot in list(range(1, slots)) + [0]:
        index = slot * half + chip
        if (slot + 1) * half <= sliced:
            here = None
        else:
            here = index < sliced

        def take(slot=slot, index=index):
            got = got16.at[slot, pl.ds(0, half - 1)]
            pltpu.make_async_copy(got, got, rs_rsem.at[slot]).wait()
            total = flat[index, core] + pair_got[index]

            def add(k, total):
                return total + got16[slot, peer(chip, k, half)].astype(f32)

            sums[slot] = lax.fori_loop(1, half, add, total, unroll=half <= 16)

        if here is None:
            take()
        else:
            sums[slot] = jnp.zeros((SLICE_ROWS, LANES), f32)
            pl.when(here)(take)
        squares = squares + lane_sum(row_sum(sums[slot] * sums[slot]))

    collect_norm = all_sum(6, jnp.where(lane == 0, squares, 0.0))

    def slice_of(slot):
        return 2 * (slot * half + chip) + core

    def each_owner(slot, act_on):
        number = slice_of(slot)
        low = number * SLICE // shard_len
        high = jnp.minimum((number * SLICE + SLICE - 1) // shard_len, n - 1)
        for side in range(sides):
            owner = low + side

            @pl.when((number * SLICE < total_len) & (owner <= high))
            def _(owner=owner, side=side):
                act_on(owner, number - owner * shard_len // SLICE, side)

    def owned_rows(k):
        return owned.at[pl.ds(pl.multiple_of(k * SLICE_ROWS, SLICE_ROWS), SLICE_ROWS)]

    def own_copy(slot, owner, k, side):
        return pltpu.make_async_remote_copy(
            src_ref=sums.at[slot],
            dst_ref=owned_rows(k),
            send_sem=own_ssem.at[slot, side],
            recv_sem=own_rsem.at[k],
            device_id=place(owner),
            device_id_type=MESH,
        )

    for slot in range(slots):

        def hand_over(owner, k, side, slot=slot):
            @pl.when(owner != me)
            def _():
                own_copy(slot, owner, k, side).start()

            @pl.when(owner == me)
            def _():
                owned_rows(k)[...] = sums[slot]

        each_owner(slot, hand_over)

    begin = me * shard_len
    first_slice = begin // SLICE
    last_slice = (begin + shard_len - 1) // SLICE
    for k in range(span):
        number = first_slice + k

        @pl.when((number <= last_slice) & (lax.rem(number, n) != me))
        def _(k=k):
            rows = owned.at[pl.ds(k * SLICE_ROWS, SLICE_ROWS)]
            pltpu.make_async_copy(rows, rows, own_rsem.at[k]).wait()

    offset = begin - first_slice * SLICE
    skip = lax.rem(offset, LANES)
    lanes_all = iota((shard_rows, LANES), 1)
    rows = owned[pl.ds(offset // LANES, shard_rows), :]
    turned = pltpu.roll(rows, lax.rem(LANES - skip, LANES), 1)
    below = pltpu.roll(turned, shard_rows - 1, 0)
    grad = jnp.where(lanes_all < LANES - skip, turned, below)
    inside = iota(grad.shape, 0) * LANES + lanes_all < shard_len
    grad = jnp.where(inside, grad, 0.0)

    stats = collect_norm()
    norm = jnp.sqrt(pick(stats, 0))
    norm_s[...] = jnp.broadcast_to(norm, norm_s.shape)
    grad = grad * jnp.minimum(1.0, clip_norm / norm)

    main = shard_len // 1024 * 1024
    spare = shard_len - main
    tail_g[...] = grad.reshape(shard_rows * LANES)
    for start, size in ((0, main), (main, spare)):
        if size == 0:
            continue
        at = pl.ds(start, size)
        p_new, m_new, s_new = adam(state[0][at], state[1][at], state[2][at], tail_g[at])
        news[0][at] = p_new
        news[1][at] = m_new
        news[2][at] = s_new
        tail_g[at] = p_new
    moved = jnp.where(inside, tail_g[...].reshape(shard_rows, LANES), 0.0)
    turned = pltpu.roll(moved, skip, 1)
    above = pltpu.roll(turned, 1, 0)
    slab_f[...] = jnp.zeros(slab_f.shape, f32)
    slab_f[pl.ds(lax.rem(begin, CHUNK) // LANES, shard_rows), :] = jnp.where(
        lanes_all < skip, above, turned
    )
    shard_w[...] = slab_f[...].astype(bf16)
    all_w[core, chip] = slab_f[...].astype(bf16)

    in_row = n_cols // 2
    row_chip = col_id // 2

    def send_slab(source, slab, row, chip_in_row):
        pltpu.make_async_remote_copy(
            src_ref=source,
            dst_ref=all_w.at[core, slab],
            send_sem=ag_ssem,
            recv_sem=ag_rsem.at[slab],
            device_id=(row, 2 * chip_in_row + core),
            device_id_type=MESH,
        ).start()

    def forward(other):
        pltpu.make_async_remote_copy(
            src_ref=all_w.at[core, other],
            dst_ref=all_w.at[core, other],
            send_sem=fw_ssem,
            recv_sem=fw_rsem,
            device_id=sibling,
            device_id_type=MESH,
        ).start()

    def arrived(other):
        pltpu.make_async_copy(shard_w, shard_w, ag_rsem.at[other]).wait()

    def send_along(k, carry):
        send_slab(shard_w, chip, peer(row_id, k, n_rows), row_chip)
        return carry

    def send_within(k, carry):
        send_slab(shard_w, chip, row_id, peer(row_chip, k, in_row))
        return carry

    lax.fori_loop(1, n_rows, send_along, 0)
    lax.fori_loop(1, in_row, send_within, 0)
    forward(chip)
    store(norm_s, gnorm_h)
    for source, target in ((0, new_master_h), (1, new_first_h), (2, new_second_h)):
        store(news[source], target)

    def spread_row(k, carry):
        other = peer(row_id, n_rows - k, n_rows) * in_row + row_chip
        arrived(other)

        def send_on(i, carry):
            send_slab(all_w.at[core, other], other, row_id, peer(row_chip, i, in_row))
            return carry

        lax.fori_loop(1, in_row, send_on, 0)
        forward(other)
        return carry

    lax.fori_loop(1, n_rows, spread_row, 0)

    def pass_on(k, carry):
        step = k // (in_row - 1)
        row = jnp.where(step == 0, row_id, peer(row_id, n_rows - step, n_rows))
        other = row * in_row + peer(row_chip, in_row - 1 - lax.rem(k, in_row - 1), in_row)
        arrived(other)
        forward(other)
        return carry

    lax.fori_loop(0, n_rows * (in_row - 1), pass_on, 0)
    pltpu.make_async_copy(all_w.at[core], all_w.at[core], fw_rsem).wait()
    rows = CHUNK // LANES

    def chunk(c):
        value = None
        last_owner = min((c * CHUNK + CHUNK - 1) // shard_len, n - 1)
        for owner in range(c * CHUNK // shard_len, last_owner + 1):
            k = c - owner * shard_len // CHUNK
            part = all_w[owner % 2, owner // 2, rows * k : rows * (k + 1)].astype(f32)
            value = part if value is None else value + part
        return value

    whole = total_len // (2 * CHUNK)
    for c in range(whole):
        both = jnp.concatenate([chunk(2 * c), chunk(2 * c + 1)], axis=0)
        weights_out[pl.ds(2 * CHUNK * c, 2 * CHUNK)] = both.astype(bf16).reshape(2 * CHUNK)
    left = total_len - whole * 2 * CHUNK
    if left:
        parts = [chunk(2 * whole)]
        parts.append(chunk(2 * whole + 1) if left > CHUNK else jnp.zeros((rows, LANES), f32))
        both = jnp.concatenate(parts, axis=0).astype(bf16).reshape(2 * CHUNK)
        weights_out[pl.ds(2 * CHUNK * whole, left)] = both[0:left]

    for index, rows in sent:
        drain_stats(index, rows)
    for copy in stores:
        copy.wait()
    pltpu.make_async_copy(all_w.at[core], all_w.at[core], fw_ssem).wait()
    rest = all_w.at[core, pl.ds(0, half - 1)]
    pltpu.make_async_copy(rest, rest, ag_ssem).wait()
    for slot in range(slots):
        count = min(sliced - slot * half, half)

        def drain(k, carry, slot=slot):
            pltpu.make_async_copy(part16.at[0], part16.at[0], rs_ssem.at[slot]).wait()
            return carry

        lax.fori_loop(0, count - (chip < count).astype(jnp.int32), drain, 0)

        def own_drain(owner, k, side, slot=slot):
            @pl.when(owner != me)
            def _():
                own_copy(slot, owner, k, side).wait_send()

        each_owner(slot, own_drain)


def finish_kernel(
    out_t, gfeat_t, gnorm_t, master_t, first_t, second_t, weights_t,
    out_h, gfeat_h, gnorm, master_h, first_h, second_h, weights_h,
    norm_s, sem,
):
    copies = [
        pltpu.make_async_copy(source, target, sem.at[k])
        for k, (source, target) in enumerate(
            (
                (weights_t, weights_h),
                (out_t, out_h),
                (gfeat_t, gfeat_h),
                (master_t, master_h),
                (first_t, first_h),
                (second_t, second_h),
                (gnorm_t, norm_s),
            )
        )
    ]
    for copy in copies:
        copy.start()
    copies[-1].wait()
    gnorm[...] = norm_s[0:1, 0:1]
    for copy in copies[:-1]:
        copy.wait()


def lane_slots(value):
    return functools.reduce(
        jnp.add, [value[:, j * LANES : (j + 1) * LANES] for j in range(NEAREST)]
    )


def shards(
    n_rows, n_cols,
    features, coords, valid_mask, neighbors, cotangent, weights, master, first_moment, second_moment,
):
    n = n_rows * n_cols
    half = n // 2
    points = features.shape[0]
    blocks = points // LANES
    shard_len = master.shape[0]
    total_len = weights.shape[0]

    def up(value, unit):
        return -(-value // unit) * unit

    shard_rows = up(-(-shard_len // LANES) + 1, 8)
    slab_rows = up(shard_rows + CHUNK // LANES, 16)
    sliced = up(-(-total_len // SLICE), 2) // 2
    slots = -(-sliced // half)
    sides = (SLICE + shard_len - 2) // shard_len + 1
    span = (SLICE + shard_len - 2) // SLICE + 1
    hbm = pl.BlockSpec(memory_space=pltpu.HBM)
    vmem = pl.BlockSpec(memory_space=pltpu.VMEM)
    dma = pltpu.SemaphoreType.DMA
    shape = jax.ShapeDtypeStruct

    def pairs(rows, dtype=f32):
        return pltpu.VMEM((blocks, rows, PAIRS), dtype)

    def shard():
        return [pltpu.VMEM(master.shape, f32) for _ in range(3)]

    scratch = [
        pltpu.VMEM(features.shape, bf16),
        pltpu.VMEM(coords.shape, f32),
        pltpu.VMEM(valid_mask.shape, jnp.int32),
        pltpu.VMEM(neighbors.shape, jnp.int32),
        pltpu.VMEM(features.shape, bf16),
        pltpu.VMEM((SQUARE,), bf16),
        pltpu.VMEM((1024,), bf16),
        pltpu.VMEM(weights.shape, bf16),
        shard(),
        shard(),
        pltpu.VMEM((2, *features.shape), bf16),
        pltpu.VMEM((1, LANES), f32),
        dma((11,)),
        dma((7,)),
        pltpu.VMEM((7, 8, LANES), f32),
        pltpu.VMEM((7, n, 8, LANES), f32),
        dma((7,)),
        dma((7,)),
        pltpu.VMEM((TAIL_PAD,), bf16),
        pltpu.VMEM((9, WIDTH, WIDTH), bf16),
        pairs(WINDOW, bf16),
        pairs(WIDTH),
        pairs(GROUPS),
        pairs(GROUPS),
        pairs(GROUPS, bf16),
        pairs(GROUPS),
        pairs(8),
        pairs(8),
        pairs(8),
        pairs(8),
        pairs(8),
        pairs(8),
        pltpu.VMEM((points, WIDTH), f32),
        pltpu.VMEM((points, WIDTH), f32),
        pltpu.VMEM((points, WIDTH), bf16),
        pltpu.VMEM((WIDTH, points), bf16),
        pltpu.VMEM((WIDTH, points), bf16),
        pltpu.VMEM((WIDTH, points), bf16),
        pltpu.VMEM((2, 2 * GROUPS, WIDTH), bf16),
        pltpu.VMEM((points, WIDTH), bf16),
        pltpu.VMEM((WIDTH, points), f32),
        pltpu.VMEM((points, WIDTH), f32),
        pltpu.VMEM((points, GROUPS), f32),
        pltpu.VMEM((3 * GROUPS, points), f32),
        pltpu.VMEM((3 * GROUPS, points), f32),
        pairs(GROUPS, bf16),
        pltpu.VMEM((WIDTH, PAIRS), bf16),
        pltpu.VMEM((points, WIDTH), f32),
        pltpu.VMEM((points, WIDTH), bf16),
        pltpu.VMEM((sliced, 2, SLICE_ROWS, LANES), f32),
        pltpu.VMEM((sliced, SLICE_ROWS, LANES), f32),
        pltpu.VMEM((sliced, SLICE_ROWS, LANES), bf16),
        pltpu.VMEM((slots, half, SLICE_ROWS, LANES), bf16),
        pltpu.VMEM((slots, SLICE_ROWS, LANES), f32),
        pltpu.VMEM((up(max(span * SLICE_ROWS, SLICE_ROWS + shard_rows), SLICE_ROWS), LANES), f32),
        pltpu.VMEM((shard_rows * LANES,), f32),
        pltpu.VMEM((slab_rows, LANES), f32),
        pltpu.VMEM((slab_rows, LANES), bf16),
        pltpu.VMEM((2, half, slab_rows, LANES), bf16),
        dma((4,)),
        dma((4,)),
        dma((slots,)),
        dma((slots,)),
        dma((slots, sides)),
        dma((span,)),
        dma,
        dma((half,)),
        dma,
        dma,
    ]
    results = pl.pallas_call(
        functools.partial(block_kernel, n_rows, n_cols),
        out_shape=(
            shape(features.shape, bf16),
            shape(features.shape, bf16),
            shape((1, LANES), f32),
            shape(master.shape, f32),
            shape(master.shape, f32),
            shape(master.shape, f32),
            pltpu.VMEM(weights.shape, bf16),
        ),
        in_specs=[hbm] * 9,
        out_specs=[pl.BlockSpec(memory_space=pl.ANY)] * 6 + [vmem],
        scratch_shapes=scratch,
        compiler_params=pltpu.CompilerParams(
            collective_id=0, has_side_effects=True, vmem_limit_bytes=40 * 2**20
        ),
    )(*(pltpu.with_memory_space_constraint(x, pltpu.HBM) for x in (features, coords, valid_mask, neighbors, cotangent, weights, master, first_moment, second_moment)))
    results = pl.pallas_call(
        finish_kernel,
        out_shape=(
            shape(features.shape, bf16),
            shape(features.shape, bf16),
            shape((1, 1), f32),
            shape(master.shape, f32),
            shape(master.shape, f32),
            shape(master.shape, f32),
            shape(weights.shape, bf16),
        ),
        in_specs=[pl.BlockSpec(memory_space=pl.ANY)] * 7,
        out_specs=[hbm, hbm, vmem, hbm, hbm, hbm, hbm],
        scratch_shapes=[pltpu.VMEM((1, LANES), f32), dma((7,))],
        compiler_params=pltpu.CompilerParams(vmem_limit_bytes=8 * 2**20),
    )(*results)
    return results[0], results[1], results[2].reshape(()), *results[3:]


def solution(mesh):
    both = ("rows", "cols")
    rows_split, cols_split, flat_split = P(both, None), P(None, both), P(both)
    return jax.shard_map(
        functools.partial(shards, mesh.shape["rows"], mesh.shape["cols"]),
        mesh=mesh,
        in_specs=(
            rows_split, cols_split, flat_split, cols_split, rows_split, P(),
            flat_split, flat_split, flat_split,
        ),
        out_specs=(rows_split, rows_split, P(), flat_split, flat_split, flat_split, P()),
        check_vma=False,
    )
```

```python
import functools

import jax
import jax.numpy as jnp
from jax import lax
from jax.experimental import pallas as pl
from jax.experimental.pallas import tpu as pltpu
from jax.sharding import PartitionSpec as P

WIDTH = 256
GROUPS = 32
NEAREST = 16
PER_GROUP = WIDTH // GROUPS
LANES = 128
WINDOW = 256
PAIRS = NEAREST * LANES

SQUARE = WIDTH * WIDTH
OFF_ATT_IN = 5 * SQUARE
OFF_ATT_OUT = OFF_ATT_IN + WIDTH * GROUPS
OFF_TAIL = OFF_ATT_OUT + GROUPS * GROUPS
NORMS = 2 * WIDTH + 3 + GROUPS
TAIL_POS_OUT = 9
TAIL_GAINS = TAIL_POS_OUT + 3 * WIDTH
TAIL_SHIFTS = TAIL_GAINS + NORMS
TAIL_USED = TAIL_SHIFTS + NORMS
TAIL_PAD = 2048
SLICE = 2048
SLICE_ROWS = SLICE // LANES
LOW_ROWS = SLICE // WIDTH * 2 * GROUPS // LANES
DENSE_FROM = 3
CHUNK = 1024

bn_eps = 1e-05
clip_norm = 0.01
learn_rate = 0.05
beta_one = 0.9
beta_two = 0.999
adam_eps = 1e-08
decay_rate = 0.01
step_count = 10
masked_logit = -1000000000.0

f32 = jnp.float32
bf16 = jnp.bfloat16
MESH = pl.DeviceIdType.MESH


def contract(a, b, left, right):
    return lax.dot_general(a, b, (((left,), (right,)), ((), ())), preferred_element_type=f32)


def nn(a, b):
    return contract(a, b, 1, 0)


def nt(a, b):
    return contract(a, b, 1, 1)


def tn(a, b):
    return contract(a, b, 0, 0)


def split(value, parts):
    pieces = []
    for _ in range(parts):
        piece = value.astype(bf16)
        pieces.append(piece)
        value = value - piece.astype(f32)
    return pieces


def silu_parts(value):
    gate = 0.5 * jnp.tanh(0.5 * value) + 0.5
    return value * gate, gate


def silu_slope(value, gate):
    return gate * (1.0 + value * (1.0 - gate))


def iota(shape, dim):
    return lax.broadcasted_iota(jnp.int32, shape, dim)


def row_to_col(row, count):
    wide = jnp.broadcast_to(row, (count, row.shape[1]))
    same = iota(wide.shape, 0) == iota(wide.shape, 1)
    return jnp.sum(jnp.where(same, wide, 0.0), axis=1, keepdims=True)


def col_to_row(col, offset):
    wide = jnp.broadcast_to(col, (col.shape[0], LANES))
    same = iota(wide.shape, 0) + offset == iota(wide.shape, 1)
    return jnp.sum(jnp.where(same, wide, 0.0), axis=0, keepdims=True)


def row_sum(value):
    return jnp.sum(value, axis=0, keepdims=True)


def lane_fold(value):
    total = value[:, 0:LANES]
    for k in range(1, value.shape[1] // LANES):
        total = total + value[:, k * LANES : (k + 1) * LANES]
    return total


def lane_sum(value):
    return jnp.sum(lane_fold(value), axis=1, keepdims=True)


def tiles(value):
    return jnp.concatenate([value] * NEAREST, axis=1)


def adam(param, moment, second, grad):
    moment_new = beta_one * moment + (1.0 - beta_one) * grad
    second_new = beta_two * second + (1.0 - beta_two) * grad * grad
    moment_hat = moment_new / (1.0 - beta_one**step_count)
    second_hat = second_new / (1.0 - beta_two**step_count)
    param_new = param - learn_rate * (
        moment_hat / (jnp.sqrt(second_hat) + adam_eps) + decay_rate * param
    )
    return param_new, moment_new, second_new


def peer(me, step, count):
    if count & (count - 1) == 0:
        return me ^ (count - step)
    return lax.rem(me + step, count)


def block_kernel(
    n_rows, n_cols,
    feat_h, coords_h, valid_h, nbrs_h, cot_h, weights_h, master_h, first_h, second_h,
    out_h, gfeat_h, gnorm_h, new_master_h, new_first_h, new_second_h, weights_out,
    feat, coords, valid, nbrs, cot, w_first, pos_first, weights, state, news, outs, norm_s, in_sem, out_sem,
    stat_send, stat_buf, stat_ssem, stat_rsem,
    tail1d, mats, onehot, vgat, att, wpre, uact, dyw, rel, pos, act, pmask, allow, dmix,
    ft_s, slope_a, slope_p, a1_s, z_s, h_s, h_ts, q_s, k_s, ba_s, o_s, do_s, dv_s, sk_s, bd_s, dp_s, ds_s, xs, dz_s, dz16,
    mu_s, flat, pair_got, part16, got16, first_f, first_got, wide16, got_wide, low_f, low_got, low_sum, got_low, sums, owned, tail_g, slab_f, shard_w, all_w,
    pair_ssem, pair_rsem, rs_ssem, rs_rsem, wd_ssem, wd_rsem, low_ssem, low_rsem, own_ssem, own_rsem, ag_ssem, ag_rsem, fw_ssem, fw_rsem,
):
    n = n_rows * n_cols
    half = n // 2
    row_id, col_id = lax.axis_index("rows"), lax.axis_index("cols")
    me = row_id * n_cols + col_id
    core = lax.rem(col_id, 2)
    chip = me // 2
    points = feat.shape[0]
    blocks = points // LANES
    starts = [min(max(LANES * b - (WINDOW - LANES) // 2, 0), points - WINDOW) for b in range(blocks)]
    total_len = weights.shape[0]
    shard_len = master_h.shape[0]
    shard_rows = -(-tail_g.shape[0] // LANES)
    per_matrix = SQUARE // SLICE // 2
    dense = DENSE_FROM * per_matrix
    sliced = dense + flat.shape[0]
    slots = got16.shape[0]
    low_kinds = got_low.shape[0]
    sides = own_ssem.shape[1]
    span = own_rsem.shape[0]

    def place(device):
        return (device // n_cols, lax.rem(device, n_cols))

    barrier = pltpu.get_barrier_semaphore()

    def greet(k, carry):
        pl.semaphore_signal(barrier, inc=1, device_id=place(peer(me, k, n)), device_id_type=MESH)
        return carry

    lax.fori_loop(1, n, greet, 0)
    loads = []

    def load(source, target):
        copy = pltpu.make_async_copy(source, target, in_sem.at[len(loads)])
        copy.start()
        loads.append(copy)
        return copy

    stores = []

    def store(source, target):
        copy = pltpu.make_async_copy(source, target, out_sem.at[len(stores)])
        copy.start()
        stores.append(copy)

    early = [
        load(feat_h, feat),
        load(weights_h.at[pl.ds(0, SQUARE)], w_first),
        load(weights_h.at[pl.ds(OFF_TAIL, 1024)], pos_first),
        load(nbrs_h, nbrs),
        load(coords_h, coords),
        load(valid_h, valid),
    ]

    late = [load(weights_h, weights), load(cot_h, cot)]
    for source, target in ((master_h, 0), (first_h, 1), (second_h, 2)):
        late.append(load(source, state[target]))
    owned[...] = jnp.zeros(owned.shape, f32)
    for copy in early:
        copy.wait()

    sent = []

    def all_sum(index, message):
        rows = message.shape[0]
        stat_send[index, 0:rows] = message
        stat_buf[index, me, 0:rows] = message

        def post(k, carry):
            pltpu.make_async_remote_copy(
                src_ref=stat_send.at[index, pl.ds(0, rows)],
                dst_ref=stat_buf.at[index, me, pl.ds(0, rows)],
                send_sem=stat_ssem.at[index],
                recv_sem=stat_rsem.at[index],
                device_id=place(peer(me, k, n)),
                device_id_type=MESH,
            ).start()
            return carry

        lax.fori_loop(1, n, post, 0)
        sent.append((index, rows))

        def collect():
            span = stat_buf.at[index, pl.ds(0, n - 1), pl.ds(0, rows)]
            pltpu.make_async_copy(span, span, stat_rsem.at[index]).wait()
            return jnp.sum(stat_buf[index, :, 0:rows], axis=0)

        return collect

    sibling = (row_id, col_id + 1 - 2 * core)
    def put_matrix(m, grad):
        at = (m - DENSE_FROM) * per_matrix
        flat[at : at + per_matrix] = grad.reshape(per_matrix, 2, SLICE_ROWS, LANES)

    def swap(group, source, target):
        copy = pltpu.make_async_remote_copy(
            src_ref=source.at[:, 1 - core],
            dst_ref=target,
            send_sem=pair_ssem.at[group],
            recv_sem=pair_rsem.at[group],
            device_id=sibling,
            device_id_type=MESH,
        )
        copy.start()
        return copy

    def to_chips(begin, count, send):
        if count == half and begin % half == 0:

            def post(k, carry):
                other = peer(chip, k, half)
                send(begin + other, other)
                return carry

            lax.fori_loop(1, half, post, 0)
        else:

            def post_any(k, carry):
                index = begin + k
                other = lax.rem(index, half)

                @pl.when(other != chip)
                def _():
                    send(index, other)

                return carry

            lax.fori_loop(0, count, post_any, 0)

    def send_dense(copy, begin, count):
        copy.wait()
        own = pl.ds(begin - dense, count)
        part16[own] = (flat[own, core] + pair_got[own]).astype(bf16)

        def send(index, other):
            pltpu.make_async_remote_copy(
                src_ref=part16.at[index - dense],
                dst_ref=got16.at[index // half, chip],
                send_sem=rs_ssem.at[index // half],
                recv_sem=rs_rsem.at[index // half],
                device_id=place(2 * other + core),
                device_id_type=MESH,
            ).start()

        at = begin
        while at < begin + count:
            step = min(half - at % half, begin + count - at)
            to_chips(at, step, send)
            at = at + step

    def send_wide(copy, which):
        copy.wait()
        for k, piece in enumerate(split(first_f[which, :, core] + first_got[which], 2)):
            wide16[which, :, k] = piece

        def send(index, other):
            pltpu.make_async_remote_copy(
                src_ref=wide16.at[which, index],
                dst_ref=got_wide.at[which, chip],
                send_sem=wd_ssem.at[which],
                recv_sem=wd_rsem.at[which],
                device_id=place(2 * other + core),
                device_id_type=MESH,
            ).start()

        to_chips(0, per_matrix, send)

    def send_low(copy):
        copy.wait()
        low_sum[...] = low_f[:, core] + low_got[...]
        for kind in range(low_kinds):

            def send(index, other, kind=kind):
                pltpu.make_async_remote_copy(
                    src_ref=low_sum.at[index - (1 + kind) * per_matrix],
                    dst_ref=got_low.at[kind, chip],
                    send_sem=low_ssem.at[kind],
                    recv_sem=low_rsem.at[kind],
                    device_id=place(2 * other + core),
                    device_id_type=MESH,
                ).start()

            to_chips((1 + kind) * per_matrix, per_matrix, send)

    def drain_stats(index, rows):
        span = stat_buf.at[index, pl.ds(0, n - 1), pl.ds(0, rows)]
        pltpu.make_async_copy(span, span, stat_ssem.at[index]).wait()

    w_in = w_first[...].reshape(WIDTH, WIDTH)
    mats[0] = w_in
    w_in = mats[0]
    pos_in = pos_first[...].reshape(1024 // LANES, LANES)[0:1].astype(f32)
    lane8 = iota((8, 1), 0)

    def pos_in_col(c):
        return jnp.where(lane8 < 3, row_to_col(pos_in[:, 3 * c : 3 * c + 8], 8), 0.0)

    valid_rows = valid[...].reshape(points // LANES, LANES).astype(f32)
    n_valid = jnp.sum(jnp.sum(valid_rows, axis=0, keepdims=True), axis=1, keepdims=True)
    point_mask = (iota((points, 1), 0).astype(f32) < n_valid).astype(f32)
    lane_mask = (iota((1, points), 1).astype(f32) < n_valid).astype(f32)

    a1 = nn(feat[...], w_in)
    a1_s[...] = a1
    masked = point_mask * a1
    sum_a, sqr_a = row_sum(masked), row_sum(masked * a1)

    weight = [[pos_in[:, 3 * c + d : 3 * c + d + 1] for d in range(3)] for c in range(3)]
    pos_one = [jnp.zeros((NEAREST, LANES), f32) for _ in range(3)]
    pos_two = [jnp.zeros((NEAREST, LANES), f32) for _ in range(3)]
    pairs_local = jnp.zeros((NEAREST, LANES), f32)
    for b in range(blocks):
        here = slice(b * LANES, (b + 1) * LANES)
        index = nbrs[:, here]
        tile, at = lax.shift_right_logical(index, 7), index & (LANES - 1)

        def fetch(c, t):
            row = jnp.broadcast_to(coords[c : c + 1, t * LANES : (t + 1) * LANES], index.shape)
            return jnp.take_along_axis(row, at, axis=1, mode="promise_in_bounds")

        r = []
        for c in range(3):
            near = fetch(c, b)
            if b > 0:
                near = jnp.where(tile < b, fetch(c, b - 1), near)
            if b < blocks - 1:
                near = jnp.where(tile > b, fetch(c, b + 1), near)
            r.append(near - coords[c : c + 1, here])
        pm = jnp.where(index.astype(f32) < n_valid, lane_mask[:, here], 0.0)
        pairs_local = pairs_local + pm
        for d in range(3):
            p = weight[0][d] * r[0] + weight[1][d] * r[1] + weight[2][d] * r[2]
            pos_one[d] = pos_one[d] + pm * p
            pos_two[d] = pos_two[d] + pm * p * p

    def total(value):
        return jnp.sum(row_sum(value), axis=1, keepdims=True)

    lane = iota((1, LANES), 1)
    last = jnp.where(lane == 16, n_valid, 0.0) + jnp.where(lane == 17, total(pairs_local), 0.0)
    for d in range(3):
        last = last + jnp.where(lane == d, total(pos_one[d]), 0.0)
        last = last + jnp.where(lane == 8 + d, total(pos_two[d]), 0.0)

    def fold(row):
        return jnp.concatenate([row[:, 0:LANES], row[:, LANES:WIDTH]], axis=0)

    def unfold(rows):
        return jnp.concatenate([rows[0:1], rows[1:2]], axis=1)

    pl.semaphore_wait(barrier, n - 1)
    collect_first = all_sum(0, jnp.concatenate([fold(sum_a), fold(sqr_a), last], axis=0))
    window_row = iota((WINDOW, LANES), 0)
    for b in range(blocks):
        for j in range(NEAREST):
            index = nbrs[j : j + 1, b * LANES : (b + 1) * LANES] - starts[b]
            onehot[b, :, j * LANES : (j + 1) * LANES] = jnp.where(
                window_row == index, 1.0, 0.0
            ).astype(bf16)

    coords8 = jnp.concatenate([coords[...], jnp.zeros((5, points), f32)], axis=0)
    table = jnp.concatenate(
        split(coords8, 3) + [jnp.broadcast_to(lane_mask, (8, points)).astype(bf16)], axis=0
    )
    slot0 = (iota((1, PAIRS), 1) < LANES).astype(f32)
    pos_in_cols = [pos_in_col(c) for c in range(3)]
    for b in range(blocks):
        here = slice(b * LANES, (b + 1) * LANES)
        fetched = nn(table[:, starts[b] : starts[b] + WINDOW], onehot[b])
        place_n = fetched[0:8] + fetched[8:16] + fetched[16:24]
        mask_n = fetched[24:32]
        r = place_n - tiles(coords8[:, here])
        pm = mask_n * tiles(lane_mask[:, here])
        p = pos_in_cols[0] * r[0:1] + pos_in_cols[1] * r[1:2] + pos_in_cols[2] * r[2:3]
        rel[b] = r
        pos[b] = p
        pmask[b] = pm
        allow[b] = jnp.maximum(mask_n, slot0)

    for copy in late:
        copy.wait()
    for m in range(1, 5):
        mats[m] = weights[pl.ds(m * SQUARE, SQUARE)].reshape(WIDTH, WIDTH)
    w_q, w_k, w_v, w_o = (mats[m] for m in range(1, 5))
    att_in = weights[pl.ds(OFF_ATT_IN, WIDTH * GROUPS)].reshape(WIDTH * GROUPS // LANES, LANES)
    att_in_f = att_in.astype(f32).reshape(WIDTH, GROUPS)
    att_in_t = att_in_f.T.astype(bf16)
    att_out_f = (
        weights[pl.ds(OFF_ATT_OUT, GROUPS * GROUPS)]
        .reshape(GROUPS * GROUPS // LANES, LANES)
        .astype(f32)
        .reshape(GROUPS, GROUPS)
    )
    att_out = att_out_f.astype(bf16)
    att_out_t = att_out_f.T.astype(bf16)
    tail1d[pl.ds(0, 1024)] = weights[pl.ds(OFF_TAIL, 1024)]
    rest = total_len - OFF_TAIL - 1024
    tail1d[pl.ds(1024, rest)] = weights[pl.ds(OFF_TAIL + 1024, rest)]
    tail = tail1d[pl.ds(0, TAIL_PAD)].reshape(TAIL_PAD // LANES, LANES).astype(f32)
    tail = jnp.concatenate([tail[k : k + 1] for k in range(TAIL_PAD // LANES)], axis=1)
    pos_rows = [tail[:, TAIL_POS_OUT + WIDTH * d : TAIL_POS_OUT + WIDTH * (d + 1)] for d in range(3)]
    def norm_pieces(start):
        ends = [0, WIDTH, WIDTH + 3, WIDTH + 3 + GROUPS, NORMS]
        return [tail[:, start + ends[k] : start + ends[k + 1]] for k in range(4)]

    gain_a, gain_p, gain_w, gain_o = norm_pieces(TAIL_GAINS)
    shift_a, shift_p, shift_w, shift_o = norm_pieces(TAIL_SHIFTS)

    def pad_col(row):
        wide = jnp.concatenate([row, jnp.zeros((1, 5), f32)], axis=1)
        return row_to_col(wide, 8)

    gain_p, shift_p = pad_col(gain_p), pad_col(shift_p)
    gain_w, shift_w = row_to_col(gain_w, GROUPS), row_to_col(shift_w, GROUPS)

    new_at = iota((WIDTH, WIDTH), 0)
    reorder = jnp.where(
        iota((WIDTH, WIDTH), 1) == new_at % GROUPS * PER_GROUP + new_at // GROUPS, 1.0, 0.0
    ).astype(bf16)
    w_o_new = nn(reorder, w_o)
    mats[4] = w_o_new.astype(bf16)
    mats[5] = w_o_new.T.astype(bf16)
    mats[6] = w_q.astype(f32).T.astype(bf16)
    mats[7] = w_k.astype(f32).T.astype(bf16)
    mats[8] = nt(reorder, w_v).astype(bf16)
    pos_mat = jnp.concatenate(pos_rows + [jnp.zeros((13, WIDTH), f32)], axis=0).astype(bf16)
    pos_cols = nt(reorder, pos_mat)
    pos_cols = [pos_cols[:, d : d + 1] for d in range(3)]
    feat_f = feat[...].astype(f32)
    ft_s[...] = feat_f.T.astype(bf16)
    sum_f = row_sum(point_mask * feat_f)
    stats = collect_first()

    def pick(row, at):
        return jnp.sum(jnp.where(lane == at, row, 0.0), axis=1, keepdims=True)

    point_count, pair_count = pick(stats[4:5], 16), pick(stats[4:5], 17)
    inv_points, inv_pairs = 1.0 / point_count, 1.0 / pair_count

    def moments(total, square, inv):
        mean = total * inv
        return mean, lax.rsqrt(square * inv - mean * mean + bn_eps)

    mean_a, rs_a = moments(unfold(stats[0:2]), unfold(stats[2:4]), inv_points)
    mean_p, rs_p = moments(
        row_to_col(stats[4:5, 0:8], 8), row_to_col(stats[4:5, 8:16], 8), inv_pairs
    )

    h = silu_parts((a1_s[...] - mean_a) * rs_a * gain_a + shift_a)[0]
    h_s[...] = h.astype(bf16)
    h_t = h.T.astype(bf16)
    q_t = nn(mats[6], h_t).astype(bf16)
    k_t = nn(mats[7], h_t).astype(bf16)
    q_s[...] = q_t
    k_s[...] = k_t
    h_ts[...] = h_t
    q_att = nn(att_in_t, q_t)
    k_att = jnp.concatenate(split(nn(att_in_t, k_t), 3), axis=0)
    pos_att = nt(att_in_t, pos_mat)
    pos_att_cols = [pos_att[:, d : d + 1] for d in range(3)]
    back_att = jnp.concatenate([nn(att_in_t, mats[6]), nn(att_in_t, mats[7])], axis=0)
    back_split = split(back_att, 2)
    ba_s[...] = jnp.concatenate([back_split[0], back_split[0], back_split[1]], axis=0)

    sum_w = jnp.zeros((GROUPS, LANES), f32)
    sqr_w = jnp.zeros((GROUPS, LANES), f32)
    for b in range(blocks):
        here = slice(b * LANES, (b + 1) * LANES)
        active = silu_parts((pos[b] - mean_p) * rs_p * gain_p + shift_p)[0]
        act[b] = active
        fetched = nn(k_att[:, starts[b] : starts[b] + WINDOW], onehot[b])
        w = tiles(q_att[:, here]) - (
            fetched[0:GROUPS] + fetched[GROUPS : 2 * GROUPS] + fetched[2 * GROUPS : 3 * GROUPS]
        )
        for d in range(3):
            w = w + pos_att_cols[d] * active[d : d + 1]
        wpre[b] = w
        mw = w * pmask[b, 0:1]
        sum_w = sum_w + lane_fold(mw)
        sqr_w = sqr_w + lane_fold(mw * w)

    def pair_row(one, two):
        one = jnp.sum(one, axis=1, keepdims=True)
        two = jnp.sum(two, axis=1, keepdims=True)
        return col_to_row(one, 0) + col_to_row(two, GROUPS)

    collect_w = all_sum(1, jnp.concatenate([pair_row(sum_w, sqr_w), fold(sum_f)], axis=0))
    v_t = nn(mats[8], h_ts[...]).astype(bf16)
    for b in range(blocks):
        vgat[b] = nn(v_t[:, starts[b] : starts[b] + WINDOW], onehot[b])
    stats = collect_w()
    mean_f = stats[1:3] * inv_points
    mean_w, rs_w = moments(
        row_to_col(stats[0:1, 0:GROUPS], GROUPS),
        row_to_col(stats[0:1, GROUPS : 2 * GROUPS], GROUPS),
        inv_pairs,
    )

    def each_channel(value):
        return jnp.concatenate([value] * PER_GROUP, axis=0)

    def over_channels(value):
        return functools.reduce(
            jnp.add, [value[c * GROUPS : (c + 1) * GROUPS] for c in range(PER_GROUP)]
        )

    def cols(j):
        return slice(j * LANES, (j + 1) * LANES)

    for b in range(blocks):
        here = slice(b * LANES, (b + 1) * LANES)
        u = silu_parts((wpre[b] - mean_w) * rs_w * gain_w + shift_w)[0].astype(bf16)
        uact[b] = u
        logit = jnp.where(allow[b, 0:1] > 0.5, nn(att_out_t, u), masked_logit)
        top = logit[:, cols(0)]
        for j in range(1, NEAREST):
            top = jnp.maximum(top, logit[:, cols(j)])
        weight = jnp.exp(logit - tiles(top))
        share = 1.0 / functools.reduce(jnp.add, [weight[:, cols(j)] for j in range(NEAREST)])
        att[b] = weight * tiles(share)
        mixed = jnp.zeros((WIDTH, LANES), f32)
        enc = [jnp.zeros((GROUPS, LANES), f32) for _ in range(3)]
        for j in range(NEAREST):
            a = att[b, :, cols(j)]
            mixed = mixed + each_channel(a) * vgat[b, :, cols(j)]
            for d in range(3):
                enc[d] = enc[d] + a * act[b, d : d + 1, cols(j)]
        bd_s[:, here] = jnp.concatenate(enc, axis=0)
        for d in range(3):
            mixed = mixed + pos_cols[d] * each_channel(enc[d])
        o_s[here, :] = mixed.T.astype(bf16)

    z = nn(o_s[...], mats[4])
    z_s[...] = z
    masked = point_mask * z
    collect_o = all_sum(2, jnp.concatenate([fold(row_sum(masked)), fold(row_sum(masked * z))], axis=0))
    for k in range(2):
        mu_s[k * LANES : (k + 1) * LANES] = jnp.broadcast_to(
            row_to_col(mean_f[k : k + 1], LANES), (LANES, LANES)
        )

    def put_first(which, value):
        first_f[which] = value.reshape(per_matrix, 2, SLICE_ROWS, LANES)
        return swap(which, first_f.at[which], first_got.at[which])

    def from_feat(value):
        return nn(
            jnp.concatenate([ft_s[...]] * 2, axis=1), jnp.concatenate(split(value, 2), axis=0)
        )

    ahat = (a1_s[...] - mean_a) * rs_a
    a1_s[...] = ahat
    ahat_pair = put_first(0, from_feat(point_mask * ahat))
    for b in range(blocks):
        what = (wpre[b] - mean_w) * rs_w
        wpre[b] = what
        y = what * gain_w + shift_w
        dyw[b] = silu_slope(y, silu_parts(y)[1])
    send_wide(ahat_pair, 0)
    stats = collect_o()
    mean_o, rs_o = moments(unfold(stats[0:2]), unfold(stats[2:4]), inv_points)

    zhat = (z_s[...] - mean_o) * rs_o
    z_s[...] = zhat
    y = feat[...].astype(f32) + zhat * gain_o + shift_o
    value, gate = silu_parts(y)
    outs[0] = (point_mask * value).astype(bf16)
    store(outs.at[0], out_h)
    dy = point_mask * cot[...].astype(f32) * silu_slope(y, gate)
    dz_s[...] = dy
    shift_grad_o, gain_grad_o = row_sum(dy), row_sum(dy * zhat)
    collect_o = all_sum(3, jnp.concatenate([fold(shift_grad_o), fold(gain_grad_o)], axis=0))
    for b in range(blocks):
        phat = (pos[b] - mean_p) * rs_p
        pos[b] = phat
        y = phat * gain_p + shift_p
        slope_p[b] = silu_slope(y, silu_parts(y)[1])
    y = a1_s[...] * gain_a + shift_a
    slope_a[...] = silu_slope(y, silu_parts(y)[1])
    pos_row = jnp.zeros((1, LANES), f32)
    for c in range(3):
        with_hat, alone = jnp.zeros((8, 1), f32), jnp.zeros((8, 1), f32)
        for b in range(blocks):
            masked = pmask[b] * rel[b, c : c + 1]
            with_hat = with_hat + lane_sum(masked * pos[b])
            alone = alone + lane_sum(masked)
        pos_row = pos_row + col_to_row(with_hat, 64 + 8 * c) + col_to_row(alone, 88 + 8 * c)
    stats = collect_o()
    one, two = unfold(stats[0:2]) * inv_points, unfold(stats[2:4]) * inv_points
    dz = (gain_o * rs_o * (dz_s[...] - point_mask * (one + z_s[...] * two))).astype(bf16)
    dz16[...] = dz
    do_s[...] = nn(dz, mats[5]).T

    sum_w = jnp.zeros((GROUPS, LANES), f32)
    sqr_w = jnp.zeros((GROUPS, LANES), f32)
    for b in range(blocks):
        here = slice(b * LANES, (b + 1) * LANES)
        do = do_s[:, here]
        do_pos = [over_channels(do * pos_cols[d]) for d in range(3)]
        dp_s[:, here] = jnp.concatenate(do_pos, axis=0)
        da = []
        for j in range(NEAREST):
            grad = over_channels(do * vgat[b, :, cols(j)])
            for d in range(3):
                grad = grad + do_pos[d] * act[b, d : d + 1, cols(j)]
            da.append(grad)
        mean_da = functools.reduce(jnp.add, [da[j] * att[b, :, cols(j)] for j in range(NEAREST)])
        ds = jnp.concatenate(
            [att[b, :, cols(j)] * (da[j] - mean_da) for j in range(NEAREST)], axis=1
        ).astype(bf16)
        ds_s[b] = ds
        dy = nn(att_out, ds) * dyw[b]
        dyw[b] = dy
        sum_w = sum_w + lane_fold(dy)
        sqr_w = sqr_w + lane_fold(dy * wpre[b])

    back_w = pair_row(sum_w, sqr_w)
    collect_w = all_sum(4, back_w + pos_row)
    put_matrix(4, tn(nn(o_s[...], reorder).astype(bf16), dz16[...]))
    dv_s[...] = jnp.zeros(dv_s.shape, f32)
    for b in range(blocks):
        here = slice(b * LANES, (b + 1) * LANES)
        do = do_s[:, here]
        for j in range(NEAREST):
            xs[:, cols(j)] = (each_channel(att[b, :, cols(j)]) * do).astype(bf16)
        dv_s[pl.ds(starts[b], WINDOW)] += nt(onehot[b], xs[...])
    dv = nn(dv_s[...].astype(bf16), reorder).astype(bf16)
    put_matrix(3, tn(h_s[...], dv))
    square_flat = pl.ds(0, 2 * per_matrix)
    late_pair = swap(2, flat.at[square_flat], pair_got.at[square_flat])
    dv_s[...] = nt(dv, w_v)
    add_groups = jnp.where(
        iota((8, 3 * GROUPS), 1) // GROUPS == iota((8, 3 * GROUPS), 0), 1.0, 0.0
    ).astype(bf16)
    d_att_out = jnp.zeros((GROUPS, GROUPS), f32)
    for b in range(blocks):
        here = slice(b * LANES, (b + 1) * LANES)
        d_att_out = d_att_out + nt(uact[b], ds_s[b])
        mix = [
            (tiles(dp_s[d * GROUPS : (d + 1) * GROUPS, here]) * att[b]).astype(bf16) for d in range(3)
        ]
        dmix[b] = nn(add_groups, jnp.concatenate(mix, axis=0))
    send_dense(late_pair, dense, 2 * per_matrix)
    stats = collect_w()
    one = row_to_col(stats[:, 0:GROUPS], GROUPS) * inv_pairs
    two = row_to_col(stats[:, GROUPS : 2 * GROUPS], GROUPS) * inv_pairs
    pos_hat = [row_to_col(stats[:, 64 + 8 * c : 72 + 8 * c], 8) for c in range(3)]
    pos_alone = [row_to_col(stats[:, 88 + 8 * c : 96 + 8 * c], 8) for c in range(3)]

    sk_s[...] = jnp.zeros(sk_s.shape, f32)
    pos_att_rows = split(pos_att[:, 0:8].T, 3)
    pos_att_rows = jnp.concatenate(pos_att_rows, axis=0)
    dw_sums = []
    along = [jnp.zeros((8, 1), f32) for _ in range(3)]
    sum_p = jnp.zeros((8, 1), f32)
    sqr_p = jnp.zeros((8, 1), f32)
    for b in range(blocks):
        dw = (gain_w * rs_w * (dyw[b] - pmask[b, 0:1] * (one + wpre[b] * two))).astype(bf16)
        sk_s[pl.ds(starts[b], WINDOW)] += nt(onehot[b], dw)
        dw_sums.append(lane_slots(dw.astype(f32)))
        ds_s[b] = dw
        back = nn(pos_att_rows, dw)
        d_act = dmix[b] + back[0:8] + back[8:16] + back[16:24]
        dy = d_act * slope_p[b]
        sum_p = sum_p + lane_sum(dy)
        sqr_p = sqr_p + lane_sum(dy * pos[b])
        for c in range(3):
            along[c] = along[c] + lane_sum(dy * rel[b, c : c + 1])
    dq_att = jnp.concatenate(dw_sums, axis=1)
    both_att = jnp.concatenate([dq_att.T, -sk_s[...]], axis=1)
    both_split = split(both_att, 2)
    dh = nn(jnp.concatenate(both_split + both_split[0:1], axis=1), ba_s[...]) + dv_s[...]
    dy = dh * slope_a[...]
    z_s[...] = dy
    shift_grad_a = row_sum(dy)
    away = jnp.concatenate(
        [mu_s[...] * shift_grad_a[:, k * LANES : (k + 1) * LANES] for k in range(2)], axis=1
    )
    first_pair = put_first(1, from_feat(dy) - away)
    low = nn(
        jnp.concatenate([h_ts[...]] * 2, axis=1), jnp.concatenate(both_split, axis=0)
    )
    low_f[...] = low.reshape(per_matrix, 2, LOW_ROWS, LANES)
    low_pair = swap(3, low_f, low_got)
    gain_grad_a = row_sum(z_s[...] * a1_s[...])
    last = col_to_row(sum_p, 0) + col_to_row(sqr_p, 8)
    for c in range(3):
        last = last + col_to_row(along[c], 16 + 8 * c)
    collect_a = all_sum(
        5, jnp.concatenate([fold(shift_grad_a), fold(gain_grad_a), last], axis=0)
    )
    send_wide(first_pair, 1)
    send_low(low_pair)

    d_pos_att = sum(
        nt(jnp.concatenate(split(act[b], 3), axis=0), ds_s[b]) for b in range(blocks)
    )
    d_pos_att = d_pos_att[0:8] + d_pos_att[8:16] + d_pos_att[16:24]
    d_pos_split = split(d_pos_att, 3)
    d_att_in = sum(
        nn(q_s[...], piece[:, 0:GROUPS]) + nn(k_s[...], piece[:, GROUPS : 2 * GROUPS])
        for piece in both_split
    )
    d_att_in = d_att_in + sum(tn(pos_mat[0:8], piece) for piece in d_pos_split)
    d_pos_out = sum(nn(piece, att_in_t) for piece in d_pos_split)
    do_split = split(do_s[...], 2)
    bd_split = split(bd_s[...], 2)
    cross = nt(bd_split[0], do_split[0]) + nt(bd_split[0], do_split[1]) + nt(bd_split[1], do_split[0])
    own_group = iota((GROUPS, WIDTH), 1) % GROUPS == iota((GROUPS, WIDTH), 0)
    cross = [
        row_sum(jnp.where(own_group, cross[d * GROUPS : (d + 1) * GROUPS], 0.0)) for d in range(3)
    ]
    cross = jnp.concatenate(cross + [jnp.zeros((5, WIDTH), f32)], axis=0)
    d_pos_out = d_pos_out + sum(nn(piece, reorder) for piece in split(cross, 3))
    d_pos_rows = [d_pos_out[d : d + 1] for d in range(3)]
    pieces = [jnp.zeros((1, TAIL_POS_OUT), f32)] + d_pos_rows
    pieces = pieces + [
        gain_grad_a, col_to_row(sqr_p, 0)[:, 0:3], back_w[:, GROUPS : 2 * GROUPS], gain_grad_o,
        shift_grad_a, col_to_row(sum_p, 0)[:, 0:3], back_w[:, 0:GROUPS], shift_grad_o,
        jnp.zeros((1, TAIL_PAD - TAIL_USED), f32),
    ]
    small = 5 * per_matrix
    used_rows = OFF_TAIL // LANES + TAIL_PAD // LANES - 5 * SQUARE // LANES
    spare_rows = (sliced - small) * 2 * SLICE_ROWS - used_rows
    pieces_rows = [
        d_att_in.reshape(WIDTH * GROUPS // LANES, LANES),
        d_att_out.reshape(GROUPS * GROUPS // LANES, LANES),
        jnp.concatenate(pieces, axis=1).reshape(TAIL_PAD // LANES, LANES),
        jnp.zeros((spare_rows, LANES), f32),
    ]
    flat[small - dense : sliced - dense] = jnp.concatenate(pieces_rows, axis=0).reshape(
        sliced - small, 2, SLICE_ROWS, LANES
    )
    small_flat = pl.ds(small - dense, sliced - small)
    small_pair = swap(4, flat.at[small_flat], pair_got.at[small_flat])
    send_dense(small_pair, small, sliced - small)

    stats = collect_a()
    one, two = unfold(stats[0:2]) * inv_points, unfold(stats[2:4]) * inv_points
    scale_tile = jnp.concatenate([fold(gain_a * rs_a)] * (SLICE_ROWS // 2), axis=0)
    two_tile = jnp.concatenate([fold(two)] * (SLICE_ROWS // 2), axis=0)
    da1 = (gain_a * rs_a * (z_s[...] - point_mask * (one + a1_s[...] * two))).astype(bf16)
    outs[1] = (dz_s[...] + nt(da1, w_in)).astype(bf16)
    store(outs.at[1], gfeat_h)
    one = row_to_col(stats[4:5, 0:8], 8) * inv_pairs
    two = row_to_col(stats[4:5, 8:16], 8) * inv_pairs
    pos_in_row = jnp.zeros((1, LANES), f32)
    for c in range(3):
        moved = row_to_col(stats[4:5, 16 + 8 * c : 24 + 8 * c], 8)
        moved = gain_p * rs_p * (moved - one * pos_alone[c] - two * pos_hat[c])
        pos_in_row = pos_in_row + col_to_row(moved, 3 * c)

    def slice_of(slot):
        return 2 * (slot * half + chip) + core

    def when_in(slot, low, high, act_on):
        if (slot + 1) * n <= low or slot * n >= high:
            return
        if slot * n >= low and (slot + 1) * n <= high:
            act_on()
        else:
            number = slice_of(slot)
            pl.when((number >= low) & (number < high))(act_on)

    def others_sum(total, part):
        def add(k, total):
            return total + part(peer(chip, k, half))

        return lax.fori_loop(1, half, add, total, unroll=half <= 16)

    def take_wide(which):
        got = got_wide.at[which, pl.ds(0, half - 1)]
        pltpu.make_async_copy(got, got, wd_rsem.at[which]).wait()
        index = lax.rem(chip, per_matrix)

        def part(other):
            return got_wide[which, other, 0].astype(f32) + got_wide[which, other, 1].astype(f32)

        return others_sum(first_f[which, index, core] + first_got[which, index], part)

    def take_low(kind):
        got = got_low.at[kind, pl.ds(0, half - 1)]
        pltpu.make_async_copy(got, got, low_rsem.at[kind]).wait()
        index = lax.rem(chip, per_matrix)
        return others_sum(low_sum[index], lambda other: got_low[kind, other])

    def low_product(factor, which):
        factor = factor.reshape(SLICE // WIDTH, 2 * GROUPS)[:, which * GROUPS : (which + 1) * GROUPS]
        return sum(nn(piece, att_in_t) for piece in split(factor, 2)).reshape(SLICE_ROWS, LANES)

    squares = jnp.zeros((1, 1), f32)
    matrix = SQUARE // SLICE
    for slot in range(slots):
        sums[slot] = jnp.zeros((SLICE_ROWS, LANES), f32)

    for slot in list(range(DENSE_FROM, slots)) + list(range(min(DENSE_FROM, slots))):
        index = slot * half + chip

        def take_dense(slot=slot, index=index):
            got = got16.at[slot, pl.ds(0, half - 1)]
            pltpu.make_async_copy(got, got, rs_rsem.at[slot]).wait()
            total = flat[index - dense, core] + pair_got[index - dense]
            sums[slot] = others_sum(total, lambda other: got16[slot, other].astype(f32))

        def add_pos_in(slot=slot):
            at_row = iota((SLICE_ROWS, LANES), 0) == OFF_TAIL % SLICE // LANES
            sums[slot] += jnp.where(at_row, pos_in_row, 0.0)

        def first(slot=slot):
            sums[slot] = scale_tile * (take_wide(1) - two_tile * take_wide(0))

        when_in(slot, DENSE_FROM * matrix, 2 * sliced, take_dense)
        when_in(slot, OFF_TAIL // SLICE, OFF_TAIL // SLICE + 1, add_pos_in)
        when_in(slot, 0, matrix, first)
    for kind in range(low_kinds):
        kinds = range(2) if low_kinds == 1 else (kind,)

        def fill(kind=kind, kinds=kinds):
            factor = take_low(kind)
            for which in kinds:
                for slot in range(slots):

                    def product(slot=slot, which=which):
                        sums[slot] = low_product(factor, which)

                    when_in(slot, (1 + which) * matrix, (2 + which) * matrix, product)

        if low_kinds == 1:
            fill()
        else:
            when_in(0, (1 + kind) * matrix, (2 + kind) * matrix, fill)
    for slot in range(slots):
        squares = squares + lane_sum(row_sum(sums[slot] * sums[slot]))

    collect_norm = all_sum(6, jnp.where(lane == 0, squares, 0.0))

    def each_owner(slot, act_on):
        number = slice_of(slot)
        low = number * SLICE // shard_len
        high = jnp.minimum((number * SLICE + SLICE - 1) // shard_len, n - 1)
        for side in range(sides):
            owner = low + side

            @pl.when((number * SLICE < total_len) & (owner <= high))
            def _(owner=owner, side=side):
                act_on(owner, number - owner * shard_len // SLICE, side)

    def owned_rows(k):
        return owned.at[pl.ds(pl.multiple_of(k * SLICE_ROWS, SLICE_ROWS), SLICE_ROWS)]

    def own_copy(slot, owner, k, side):
        return pltpu.make_async_remote_copy(
            src_ref=sums.at[slot],
            dst_ref=owned_rows(k),
            send_sem=own_ssem.at[slot, side],
            recv_sem=own_rsem.at[k],
            device_id=place(owner),
            device_id_type=MESH,
        )

    for slot in range(slots):

        def hand_over(owner, k, side, slot=slot):
            @pl.when(owner != me)
            def _():
                own_copy(slot, owner, k, side).start()

            @pl.when(owner == me)
            def _():
                owned_rows(k)[...] = sums[slot]

        each_owner(slot, hand_over)

    begin = me * shard_len
    first_slice = begin // SLICE
    last_slice = (begin + shard_len - 1) // SLICE
    for k in range(span):
        number = first_slice + k

        @pl.when((number <= last_slice) & (lax.rem(number, n) != me))
        def _(k=k):
            rows = owned.at[pl.ds(k * SLICE_ROWS, SLICE_ROWS)]
            pltpu.make_async_copy(rows, rows, own_rsem.at[k]).wait()

    offset = begin - first_slice * SLICE
    skip = lax.rem(offset, LANES)
    lanes_all = iota((shard_rows, LANES), 1)
    rows = owned[pl.ds(offset // LANES, shard_rows), :]
    turned = pltpu.roll(rows, lax.rem(LANES - skip, LANES), 1)
    below = pltpu.roll(turned, shard_rows - 1, 0)
    grad = jnp.where(lanes_all < LANES - skip, turned, below)
    inside = iota(grad.shape, 0) * LANES + lanes_all < shard_len
    grad = jnp.where(inside, grad, 0.0)

    stats = collect_norm()
    norm = jnp.sqrt(pick(stats, 0))
    norm_s[...] = jnp.broadcast_to(norm, norm_s.shape)
    grad = grad * jnp.minimum(1.0, clip_norm / norm)

    main = shard_len // 1024 * 1024
    spare = shard_len - main
    tail_g[...] = grad.reshape(shard_rows * LANES)
    for start, size in ((0, main), (main, spare)):
        if size == 0:
            continue
        at = pl.ds(start, size)
        p_new, m_new, s_new = adam(state[0][at], state[1][at], state[2][at], tail_g[at])
        news[0][at] = p_new
        news[1][at] = m_new
        news[2][at] = s_new
        tail_g[at] = p_new
    moved = jnp.where(inside, tail_g[...].reshape(shard_rows, LANES), 0.0)
    turned = pltpu.roll(moved, skip, 1)
    above = pltpu.roll(turned, 1, 0)
    slab_f[...] = jnp.zeros(slab_f.shape, f32)
    slab_f[pl.ds(lax.rem(begin, CHUNK) // LANES, shard_rows), :] = jnp.where(
        lanes_all < skip, above, turned
    )
    shard_w[...] = slab_f[...].astype(bf16)
    all_w[core, chip] = slab_f[...].astype(bf16)

    in_row = n_cols // 2
    row_chip = col_id // 2

    def send_slab(source, slab, row, chip_in_row):
        pltpu.make_async_remote_copy(
            src_ref=source,
            dst_ref=all_w.at[core, slab],
            send_sem=ag_ssem,
            recv_sem=ag_rsem.at[slab],
            device_id=(row, 2 * chip_in_row + core),
            device_id_type=MESH,
        ).start()

    def forward(other):
        pltpu.make_async_remote_copy(
            src_ref=all_w.at[core, other],
            dst_ref=all_w.at[core, other],
            send_sem=fw_ssem,
            recv_sem=fw_rsem,
            device_id=sibling,
            device_id_type=MESH,
        ).start()

    def arrived(other):
        pltpu.make_async_copy(shard_w, shard_w, ag_rsem.at[other]).wait()

    def send_along(k, carry):
        send_slab(shard_w, chip, peer(row_id, k, n_rows), row_chip)
        return carry

    def send_within(k, carry):
        send_slab(shard_w, chip, row_id, peer(row_chip, k, in_row))
        return carry

    lax.fori_loop(1, n_rows, send_along, 0)
    lax.fori_loop(1, in_row, send_within, 0)
    forward(chip)
    store(norm_s, gnorm_h)
    for source, target in ((0, new_master_h), (1, new_first_h), (2, new_second_h)):
        store(news[source], target)

    def spread_row(k, carry):
        other = peer(row_id, n_rows - k, n_rows) * in_row + row_chip
        arrived(other)

        def send_on(i, carry):
            send_slab(all_w.at[core, other], other, row_id, peer(row_chip, i, in_row))
            return carry

        lax.fori_loop(1, in_row, send_on, 0)
        forward(other)
        return carry

    lax.fori_loop(1, n_rows, spread_row, 0)

    def pass_on(k, carry):
        step = k // (in_row - 1)
        row = jnp.where(step == 0, row_id, peer(row_id, n_rows - step, n_rows))
        other = row * in_row + peer(row_chip, in_row - 1 - lax.rem(k, in_row - 1), in_row)
        arrived(other)
        forward(other)
        return carry

    lax.fori_loop(0, n_rows * (in_row - 1), pass_on, 0)
    pltpu.make_async_copy(all_w.at[core], all_w.at[core], fw_rsem).wait()
    rows = CHUNK // LANES

    def chunk(c):
        value = None
        last_owner = min((c * CHUNK + CHUNK - 1) // shard_len, n - 1)
        for owner in range(c * CHUNK // shard_len, last_owner + 1):
            k = c - owner * shard_len // CHUNK
            part = all_w[owner % 2, owner // 2, rows * k : rows * (k + 1)].astype(f32)
            value = part if value is None else value + part
        return value

    whole = total_len // (2 * CHUNK)
    for c in range(whole):
        both = jnp.concatenate([chunk(2 * c), chunk(2 * c + 1)], axis=0)
        weights_out[pl.ds(2 * CHUNK * c, 2 * CHUNK)] = both.astype(bf16).reshape(2 * CHUNK)
    left = total_len - whole * 2 * CHUNK
    if left:
        parts = [chunk(2 * whole)]
        parts.append(chunk(2 * whole + 1) if left > CHUNK else jnp.zeros((rows, LANES), f32))
        both = jnp.concatenate(parts, axis=0).astype(bf16).reshape(2 * CHUNK)
        weights_out[pl.ds(2 * CHUNK * whole, left)] = both[0:left]

    for index, rows in sent:
        drain_stats(index, rows)
    for copy in stores:
        copy.wait()
    pltpu.make_async_copy(all_w.at[core], all_w.at[core], fw_ssem).wait()
    rest = all_w.at[core, pl.ds(0, half - 1)]
    pltpu.make_async_copy(rest, rest, ag_ssem).wait()
    def drain(count, ref, sem):
        def wait_one(k, carry):
            pltpu.make_async_copy(ref, ref, sem).wait()
            return carry

        lax.fori_loop(0, count, wait_one, 0)

    def others(low, high):
        inside = (chip >= low) & (chip < high)
        return high - low - inside.astype(jnp.int32)

    for which in range(2):
        drain(others(0, per_matrix), wide16.at[0, 0], wd_ssem.at[which])
    for kind in range(low_kinds):
        low_at = (1 + kind) * per_matrix % half
        drain(others(low_at, low_at + per_matrix), low_sum.at[0], low_ssem.at[kind])
    for slot in range(slots):
        low_at = max(dense - slot * half, 0)
        high_at = min(sliced - slot * half, half)
        if high_at > low_at:
            drain(others(low_at, high_at), part16.at[0], rs_ssem.at[slot])

        def own_drain(owner, k, side, slot=slot):
            @pl.when(owner != me)
            def _():
                own_copy(slot, owner, k, side).wait_send()

        each_owner(slot, own_drain)


def finish_kernel(
    out_t, gfeat_t, gnorm_t, master_t, first_t, second_t, weights_t,
    out_h, gfeat_h, gnorm, master_h, first_h, second_h, weights_h,
    norm_s, sem,
):
    copies = [
        pltpu.make_async_copy(source, target, sem.at[k])
        for k, (source, target) in enumerate(
            (
                (weights_t, weights_h),
                (out_t, out_h),
                (gfeat_t, gfeat_h),
                (master_t, master_h),
                (first_t, first_h),
                (second_t, second_h),
                (gnorm_t, norm_s),
            )
        )
    ]
    for copy in copies:
        copy.start()
    copies[-1].wait()
    gnorm[...] = norm_s[0:1, 0:1]
    for copy in copies[:-1]:
        copy.wait()


def lane_slots(value):
    return functools.reduce(
        jnp.add, [value[:, j * LANES : (j + 1) * LANES] for j in range(NEAREST)]
    )


def shards(
    n_rows, n_cols,
    features, coords, valid_mask, neighbors, cotangent, weights, master, first_moment, second_moment,
):
    n = n_rows * n_cols
    half = n // 2
    points = features.shape[0]
    blocks = points // LANES
    shard_len = master.shape[0]
    total_len = weights.shape[0]

    def up(value, unit):
        return -(-value // unit) * unit

    shard_rows = up(-(-shard_len // LANES) + 1, 8)
    slab_rows = up(shard_rows + CHUNK // LANES, 16)
    sliced = up(-(-total_len // SLICE), 2) // 2
    slots = -(-sliced // half)
    per_matrix = SQUARE // SLICE // 2
    dense_pairs = sliced - DENSE_FROM * per_matrix
    low_kinds = 1 if per_matrix % half == 0 else 2
    sides = (SLICE + shard_len - 2) // shard_len + 1
    span = (SLICE + shard_len - 2) // SLICE + 1
    hbm = pl.BlockSpec(memory_space=pltpu.HBM)
    vmem = pl.BlockSpec(memory_space=pltpu.VMEM)
    dma = pltpu.SemaphoreType.DMA
    shape = jax.ShapeDtypeStruct

    def pairs(rows, dtype=f32):
        return pltpu.VMEM((blocks, rows, PAIRS), dtype)

    def shard():
        return [pltpu.VMEM(master.shape, f32) for _ in range(3)]

    scratch = [
        pltpu.VMEM(features.shape, bf16),
        pltpu.VMEM(coords.shape, f32),
        pltpu.VMEM(valid_mask.shape, jnp.int32),
        pltpu.VMEM(neighbors.shape, jnp.int32),
        pltpu.VMEM(features.shape, bf16),
        pltpu.VMEM((SQUARE,), bf16),
        pltpu.VMEM((1024,), bf16),
        pltpu.VMEM(weights.shape, bf16),
        shard(),
        shard(),
        pltpu.VMEM((2, *features.shape), bf16),
        pltpu.VMEM((1, LANES), f32),
        dma((11,)),
        dma((7,)),
        pltpu.VMEM((7, 8, LANES), f32),
        pltpu.VMEM((7, n, 8, LANES), f32),
        dma((7,)),
        dma((7,)),
        pltpu.VMEM((TAIL_PAD,), bf16),
        pltpu.VMEM((9, WIDTH, WIDTH), bf16),
        pairs(WINDOW, bf16),
        pairs(WIDTH),
        pairs(GROUPS),
        pairs(GROUPS),
        pairs(GROUPS, bf16),
        pairs(GROUPS),
        pairs(8),
        pairs(8),
        pairs(8),
        pairs(8),
        pairs(8),
        pairs(8),
        pltpu.VMEM((WIDTH, points), bf16),
        pltpu.VMEM((points, WIDTH), f32),
        pairs(8),
        pltpu.VMEM((points, WIDTH), f32),
        pltpu.VMEM((points, WIDTH), f32),
        pltpu.VMEM((points, WIDTH), bf16),
        pltpu.VMEM((WIDTH, points), bf16),
        pltpu.VMEM((WIDTH, points), bf16),
        pltpu.VMEM((WIDTH, points), bf16),
        pltpu.VMEM((6 * GROUPS, WIDTH), bf16),
        pltpu.VMEM((points, WIDTH), bf16),
        pltpu.VMEM((WIDTH, points), f32),
        pltpu.VMEM((points, WIDTH), f32),
        pltpu.VMEM((points, GROUPS), f32),
        pltpu.VMEM((3 * GROUPS, points), f32),
        pltpu.VMEM((3 * GROUPS, points), f32),
        pairs(GROUPS, bf16),
        pltpu.VMEM((WIDTH, PAIRS), bf16),
        pltpu.VMEM((points, WIDTH), f32),
        pltpu.VMEM((points, WIDTH), bf16),
        pltpu.VMEM((WIDTH, LANES), f32),
        pltpu.VMEM((dense_pairs, 2, SLICE_ROWS, LANES), f32),
        pltpu.VMEM((dense_pairs, SLICE_ROWS, LANES), f32),
        pltpu.VMEM((dense_pairs, SLICE_ROWS, LANES), bf16),
        pltpu.VMEM((slots, half, SLICE_ROWS, LANES), bf16),
        pltpu.VMEM((2, per_matrix, 2, SLICE_ROWS, LANES), f32),
        pltpu.VMEM((2, per_matrix, SLICE_ROWS, LANES), f32),
        pltpu.VMEM((2, per_matrix, 2, SLICE_ROWS, LANES), bf16),
        pltpu.VMEM((2, half, 2, SLICE_ROWS, LANES), bf16),
        pltpu.VMEM((per_matrix, 2, LOW_ROWS, LANES), f32),
        pltpu.VMEM((per_matrix, LOW_ROWS, LANES), f32),
        pltpu.VMEM((per_matrix, LOW_ROWS, LANES), f32),
        pltpu.VMEM((low_kinds, half, LOW_ROWS, LANES), f32),
        pltpu.VMEM((slots, SLICE_ROWS, LANES), f32),
        pltpu.VMEM((up(max(span * SLICE_ROWS, SLICE_ROWS + shard_rows), SLICE_ROWS), LANES), f32),
        pltpu.VMEM((shard_rows * LANES,), f32),
        pltpu.VMEM((slab_rows, LANES), f32),
        pltpu.VMEM((slab_rows, LANES), bf16),
        pltpu.VMEM((2, half, slab_rows, LANES), bf16),
        dma((5,)),
        dma((5,)),
        dma((slots,)),
        dma((slots,)),
        dma((2,)),
        dma((2,)),
        dma((low_kinds,)),
        dma((low_kinds,)),
        dma((slots, sides)),
        dma((span,)),
        dma,
        dma((half,)),
        dma,
        dma,
    ]
    results = pl.pallas_call(
        functools.partial(block_kernel, n_rows, n_cols),
        out_shape=(
            shape(features.shape, bf16),
            shape(features.shape, bf16),
            shape((1, LANES), f32),
            shape(master.shape, f32),
            shape(master.shape, f32),
            shape(master.shape, f32),
            pltpu.VMEM(weights.shape, bf16),
        ),
        in_specs=[hbm] * 9,
        out_specs=[pl.BlockSpec(memory_space=pl.ANY)] * 6 + [vmem],
        scratch_shapes=scratch,
        compiler_params=pltpu.CompilerParams(
            collective_id=0, has_side_effects=True, vmem_limit_bytes=48 * 2**20
        ),
    )(*(pltpu.with_memory_space_constraint(x, pltpu.HBM) for x in (features, coords, valid_mask, neighbors, cotangent, weights, master, first_moment, second_moment)))
    results = pl.pallas_call(
        finish_kernel,
        out_shape=(
            shape(features.shape, bf16),
            shape(features.shape, bf16),
            shape((1, 1), f32),
            shape(master.shape, f32),
            shape(master.shape, f32),
            shape(master.shape, f32),
            shape(weights.shape, bf16),
        ),
        in_specs=[pl.BlockSpec(memory_space=pl.ANY)] * 7,
        out_specs=[hbm, hbm, vmem, hbm, hbm, hbm, hbm],
        scratch_shapes=[pltpu.VMEM((1, LANES), f32), dma((7,))],
        compiler_params=pltpu.CompilerParams(vmem_limit_bytes=8 * 2**20),
    )(*results)
    return results[0], results[1], results[2].reshape(()), *results[3:]


def solution(mesh):
    both = ("rows", "cols")
    rows_split, cols_split, flat_split = P(both, None), P(None, both), P(both)
    return jax.shard_map(
        functools.partial(shards, mesh.shape["rows"], mesh.shape["cols"]),
        mesh=mesh,
        in_specs=(
            rows_split, cols_split, flat_split, cols_split, rows_split, P(),
            flat_split, flat_split, flat_split,
        ),
        out_specs=(rows_split, rows_split, P(), flat_split, flat_split, flat_split, P()),
        check_vma=False,
    )
```

```python
import functools

import jax
import jax.numpy as jnp
from jax import lax
from jax.experimental import pallas as pl
from jax.experimental.pallas import tpu as pltpu
from jax.sharding import PartitionSpec as P

WIDTH = 256
GROUPS = 32
NEAREST = 16
PER_GROUP = WIDTH // GROUPS
LANES = 128
WINDOW = 256
PAIRS = NEAREST * LANES

SQUARE = WIDTH * WIDTH
OFF_ATT_IN = 5 * SQUARE
OFF_ATT_OUT = OFF_ATT_IN + WIDTH * GROUPS
OFF_TAIL = OFF_ATT_OUT + GROUPS * GROUPS
NORMS = 2 * WIDTH + 3 + GROUPS
TAIL_POS_OUT = 9
TAIL_GAINS = TAIL_POS_OUT + 3 * WIDTH
TAIL_SHIFTS = TAIL_GAINS + NORMS
TAIL_USED = TAIL_SHIFTS + NORMS
TAIL_PAD = 2048
SLICE = 2048
SLICE_ROWS = SLICE // LANES
LOW_ROWS = SLICE // WIDTH * 2 * GROUPS // LANES
DENSE_FROM = 3
CHUNK = 1024

bn_eps = 1e-05
clip_norm = 0.01
learn_rate = 0.05
beta_one = 0.9
beta_two = 0.999
adam_eps = 1e-08
decay_rate = 0.01
step_count = 10
masked_logit = -1000000000.0

f32 = jnp.float32
bf16 = jnp.bfloat16
MESH = pl.DeviceIdType.MESH


def contract(a, b, left, right):
    return lax.dot_general(a, b, (((left,), (right,)), ((), ())), preferred_element_type=f32)


def nn(a, b):
    return contract(a, b, 1, 0)


def nt(a, b):
    return contract(a, b, 1, 1)


def tn(a, b):
    return contract(a, b, 0, 0)


def split(value, parts):
    pieces = []
    for _ in range(parts):
        piece = value.astype(bf16)
        pieces.append(piece)
        value = value - piece.astype(f32)
    return pieces


def silu_parts(value):
    gate = 0.5 * jnp.tanh(0.5 * value) + 0.5
    return value * gate, gate


def silu_slope(value, gate):
    return gate * (1.0 + value * (1.0 - gate))


def iota(shape, dim):
    return lax.broadcasted_iota(jnp.int32, shape, dim)


def loop(begin, end, body):
    if end - begin <= 31:
        for k in range(begin, end):
            body(k, 0)
    else:
        lax.fori_loop(begin, end, body, 0)


def row_to_col(row, count):
    wide = jnp.broadcast_to(row, (count, row.shape[1]))
    same = iota(wide.shape, 0) == iota(wide.shape, 1)
    return jnp.sum(jnp.where(same, wide, 0.0), axis=1, keepdims=True)


def col_to_row(col, offset):
    wide = jnp.broadcast_to(col, (col.shape[0], LANES))
    same = iota(wide.shape, 0) + offset == iota(wide.shape, 1)
    return jnp.sum(jnp.where(same, wide, 0.0), axis=0, keepdims=True)


def row_sum(value):
    return jnp.sum(value, axis=0, keepdims=True)


def lane_fold(value):
    total = value[:, 0:LANES]
    for k in range(1, value.shape[1] // LANES):
        total = total + value[:, k * LANES : (k + 1) * LANES]
    return total


def lane_sum(value):
    return jnp.sum(lane_fold(value), axis=1, keepdims=True)


def tiles(value):
    return jnp.concatenate([value] * NEAREST, axis=1)


def adam(param, moment, second, grad):
    moment_new = beta_one * moment + (1.0 - beta_one) * grad
    second_new = beta_two * second + (1.0 - beta_two) * grad * grad
    moment_hat = moment_new / (1.0 - beta_one**step_count)
    second_hat = second_new / (1.0 - beta_two**step_count)
    param_new = param - learn_rate * (
        moment_hat / (jnp.sqrt(second_hat) + adam_eps) + decay_rate * param
    )
    return param_new, moment_new, second_new


def peer(me, step, count):
    if count & (count - 1) == 0:
        return me ^ (count - step)
    return lax.rem(me + step, count)


def block_kernel(
    n_rows, n_cols,
    feat_h, coords_h, valid_h, nbrs_h, cot_h, weights_h, master_h, first_h, second_h,
    out_h, gfeat_h, gnorm_h, new_master_h, new_first_h, new_second_h, weights_out,
    feat, coords, valid, nbrs, cot, w_first, pos_first, weights, state, news, outs, norm_s, in_sem, out_sem,
    stat_send, stat_buf, stat_ssem, stat_rsem,
    tail1d, mats, onehot, vgat, att, wpre, uact, dyw, rel, pos, act, pmask, allow, dmix,
    ft_s, slope_a, slope_p, a1_s, z_s, h_s, h_ts, q_s, k_s, ba_s, o_s, o_ts, do_s, dv_s, sk_s, bd_s, dp_s, ds_s, dw_s, xs, dz_s, dz16,
    mu_s, flat, pair_got, part16, got16, first_f, first_got, wide16, got_wide, low_f, low_got, low_sum, got_low, hat_s, sums, owned, tail_g, slab_f, shard_w, all_w,
    pair_ssem, pair_rsem, rs_ssem, rs_rsem, wd_ssem, wd_rsem, low_ssem, low_rsem, own_ssem, own_rsem, ag_ssem, ag_rsem, fw_ssem, fw_rsem,
):
    n = n_rows * n_cols
    half = n // 2
    row_id, col_id = lax.axis_index("rows"), lax.axis_index("cols")
    me = row_id * n_cols + col_id
    core = lax.rem(col_id, 2)
    chip = me // 2
    points = feat.shape[0]
    blocks = points // LANES
    starts = [min(max(LANES * b - (WINDOW - LANES) // 2, 0), points - WINDOW) for b in range(blocks)]
    total_len = weights.shape[0]
    shard_len = master_h.shape[0]
    shard_rows = -(-tail_g.shape[0] // LANES)
    per_matrix = SQUARE // SLICE // 2
    dense = DENSE_FROM * per_matrix
    sliced = dense + flat.shape[0]
    slots = got16.shape[0]
    low_kinds = got_low.shape[0]
    sides = own_ssem.shape[1]
    span = own_rsem.shape[0]

    def place(device):
        return (device // n_cols, lax.rem(device, n_cols))

    barrier = pltpu.get_barrier_semaphore()

    def greet(k, carry):
        pl.semaphore_signal(barrier, inc=1, device_id=place(peer(me, k, n)), device_id_type=MESH)
        return carry

    loop(1, n, greet)
    loads = []

    def load(source, target):
        copy = pltpu.make_async_copy(source, target, in_sem.at[len(loads)])
        copy.start()
        loads.append(copy)
        return copy

    stores = []

    def store(source, target):
        copy = pltpu.make_async_copy(source, target, out_sem.at[len(stores)])
        copy.start()
        stores.append(copy)

    early = [
        load(feat_h, feat),
        load(weights_h.at[pl.ds(0, SQUARE)], w_first),
        load(weights_h.at[pl.ds(OFF_TAIL, 1024)], pos_first),
        load(nbrs_h, nbrs),
        load(coords_h, coords),
        load(valid_h, valid),
    ]

    late = [load(weights_h, weights), load(cot_h, cot)]
    for source, target in ((master_h, 0), (first_h, 1), (second_h, 2)):
        late.append(load(source, state[target]))
    owned[...] = jnp.zeros(owned.shape, f32)
    for copy in early:
        copy.wait()

    sent = []

    def all_sum(index, message):
        rows = message.shape[0]
        stat_send[index, 0:rows] = message
        stat_buf[index, me, 0:rows] = message

        def post(k, carry):
            pltpu.make_async_remote_copy(
                src_ref=stat_send.at[index, pl.ds(0, rows)],
                dst_ref=stat_buf.at[index, me, pl.ds(0, rows)],
                send_sem=stat_ssem.at[index],
                recv_sem=stat_rsem.at[index],
                device_id=place(peer(me, k, n)),
                device_id_type=MESH,
            ).start()
            return carry

        loop(1, n, post)
        sent.append((index, rows))

        def collect():
            span = stat_buf.at[index, pl.ds(0, n - 1), pl.ds(0, rows)]
            pltpu.make_async_copy(span, span, stat_rsem.at[index]).wait()
            return jnp.sum(stat_buf[index, :, 0:rows], axis=0)

        return collect

    sibling = (row_id, col_id + 1 - 2 * core)
    def put_halves(target, value):
        rows = SLICE_ROWS // 2
        for k in range(2):
            part = value[:, k * LANES : (k + 1) * LANES]
            target[:, :, k * rows : (k + 1) * rows] = part.reshape(per_matrix, 2, rows, LANES)

    def whole_rows(piece):
        rows = SLICE_ROWS // 2
        return jnp.concatenate([piece[0:rows], piece[rows:]], axis=1).reshape(SLICE_ROWS, LANES)

    def put_matrix(m, grad):
        at = (m - DENSE_FROM) * per_matrix
        put_halves(flat.at[at : at + per_matrix], grad)

    def swap(group, source, target):
        copy = pltpu.make_async_remote_copy(
            src_ref=source.at[:, 1 - core],
            dst_ref=target,
            send_sem=pair_ssem.at[group],
            recv_sem=pair_rsem.at[group],
            device_id=sibling,
            device_id_type=MESH,
        )
        copy.start()
        return copy

    def to_chips(begin, count, send):
        if count == half and begin % half == 0:

            def post(k, carry):
                other = peer(chip, k, half)
                send(begin + other, other)
                return carry

            loop(1, half, post)
        else:

            def post_any(k, carry):
                index = begin + k
                other = lax.rem(index, half)

                @pl.when(other != chip)
                def _():
                    send(index, other)

                return carry

            loop(0, count, post_any)

    def send_dense(copy, begin, count):
        copy.wait()
        own = pl.ds(begin - dense, count)
        part16[own] = (flat[own, core] + pair_got[own]).astype(bf16)

        def send(index, other):
            pltpu.make_async_remote_copy(
                src_ref=part16.at[index - dense],
                dst_ref=got16.at[index // half, chip],
                send_sem=rs_ssem.at[index // half],
                recv_sem=rs_rsem.at[index // half],
                device_id=place(2 * other + core),
                device_id_type=MESH,
            ).start()

        at = begin
        while at < begin + count:
            step = min(half - at % half, begin + count - at)
            to_chips(at, step, send)
            at = at + step

    def send_wide(copy, which):
        copy.wait()
        for k, piece in enumerate(split(first_f[which, :, core] + first_got[which], 2)):
            wide16[which, :, k] = piece

        def send(index, other):
            pltpu.make_async_remote_copy(
                src_ref=wide16.at[which, index],
                dst_ref=got_wide.at[which, chip],
                send_sem=wd_ssem.at[which],
                recv_sem=wd_rsem.at[which],
                device_id=place(2 * other + core),
                device_id_type=MESH,
            ).start()

        to_chips(0, per_matrix, send)

    def send_low(copy):
        copy.wait()
        low_sum[...] = low_f[:, core] + low_got[...]
        for kind in range(low_kinds):

            def send(index, other, kind=kind):
                pltpu.make_async_remote_copy(
                    src_ref=low_sum.at[index - (1 + kind) * per_matrix],
                    dst_ref=got_low.at[kind, chip],
                    send_sem=low_ssem.at[kind],
                    recv_sem=low_rsem.at[kind],
                    device_id=place(2 * other + core),
                    device_id_type=MESH,
                ).start()

            to_chips((1 + kind) * per_matrix, per_matrix, send)

    def drain_stats(index, rows):
        span = stat_buf.at[index, pl.ds(0, n - 1), pl.ds(0, rows)]
        pltpu.make_async_copy(span, span, stat_ssem.at[index]).wait()

    w_in = w_first[...].reshape(WIDTH, WIDTH)
    mats[0] = w_in
    w_in = mats[0]
    pos_in = pos_first[...].reshape(1024 // LANES, LANES)[0:1].astype(f32)
    lane8 = iota((8, 1), 0)

    def pos_in_col(c):
        return jnp.where(lane8 < 3, row_to_col(pos_in[:, 3 * c : 3 * c + 8], 8), 0.0)

    valid_rows = valid[...].reshape(points // LANES, LANES).astype(f32)
    n_valid = jnp.sum(jnp.sum(valid_rows, axis=0, keepdims=True), axis=1, keepdims=True)
    point_mask = (iota((points, 1), 0).astype(f32) < n_valid).astype(f32)
    lane_mask = (iota((1, points), 1).astype(f32) < n_valid).astype(f32)

    a1 = nn(feat[...], w_in)
    a1_s[...] = a1
    masked = point_mask * a1
    sum_a, sqr_a = row_sum(masked), row_sum(masked * a1)

    weight = [[pos_in[:, 3 * c + d : 3 * c + d + 1] for d in range(3)] for c in range(3)]
    pos_one = [jnp.zeros((NEAREST, LANES), f32) for _ in range(3)]
    pos_two = [jnp.zeros((NEAREST, LANES), f32) for _ in range(3)]
    pairs_local = jnp.zeros((NEAREST, LANES), f32)
    for b in range(blocks):
        here = slice(b * LANES, (b + 1) * LANES)
        index = nbrs[:, here]
        tile, at = lax.shift_right_logical(index, 7), index & (LANES - 1)

        def fetch(c, t):
            row = jnp.broadcast_to(coords[c : c + 1, t * LANES : (t + 1) * LANES], index.shape)
            return jnp.take_along_axis(row, at, axis=1, mode="promise_in_bounds")

        r = []
        for c in range(3):
            near = fetch(c, b)
            if b > 0:
                near = jnp.where(tile < b, fetch(c, b - 1), near)
            if b < blocks - 1:
                near = jnp.where(tile > b, fetch(c, b + 1), near)
            r.append(near - coords[c : c + 1, here])
        pm = jnp.where(index.astype(f32) < n_valid, lane_mask[:, here], 0.0)
        pairs_local = pairs_local + pm
        for d in range(3):
            p = weight[0][d] * r[0] + weight[1][d] * r[1] + weight[2][d] * r[2]
            pos_one[d] = pos_one[d] + pm * p
            pos_two[d] = pos_two[d] + pm * p * p

    def total(value):
        return jnp.sum(row_sum(value), axis=1, keepdims=True)

    lane = iota((1, LANES), 1)
    last = jnp.where(lane == 16, n_valid, 0.0) + jnp.where(lane == 17, total(pairs_local), 0.0)
    for d in range(3):
        last = last + jnp.where(lane == d, total(pos_one[d]), 0.0)
        last = last + jnp.where(lane == 8 + d, total(pos_two[d]), 0.0)

    def fold(row):
        return jnp.concatenate([row[:, 0:LANES], row[:, LANES:WIDTH]], axis=0)

    def unfold(rows):
        return jnp.concatenate([rows[0:1], rows[1:2]], axis=1)

    pl.semaphore_wait(barrier, n - 1)
    collect_first = all_sum(0, jnp.concatenate([fold(sum_a), fold(sqr_a), last], axis=0))
    window_row = iota((WINDOW, LANES), 0)
    for b in range(blocks):
        for j in range(NEAREST):
            index = nbrs[j : j + 1, b * LANES : (b + 1) * LANES] - starts[b]
            onehot[b, :, j * LANES : (j + 1) * LANES] = jnp.where(
                window_row == index, 1.0, 0.0
            ).astype(bf16)

    coords8 = jnp.concatenate([coords[...], jnp.zeros((5, points), f32)], axis=0)
    table = jnp.concatenate(
        split(coords8, 3) + [jnp.broadcast_to(lane_mask, (8, points)).astype(bf16)], axis=0
    )
    slot0 = (iota((1, PAIRS), 1) < LANES).astype(f32)
    pos_in_cols = [pos_in_col(c) for c in range(3)]
    for b in range(blocks):
        here = slice(b * LANES, (b + 1) * LANES)
        fetched = nn(table[:, starts[b] : starts[b] + WINDOW], onehot[b])
        place_n = fetched[0:8] + fetched[8:16] + fetched[16:24]
        mask_n = fetched[24:32]
        r = place_n - tiles(coords8[:, here])
        pm = mask_n * tiles(lane_mask[:, here])
        p = pos_in_cols[0] * r[0:1] + pos_in_cols[1] * r[1:2] + pos_in_cols[2] * r[2:3]
        rel[b] = r
        pos[b] = p
        pmask[b] = pm
        allow[b] = jnp.maximum(mask_n, slot0)

    for copy in late:
        copy.wait()
    for m in range(1, 5):
        mats[m] = weights[pl.ds(m * SQUARE, SQUARE)].reshape(WIDTH, WIDTH)
    w_q, w_k, w_v, w_o = (mats[m] for m in range(1, 5))
    att_in = weights[pl.ds(OFF_ATT_IN, WIDTH * GROUPS)].reshape(WIDTH * GROUPS // LANES, LANES)
    att_in_f = att_in.astype(f32).reshape(WIDTH, GROUPS)
    att_in_t = att_in_f.T.astype(bf16)
    att_out_f = (
        weights[pl.ds(OFF_ATT_OUT, GROUPS * GROUPS)]
        .reshape(GROUPS * GROUPS // LANES, LANES)
        .astype(f32)
        .reshape(GROUPS, GROUPS)
    )
    att_out = att_out_f.astype(bf16)
    att_out_t = att_out_f.T.astype(bf16)
    tail1d[pl.ds(0, 1024)] = weights[pl.ds(OFF_TAIL, 1024)]
    rest = total_len - OFF_TAIL - 1024
    tail1d[pl.ds(1024, rest)] = weights[pl.ds(OFF_TAIL + 1024, rest)]
    tail = tail1d[pl.ds(0, TAIL_PAD)].reshape(TAIL_PAD // LANES, LANES).astype(f32)
    tail = jnp.concatenate([tail[k : k + 1] for k in range(TAIL_PAD // LANES)], axis=1)
    pos_rows = [tail[:, TAIL_POS_OUT + WIDTH * d : TAIL_POS_OUT + WIDTH * (d + 1)] for d in range(3)]
    def norm_pieces(start):
        ends = [0, WIDTH, WIDTH + 3, WIDTH + 3 + GROUPS, NORMS]
        return [tail[:, start + ends[k] : start + ends[k + 1]] for k in range(4)]

    gain_a, gain_p, gain_w, gain_o = norm_pieces(TAIL_GAINS)
    shift_a, shift_p, shift_w, shift_o = norm_pieces(TAIL_SHIFTS)

    def pad_col(row):
        wide = jnp.concatenate([row, jnp.zeros((1, 5), f32)], axis=1)
        return row_to_col(wide, 8)

    gain_p, shift_p = pad_col(gain_p), pad_col(shift_p)
    gain_w, shift_w = row_to_col(gain_w, GROUPS), row_to_col(shift_w, GROUPS)

    new_at = iota((WIDTH, WIDTH), 0)
    reorder = jnp.where(
        iota((WIDTH, WIDTH), 1) == new_at % GROUPS * PER_GROUP + new_at // GROUPS, 1.0, 0.0
    ).astype(bf16)
    w_o_new = nn(reorder, w_o)
    mats[4] = w_o_new.astype(bf16)
    mats[5] = w_o_new.T.astype(bf16)
    mats[6] = w_q.astype(f32).T.astype(bf16)
    mats[7] = w_k.astype(f32).T.astype(bf16)
    mats[8] = nt(reorder, w_v).astype(bf16)
    pos_mat = jnp.concatenate(pos_rows + [jnp.zeros((13, WIDTH), f32)], axis=0).astype(bf16)
    pos_cols = nt(reorder, pos_mat)
    pos_cols = [pos_cols[:, d : d + 1] for d in range(3)]
    feat_f = feat[...].astype(f32)
    ft_s[...] = feat_f.T.astype(bf16)
    sum_f = row_sum(point_mask * feat_f)
    stats = collect_first()

    def pick(row, at):
        return jnp.sum(jnp.where(lane == at, row, 0.0), axis=1, keepdims=True)

    point_count, pair_count = pick(stats[4:5], 16), pick(stats[4:5], 17)
    inv_points, inv_pairs = 1.0 / point_count, 1.0 / pair_count

    def moments(total, square, inv):
        mean = total * inv
        return mean, lax.rsqrt(square * inv - mean * mean + bn_eps)

    mean_a, rs_a = moments(unfold(stats[0:2]), unfold(stats[2:4]), inv_points)
    mean_p, rs_p = moments(
        row_to_col(stats[4:5, 0:8], 8), row_to_col(stats[4:5, 8:16], 8), inv_pairs
    )

    h = silu_parts((a1_s[...] - mean_a) * rs_a * gain_a + shift_a)[0]
    h_s[...] = h.astype(bf16)
    h_t = h.T.astype(bf16)
    q_t = nn(mats[6], h_t).astype(bf16)
    k_t = nn(mats[7], h_t).astype(bf16)
    q_s[...] = q_t
    k_s[...] = k_t
    h_ts[...] = h_t
    q_att = nn(att_in_t, q_t)
    k_att = jnp.concatenate(split(nn(att_in_t, k_t), 3), axis=0)
    pos_att = nt(att_in_t, pos_mat)
    pos_att_cols = [pos_att[:, d : d + 1] for d in range(3)]
    back_att = jnp.concatenate([nn(att_in_t, mats[6]), nn(att_in_t, mats[7])], axis=0)
    back_split = split(back_att, 2)
    ba_s[...] = jnp.concatenate([back_split[0], back_split[0], back_split[1]], axis=0)

    sum_w = jnp.zeros((GROUPS, LANES), f32)
    sqr_w = jnp.zeros((GROUPS, LANES), f32)
    for b in range(blocks):
        here = slice(b * LANES, (b + 1) * LANES)
        active = silu_parts((pos[b] - mean_p) * rs_p * gain_p + shift_p)[0]
        act[b] = active
        fetched = nn(k_att[:, starts[b] : starts[b] + WINDOW], onehot[b])
        w = tiles(q_att[:, here]) - (
            fetched[0:GROUPS] + fetched[GROUPS : 2 * GROUPS] + fetched[2 * GROUPS : 3 * GROUPS]
        )
        for d in range(3):
            w = w + pos_att_cols[d] * active[d : d + 1]
        wpre[b] = w
        mw = w * pmask[b, 0:1]
        sum_w = sum_w + lane_fold(mw)
        sqr_w = sqr_w + lane_fold(mw * w)

    def pair_row(one, two):
        one = jnp.sum(one, axis=1, keepdims=True)
        two = jnp.sum(two, axis=1, keepdims=True)
        return col_to_row(one, 0) + col_to_row(two, GROUPS)

    collect_w = all_sum(1, jnp.concatenate([pair_row(sum_w, sqr_w), fold(sum_f)], axis=0))
    v_t = nn(mats[8], h_ts[...]).astype(bf16)
    for b in range(blocks):
        vgat[b] = nn(v_t[:, starts[b] : starts[b] + WINDOW], onehot[b])
    stats = collect_w()
    mean_f = stats[1:3] * inv_points
    mean_w, rs_w = moments(
        row_to_col(stats[0:1, 0:GROUPS], GROUPS),
        row_to_col(stats[0:1, GROUPS : 2 * GROUPS], GROUPS),
        inv_pairs,
    )

    def each_channel(value):
        return jnp.concatenate([value] * PER_GROUP, axis=0)

    def over_channels(value):
        return functools.reduce(
            jnp.add, [value[c * GROUPS : (c + 1) * GROUPS] for c in range(PER_GROUP)]
        )

    def cols(j):
        return slice(j * LANES, (j + 1) * LANES)

    for b in range(blocks):
        here = slice(b * LANES, (b + 1) * LANES)
        u = silu_parts((wpre[b] - mean_w) * rs_w * gain_w + shift_w)[0].astype(bf16)
        uact[b] = u
        logit = jnp.where(allow[b, 0:1] > 0.5, nn(att_out_t, u), masked_logit)
        top = logit[:, cols(0)]
        for j in range(1, NEAREST):
            top = jnp.maximum(top, logit[:, cols(j)])
        weight = jnp.exp(logit - tiles(top))
        share = 1.0 / functools.reduce(jnp.add, [weight[:, cols(j)] for j in range(NEAREST)])
        att[b] = weight * tiles(share)
        mixed = jnp.zeros((WIDTH, LANES), f32)
        enc = [jnp.zeros((GROUPS, LANES), f32) for _ in range(3)]
        for j in range(NEAREST):
            a = att[b, :, cols(j)]
            mixed = mixed + each_channel(a) * vgat[b, :, cols(j)]
            for d in range(3):
                enc[d] = enc[d] + a * act[b, d : d + 1, cols(j)]
        bd_s[:, here] = jnp.concatenate(enc, axis=0)
        for d in range(3):
            mixed = mixed + pos_cols[d] * each_channel(enc[d])
        o_s[here, :] = mixed.T.astype(bf16)

    z = nn(o_s[...], mats[4])
    z_s[...] = z
    masked = point_mask * z
    collect_o = all_sum(2, jnp.concatenate([fold(row_sum(masked)), fold(row_sum(masked * z))], axis=0))
    for k in range(2):
        mu_s[k * LANES : (k + 1) * LANES] = jnp.broadcast_to(
            row_to_col(mean_f[k : k + 1], LANES), (LANES, LANES)
        )

    def put_first(which, value):
        put_halves(first_f.at[which], value)
        return swap(which, first_f.at[which], first_got.at[which])

    def from_feat(value):
        return nn(
            jnp.concatenate([ft_s[...]] * 2, axis=1), jnp.concatenate(split(value, 2), axis=0)
        )

    ahat = (a1_s[...] - mean_a) * rs_a
    a1_s[...] = ahat
    ahat_pair = put_first(0, from_feat(point_mask * ahat))
    for b in range(blocks):
        what = (wpre[b] - mean_w) * rs_w
        wpre[b] = what
        y = what * gain_w + shift_w
        dyw[b] = silu_slope(y, silu_parts(y)[1])
    send_wide(ahat_pair, 0)
    o_ts[...] = nn(o_s[...], reorder).T.astype(bf16)
    stats = collect_o()
    mean_o, rs_o = moments(unfold(stats[0:2]), unfold(stats[2:4]), inv_points)

    zhat = (z_s[...] - mean_o) * rs_o
    z_s[...] = zhat
    y = feat[...].astype(f32) + zhat * gain_o + shift_o
    value, gate = silu_parts(y)
    outs[0] = (point_mask * value).astype(bf16)
    store(outs.at[0], out_h)
    dy = point_mask * cot[...].astype(f32) * silu_slope(y, gate)
    dz_s[...] = dy
    shift_grad_o, gain_grad_o = row_sum(dy), row_sum(dy * zhat)
    collect_o = all_sum(3, jnp.concatenate([fold(shift_grad_o), fold(gain_grad_o)], axis=0))
    for b in range(blocks):
        phat = (pos[b] - mean_p) * rs_p
        pos[b] = phat
        y = phat * gain_p + shift_p
        slope_p[b] = silu_slope(y, silu_parts(y)[1])
    y = a1_s[...] * gain_a + shift_a
    slope_a[...] = silu_slope(y, silu_parts(y)[1])
    pos_row = jnp.zeros((1, LANES), f32)
    for c in range(3):
        with_hat, alone = jnp.zeros((8, 1), f32), jnp.zeros((8, 1), f32)
        for b in range(blocks):
            masked = pmask[b] * rel[b, c : c + 1]
            with_hat = with_hat + lane_sum(masked * pos[b])
            alone = alone + lane_sum(masked)
        pos_row = pos_row + col_to_row(with_hat, 64 + 8 * c) + col_to_row(alone, 88 + 8 * c)
    stats = collect_o()
    one, two = unfold(stats[0:2]) * inv_points, unfold(stats[2:4]) * inv_points
    dz = (gain_o * rs_o * (dz_s[...] - point_mask * (one + z_s[...] * two))).astype(bf16)
    dz16[...] = dz
    do_s[...] = nn(dz, mats[5]).T

    sum_w = jnp.zeros((GROUPS, LANES), f32)
    sqr_w = jnp.zeros((GROUPS, LANES), f32)
    for b in range(blocks):
        here = slice(b * LANES, (b + 1) * LANES)
        do = do_s[:, here]
        do_pos = [over_channels(do * pos_cols[d]) for d in range(3)]
        dp_s[:, here] = jnp.concatenate(do_pos, axis=0)
        da = []
        for j in range(NEAREST):
            grad = over_channels(do * vgat[b, :, cols(j)])
            for d in range(3):
                grad = grad + do_pos[d] * act[b, d : d + 1, cols(j)]
            da.append(grad)
        mean_da = functools.reduce(jnp.add, [da[j] * att[b, :, cols(j)] for j in range(NEAREST)])
        ds = jnp.concatenate(
            [att[b, :, cols(j)] * (da[j] - mean_da) for j in range(NEAREST)], axis=1
        ).astype(bf16)
        ds_s[b] = ds
        dy = nn(att_out, ds) * dyw[b]
        dyw[b] = dy
        sum_w = sum_w + lane_fold(dy)
        sqr_w = sqr_w + lane_fold(dy * wpre[b])

    back_w = pair_row(sum_w, sqr_w)
    collect_w = all_sum(4, back_w + pos_row)
    put_matrix(4, nn(o_ts[...], dz16[...]))
    o_flat, v_flat = pl.ds(per_matrix, per_matrix), pl.ds(0, per_matrix)
    o_pair = swap(2, flat.at[o_flat], pair_got.at[o_flat])
    add_groups = jnp.where(
        iota((8, 3 * GROUPS), 1) // GROUPS == iota((8, 3 * GROUPS), 0), 1.0, 0.0
    ).astype(bf16)
    dv_s[...] = jnp.zeros(dv_s.shape, f32)
    for b in range(blocks):
        here = slice(b * LANES, (b + 1) * LANES)
        do = do_s[:, here]
        for j in range(NEAREST):
            xs[b, :, cols(j)] = (each_channel(att[b, :, cols(j)]) * do).astype(bf16)
        mix = [
            (tiles(dp_s[d * GROUPS : (d + 1) * GROUPS, here]) * att[b]).astype(bf16) for d in range(3)
        ]
        dmix[b] = nn(add_groups, jnp.concatenate(mix, axis=0))
        dv_s[pl.ds(starts[b], WINDOW)] += nt(onehot[b], xs[b])
    dv = dv_s[...].astype(bf16)
    dv_s[...] = nn(dv, mats[8])
    put_matrix(3, nn(h_ts[...], nn(dv, reorder).astype(bf16)))
    v_pair = swap(5, flat.at[v_flat], pair_got.at[v_flat])
    send_dense(o_pair, dense + per_matrix, per_matrix)
    send_dense(v_pair, dense, per_matrix)
    stats = collect_w()
    one = row_to_col(stats[:, 0:GROUPS], GROUPS) * inv_pairs
    two = row_to_col(stats[:, GROUPS : 2 * GROUPS], GROUPS) * inv_pairs
    pos_hat = [row_to_col(stats[:, 64 + 8 * c : 72 + 8 * c], 8) for c in range(3)]
    pos_alone = [row_to_col(stats[:, 88 + 8 * c : 96 + 8 * c], 8) for c in range(3)]

    sk_s[...] = jnp.zeros(sk_s.shape, f32)
    pos_att_rows = split(pos_att[:, 0:8].T, 3)
    pos_att_rows = jnp.concatenate(pos_att_rows, axis=0)
    dw_sums = []
    for b in range(blocks):
        dw = (gain_w * rs_w * (dyw[b] - pmask[b, 0:1] * (one + wpre[b] * two))).astype(bf16)
        sk_s[pl.ds(starts[b], WINDOW)] += nt(onehot[b], dw)
        dw_sums.append(lane_slots(dw.astype(f32)))
        dw_s[b] = dw
    dq_att = jnp.concatenate(dw_sums, axis=1)
    both_att = jnp.concatenate([dq_att.T, -sk_s[...]], axis=1)
    both_split = split(both_att, 2)
    low = nn(
        jnp.concatenate([h_ts[...]] * 2, axis=1), jnp.concatenate(both_split, axis=0)
    )
    low_f[...] = low.reshape(per_matrix, 2, LOW_ROWS, LANES)
    low_pair = swap(3, low_f, low_got)
    dh = nn(jnp.concatenate(both_split + both_split[0:1], axis=1), ba_s[...]) + dv_s[...]
    dy = dh * slope_a[...]
    z_s[...] = dy
    shift_grad_a = row_sum(dy)
    away = jnp.concatenate(
        [mu_s[...] * shift_grad_a[:, k * LANES : (k + 1) * LANES] for k in range(2)], axis=1
    )
    first_pair = put_first(1, from_feat(dy) - away)
    along = [jnp.zeros((8, 1), f32) for _ in range(3)]
    sum_p = jnp.zeros((8, 1), f32)
    sqr_p = jnp.zeros((8, 1), f32)
    for b in range(blocks):
        back = nn(pos_att_rows, dw_s[b])
        d_act = dmix[b] + back[0:8] + back[8:16] + back[16:24]
        dy = d_act * slope_p[b]
        sum_p = sum_p + lane_sum(dy)
        sqr_p = sqr_p + lane_sum(dy * pos[b])
        for c in range(3):
            along[c] = along[c] + lane_sum(dy * rel[b, c : c + 1])
    gain_grad_a = row_sum(z_s[...] * a1_s[...])
    last = col_to_row(sum_p, 0) + col_to_row(sqr_p, 8)
    for c in range(3):
        last = last + col_to_row(along[c], 16 + 8 * c)
    collect_a = all_sum(
        5, jnp.concatenate([fold(shift_grad_a), fold(gain_grad_a), last], axis=0)
    )
    send_wide(first_pair, 1)
    send_low(low_pair)

    d_att_out = sum(nt(uact[b], ds_s[b]) for b in range(blocks))
    d_pos_att = sum(
        nt(jnp.concatenate(split(act[b], 3), axis=0), dw_s[b]) for b in range(blocks)
    )
    d_pos_att = d_pos_att[0:8] + d_pos_att[8:16] + d_pos_att[16:24]
    d_pos_split = split(d_pos_att, 3)
    d_att_in = sum(
        nn(q_s[...], piece[:, 0:GROUPS]) + nn(k_s[...], piece[:, GROUPS : 2 * GROUPS])
        for piece in both_split
    )
    d_att_in = d_att_in + sum(tn(pos_mat[0:8], piece) for piece in d_pos_split)
    d_pos_out = sum(nn(piece, att_in_t) for piece in d_pos_split)
    do_split = split(do_s[...], 2)
    bd_split = split(bd_s[...], 2)
    cross = nt(bd_split[0], do_split[0]) + nt(bd_split[0], do_split[1]) + nt(bd_split[1], do_split[0])
    own_group = iota((GROUPS, WIDTH), 1) % GROUPS == iota((GROUPS, WIDTH), 0)
    cross = [
        row_sum(jnp.where(own_group, cross[d * GROUPS : (d + 1) * GROUPS], 0.0)) for d in range(3)
    ]
    cross = jnp.concatenate(cross + [jnp.zeros((5, WIDTH), f32)], axis=0)
    d_pos_out = d_pos_out + sum(nn(piece, reorder) for piece in split(cross, 3))
    d_pos_rows = [d_pos_out[d : d + 1] for d in range(3)]
    pieces = [jnp.zeros((1, TAIL_POS_OUT), f32)] + d_pos_rows
    pieces = pieces + [
        gain_grad_a, col_to_row(sqr_p, 0)[:, 0:3], back_w[:, GROUPS : 2 * GROUPS], gain_grad_o,
        shift_grad_a, col_to_row(sum_p, 0)[:, 0:3], back_w[:, 0:GROUPS], shift_grad_o,
        jnp.zeros((1, TAIL_PAD - TAIL_USED), f32),
    ]
    small = 5 * per_matrix
    used_rows = OFF_TAIL // LANES + TAIL_PAD // LANES - 5 * SQUARE // LANES
    spare_rows = (sliced - small) * 2 * SLICE_ROWS - used_rows
    pieces_rows = [
        d_att_in.reshape(WIDTH * GROUPS // LANES, LANES),
        d_att_out.reshape(GROUPS * GROUPS // LANES, LANES),
        jnp.concatenate(pieces, axis=1).reshape(TAIL_PAD // LANES, LANES),
        jnp.zeros((spare_rows, LANES), f32),
    ]
    flat[small - dense : sliced - dense] = jnp.concatenate(pieces_rows, axis=0).reshape(
        sliced - small, 2, SLICE_ROWS, LANES
    )
    small_flat = pl.ds(small - dense, sliced - small)
    small_pair = swap(4, flat.at[small_flat], pair_got.at[small_flat])
    send_dense(small_pair, small, sliced - small)

    stats = collect_a()
    one, two = unfold(stats[0:2]) * inv_points, unfold(stats[2:4]) * inv_points
    def halves(row):
        return jnp.concatenate(
            [
                jnp.broadcast_to(row[:, k * LANES : (k + 1) * LANES], (SLICE_ROWS // 2, LANES))
                for k in range(2)
            ],
            axis=0,
        )

    scale_tile, two_tile = halves(gain_a * rs_a), halves(two)
    da1 = (gain_a * rs_a * (z_s[...] - point_mask * (one + a1_s[...] * two))).astype(bf16)
    outs[1] = (dz_s[...] + nt(da1, w_in)).astype(bf16)
    store(outs.at[1], gfeat_h)
    one = row_to_col(stats[4:5, 0:8], 8) * inv_pairs
    two = row_to_col(stats[4:5, 8:16], 8) * inv_pairs
    pos_in_row = jnp.zeros((1, LANES), f32)
    for c in range(3):
        moved = row_to_col(stats[4:5, 16 + 8 * c : 24 + 8 * c], 8)
        moved = gain_p * rs_p * (moved - one * pos_alone[c] - two * pos_hat[c])
        pos_in_row = pos_in_row + col_to_row(moved, 3 * c)

    def slice_of(slot):
        return 2 * (slot * half + chip) + core

    def when_in(slot, low, high, act_on):
        if (slot + 1) * n <= low or slot * n >= high:
            return
        if slot * n >= low and (slot + 1) * n <= high:
            act_on()
        else:
            number = slice_of(slot)
            pl.when((number >= low) & (number < high))(act_on)

    def others_sum(total, part):
        def add(k, total):
            return total + part(peer(chip, k, half))

        return lax.fori_loop(1, half, add, total, unroll=half <= 16)

    def take_wide(which):
        got = got_wide.at[which, pl.ds(0, half - 1)]
        pltpu.make_async_copy(got, got, wd_rsem.at[which]).wait()
        index = lax.rem(chip, per_matrix)

        def part(other):
            return got_wide[which, other, 0].astype(f32) + got_wide[which, other, 1].astype(f32)

        return others_sum(first_f[which, index, core] + first_got[which, index], part)

    def take_low(kind):
        got = got_low.at[kind, pl.ds(0, half - 1)]
        pltpu.make_async_copy(got, got, low_rsem.at[kind]).wait()
        index = lax.rem(chip, per_matrix)
        return others_sum(low_sum[index], lambda other: got_low[kind, other])

    def low_product(factor, which):
        factor = factor.reshape(SLICE // WIDTH, 2 * GROUPS)[:, which * GROUPS : (which + 1) * GROUPS]
        return sum(nn(piece, att_in_t) for piece in split(factor, 2)).reshape(SLICE_ROWS, LANES)

    squares = jnp.zeros((1, 1), f32)
    matrix = SQUARE // SLICE
    for slot in range(slots):
        sums[slot] = jnp.zeros((SLICE_ROWS, LANES), f32)

    def take_dense(in_order, slot):
        index = slot * half + chip
        got = got16.at[slot, pl.ds(0, half - 1)]
        pltpu.make_async_copy(got, got, rs_rsem.at[slot]).wait()
        total = flat[index - dense, core] + pair_got[index - dense]
        total = others_sum(total, lambda other: got16[slot, other].astype(f32))
        sums[slot] = total if in_order else whole_rows(total)

    def take_hat():
        hat_s[...] = two_tile * take_wide(0)

    def first(slot):
        sums[slot] = whole_rows(scale_tile * (take_wide(1) - hat_s[...]))

    def add_pos_in(slot):
        at_row = iota((SLICE_ROWS, LANES), 0) == OFF_TAIL % SLICE // LANES
        sums[slot] += jnp.where(at_row, pos_in_row, 0.0)

    def each_slot(low, high, act_on):
        for slot in range(slots):
            when_in(slot, low, high, functools.partial(act_on, slot))

    each_slot(DENSE_FROM * matrix, 5 * matrix, functools.partial(take_dense, False))
    each_slot(0, matrix, lambda slot: take_hat())
    each_slot(0, matrix, first)
    for kind in range(low_kinds):
        kinds = range(2) if low_kinds == 1 else (kind,)

        def fill(kind=kind, kinds=kinds):
            factor = take_low(kind)
            for which in kinds:
                for slot in range(slots):

                    def product(slot=slot, which=which):
                        sums[slot] = low_product(factor, which)

                    when_in(slot, (1 + which) * matrix, (2 + which) * matrix, product)

        if low_kinds == 1:
            fill()
        else:
            when_in(0, (1 + kind) * matrix, (2 + kind) * matrix, fill)
    each_slot(5 * matrix, 2 * sliced, functools.partial(take_dense, True))
    each_slot(OFF_TAIL // SLICE, OFF_TAIL // SLICE + 1, add_pos_in)
    for slot in range(slots):
        squares = squares + lane_sum(row_sum(sums[slot] * sums[slot]))

    collect_norm = all_sum(6, jnp.where(lane == 0, squares, 0.0))

    def each_owner(slot, act_on):
        number = slice_of(slot)
        low = number * SLICE // shard_len
        high = jnp.minimum((number * SLICE + SLICE - 1) // shard_len, n - 1)
        for side in range(sides):
            owner = low + side

            @pl.when((number * SLICE < total_len) & (owner <= high))
            def _(owner=owner, side=side):
                act_on(owner, number - owner * shard_len // SLICE, side)

    def owned_rows(k):
        return owned.at[pl.ds(pl.multiple_of(k * SLICE_ROWS, SLICE_ROWS), SLICE_ROWS)]

    def own_copy(slot, owner, k, side):
        return pltpu.make_async_remote_copy(
            src_ref=sums.at[slot],
            dst_ref=owned_rows(k),
            send_sem=own_ssem.at[slot, side],
            recv_sem=own_rsem.at[k],
            device_id=place(owner),
            device_id_type=MESH,
        )

    for slot in range(slots):

        def hand_over(owner, k, side, slot=slot):
            @pl.when(owner != me)
            def _():
                own_copy(slot, owner, k, side).start()

            @pl.when(owner == me)
            def _():
                owned_rows(k)[...] = sums[slot]

        each_owner(slot, hand_over)

    begin = me * shard_len
    first_slice = begin // SLICE
    last_slice = (begin + shard_len - 1) // SLICE
    for k in range(span):
        number = first_slice + k

        @pl.when((number <= last_slice) & (lax.rem(number, n) != me))
        def _(k=k):
            rows = owned.at[pl.ds(k * SLICE_ROWS, SLICE_ROWS)]
            pltpu.make_async_copy(rows, rows, own_rsem.at[k]).wait()

    offset = begin - first_slice * SLICE
    skip = lax.rem(offset, LANES)
    lanes_all = iota((shard_rows, LANES), 1)
    rows = owned[pl.ds(offset // LANES, shard_rows), :]
    turned = pltpu.roll(rows, lax.rem(LANES - skip, LANES), 1)
    below = pltpu.roll(turned, shard_rows - 1, 0)
    grad = jnp.where(lanes_all < LANES - skip, turned, below)
    inside = iota(grad.shape, 0) * LANES + lanes_all < shard_len
    grad = jnp.where(inside, grad, 0.0)

    stats = collect_norm()
    norm = jnp.sqrt(pick(stats, 0))
    norm_s[...] = jnp.broadcast_to(norm, norm_s.shape)
    grad = grad * jnp.minimum(1.0, clip_norm / norm)

    main = shard_len // 1024 * 1024
    spare = shard_len - main
    tail_g[...] = grad.reshape(shard_rows * LANES)
    for start, size in ((0, main), (main, spare)):
        if size == 0:
            continue
        at = pl.ds(start, size)
        p_new, m_new, s_new = adam(state[0][at], state[1][at], state[2][at], tail_g[at])
        news[0][at] = p_new
        news[1][at] = m_new
        news[2][at] = s_new
        tail_g[at] = p_new
    moved = jnp.where(inside, tail_g[...].reshape(shard_rows, LANES), 0.0)
    turned = pltpu.roll(moved, skip, 1)
    above = pltpu.roll(turned, 1, 0)
    slab_f[...] = jnp.zeros(slab_f.shape, f32)
    slab_f[pl.ds(lax.rem(begin, CHUNK) // LANES, shard_rows), :] = jnp.where(
        lanes_all < skip, above, turned
    )
    shard_w[...] = slab_f[...].astype(bf16)
    all_w[core, chip] = slab_f[...].astype(bf16)

    in_row = n_cols // 2
    row_chip = col_id // 2

    def send_slab(source, slab, row, chip_in_row):
        pltpu.make_async_remote_copy(
            src_ref=source,
            dst_ref=all_w.at[core, slab],
            send_sem=ag_ssem,
            recv_sem=ag_rsem.at[slab],
            device_id=(row, 2 * chip_in_row + core),
            device_id_type=MESH,
        ).start()

    def forward(other):
        pltpu.make_async_remote_copy(
            src_ref=all_w.at[core, other],
            dst_ref=all_w.at[core, other],
            send_sem=fw_ssem,
            recv_sem=fw_rsem,
            device_id=sibling,
            device_id_type=MESH,
        ).start()

    def arrived(other):
        pltpu.make_async_copy(shard_w, shard_w, ag_rsem.at[other]).wait()

    def send_along(k, carry):
        send_slab(shard_w, chip, peer(row_id, k, n_rows), row_chip)
        return carry

    def send_within(k, carry):
        send_slab(shard_w, chip, row_id, peer(row_chip, k, in_row))
        return carry

    loop(1, n_rows, send_along)
    loop(1, in_row, send_within)
    forward(chip)
    store(norm_s, gnorm_h)
    for source, target in ((0, new_master_h), (1, new_first_h), (2, new_second_h)):
        store(news[source], target)

    def spread_row(k, carry):
        other = peer(row_id, n_rows - k, n_rows) * in_row + row_chip
        arrived(other)

        def send_on(i, carry):
            send_slab(all_w.at[core, other], other, row_id, peer(row_chip, i, in_row))
            return carry

        loop(1, in_row, send_on)
        forward(other)
        return carry

    loop(1, n_rows, spread_row)

    def pass_on(k, carry):
        step = k // (in_row - 1)
        row = jnp.where(step == 0, row_id, peer(row_id, n_rows - step, n_rows))
        other = row * in_row + peer(row_chip, in_row - 1 - lax.rem(k, in_row - 1), in_row)
        arrived(other)
        forward(other)
        return carry

    loop(0, n_rows * (in_row - 1), pass_on)
    pltpu.make_async_copy(all_w.at[core], all_w.at[core], fw_rsem).wait()
    rows = CHUNK // LANES

    def chunk(c):
        value = None
        last_owner = min((c * CHUNK + CHUNK - 1) // shard_len, n - 1)
        for owner in range(c * CHUNK // shard_len, last_owner + 1):
            k = c - owner * shard_len // CHUNK
            part = all_w[owner % 2, owner // 2, rows * k : rows * (k + 1)].astype(f32)
            value = part if value is None else value + part
        return value

    whole = total_len // (2 * CHUNK)
    for c in range(whole):
        both = jnp.concatenate([chunk(2 * c), chunk(2 * c + 1)], axis=0)
        weights_out[pl.ds(2 * CHUNK * c, 2 * CHUNK)] = both.astype(bf16).reshape(2 * CHUNK)
    left = total_len - whole * 2 * CHUNK
    if left:
        parts = [chunk(2 * whole)]
        parts.append(chunk(2 * whole + 1) if left > CHUNK else jnp.zeros((rows, LANES), f32))
        both = jnp.concatenate(parts, axis=0).astype(bf16).reshape(2 * CHUNK)
        weights_out[pl.ds(2 * CHUNK * whole, left)] = both[0:left]

    for index, rows in sent:
        drain_stats(index, rows)
    for copy in stores:
        copy.wait()
    pltpu.make_async_copy(all_w.at[core], all_w.at[core], fw_ssem).wait()
    rest = all_w.at[core, pl.ds(0, half - 1)]
    pltpu.make_async_copy(rest, rest, ag_ssem).wait()
    def drain(count, ref, sem):
        def wait_one(k, carry):
            pltpu.make_async_copy(ref, ref, sem).wait()
            return carry

        lax.fori_loop(0, count, wait_one, 0)

    def others(low, high):
        inside = (chip >= low) & (chip < high)
        return high - low - inside.astype(jnp.int32)

    for which in range(2):
        drain(others(0, per_matrix), wide16.at[0, 0], wd_ssem.at[which])
    for kind in range(low_kinds):
        low_at = (1 + kind) * per_matrix % half
        drain(others(low_at, low_at + per_matrix), low_sum.at[0], low_ssem.at[kind])
    for slot in range(slots):
        low_at = max(dense - slot * half, 0)
        high_at = min(sliced - slot * half, half)
        if high_at > low_at:
            drain(others(low_at, high_at), part16.at[0], rs_ssem.at[slot])

        def own_drain(owner, k, side, slot=slot):
            @pl.when(owner != me)
            def _():
                own_copy(slot, owner, k, side).wait_send()

        each_owner(slot, own_drain)


def finish_kernel(
    out_t, gfeat_t, gnorm_t, master_t, first_t, second_t, weights_t,
    out_h, gfeat_h, gnorm, master_h, first_h, second_h, weights_h,
    norm_s, sem,
):
    copies = [
        pltpu.make_async_copy(source, target, sem.at[k])
        for k, (source, target) in enumerate(
            (
                (weights_t, weights_h),
                (out_t, out_h),
                (gfeat_t, gfeat_h),
                (master_t, master_h),
                (first_t, first_h),
                (second_t, second_h),
                (gnorm_t, norm_s),
            )
        )
    ]
    for copy in copies:
        copy.start()
    copies[-1].wait()
    gnorm[...] = norm_s[0:1, 0:1]
    for copy in copies[:-1]:
        copy.wait()


def lane_slots(value):
    return functools.reduce(
        jnp.add, [value[:, j * LANES : (j + 1) * LANES] for j in range(NEAREST)]
    )


def shards(
    n_rows, n_cols,
    features, coords, valid_mask, neighbors, cotangent, weights, master, first_moment, second_moment,
):
    n = n_rows * n_cols
    half = n // 2
    points = features.shape[0]
    blocks = points // LANES
    shard_len = master.shape[0]
    total_len = weights.shape[0]

    def up(value, unit):
        return -(-value // unit) * unit

    shard_rows = up(-(-shard_len // LANES) + 1, 8)
    slab_rows = up(shard_rows + CHUNK // LANES, 16)
    sliced = up(-(-total_len // SLICE), 2) // 2
    slots = -(-sliced // half)
    per_matrix = SQUARE // SLICE // 2
    dense_pairs = sliced - DENSE_FROM * per_matrix
    low_kinds = 1 if per_matrix % half == 0 else 2
    sides = (SLICE + shard_len - 2) // shard_len + 1
    span = (SLICE + shard_len - 2) // SLICE + 1
    hbm = pl.BlockSpec(memory_space=pltpu.HBM)
    vmem = pl.BlockSpec(memory_space=pltpu.VMEM)
    dma = pltpu.SemaphoreType.DMA
    shape = jax.ShapeDtypeStruct

    def pairs(rows, dtype=f32):
        return pltpu.VMEM((blocks, rows, PAIRS), dtype)

    def shard():
        return [pltpu.VMEM(master.shape, f32) for _ in range(3)]

    scratch = [
        pltpu.VMEM(features.shape, bf16),
        pltpu.VMEM(coords.shape, f32),
        pltpu.VMEM(valid_mask.shape, jnp.int32),
        pltpu.VMEM(neighbors.shape, jnp.int32),
        pltpu.VMEM(features.shape, bf16),
        pltpu.VMEM((SQUARE,), bf16),
        pltpu.VMEM((1024,), bf16),
        pltpu.VMEM(weights.shape, bf16),
        shard(),
        shard(),
        pltpu.VMEM((2, *features.shape), bf16),
        pltpu.VMEM((1, LANES), f32),
        dma((11,)),
        dma((7,)),
        pltpu.VMEM((7, 8, LANES), f32),
        pltpu.VMEM((7, n, 8, LANES), f32),
        dma((7,)),
        dma((7,)),
        pltpu.VMEM((TAIL_PAD,), bf16),
        pltpu.VMEM((9, WIDTH, WIDTH), bf16),
        pairs(WINDOW, bf16),
        pairs(WIDTH),
        pairs(GROUPS),
        pairs(GROUPS),
        pairs(GROUPS, bf16),
        pairs(GROUPS),
        pairs(8),
        pairs(8),
        pairs(8),
        pairs(8),
        pairs(8),
        pairs(8),
        pltpu.VMEM((WIDTH, points), bf16),
        pltpu.VMEM((points, WIDTH), f32),
        pairs(8),
        pltpu.VMEM((points, WIDTH), f32),
        pltpu.VMEM((points, WIDTH), f32),
        pltpu.VMEM((points, WIDTH), bf16),
        pltpu.VMEM((WIDTH, points), bf16),
        pltpu.VMEM((WIDTH, points), bf16),
        pltpu.VMEM((WIDTH, points), bf16),
        pltpu.VMEM((6 * GROUPS, WIDTH), bf16),
        pltpu.VMEM((points, WIDTH), bf16),
        pltpu.VMEM((WIDTH, points), bf16),
        pltpu.VMEM((WIDTH, points), f32),
        pltpu.VMEM((points, WIDTH), f32),
        pltpu.VMEM((points, GROUPS), f32),
        pltpu.VMEM((3 * GROUPS, points), f32),
        pltpu.VMEM((3 * GROUPS, points), f32),
        pairs(GROUPS, bf16),
        pairs(GROUPS, bf16),
        pairs(WIDTH, bf16),
        pltpu.VMEM((points, WIDTH), f32),
        pltpu.VMEM((points, WIDTH), bf16),
        pltpu.VMEM((WIDTH, LANES), f32),
        pltpu.VMEM((dense_pairs, 2, SLICE_ROWS, LANES), f32),
        pltpu.VMEM((dense_pairs, SLICE_ROWS, LANES), f32),
        pltpu.VMEM((dense_pairs, SLICE_ROWS, LANES), bf16),
        pltpu.VMEM((slots, half, SLICE_ROWS, LANES), bf16),
        pltpu.VMEM((2, per_matrix, 2, SLICE_ROWS, LANES), f32),
        pltpu.VMEM((2, per_matrix, SLICE_ROWS, LANES), f32),
        pltpu.VMEM((2, per_matrix, 2, SLICE_ROWS, LANES), bf16),
        pltpu.VMEM((2, half, 2, SLICE_ROWS, LANES), bf16),
        pltpu.VMEM((per_matrix, 2, LOW_ROWS, LANES), f32),
        pltpu.VMEM((per_matrix, LOW_ROWS, LANES), f32),
        pltpu.VMEM((per_matrix, LOW_ROWS, LANES), f32),
        pltpu.VMEM((low_kinds, half, LOW_ROWS, LANES), f32),
        pltpu.VMEM((SLICE_ROWS, LANES), f32),
        pltpu.VMEM((slots, SLICE_ROWS, LANES), f32),
        pltpu.VMEM((up(max(span * SLICE_ROWS, SLICE_ROWS + shard_rows), SLICE_ROWS), LANES), f32),
        pltpu.VMEM((shard_rows * LANES,), f32),
        pltpu.VMEM((slab_rows, LANES), f32),
        pltpu.VMEM((slab_rows, LANES), bf16),
        pltpu.VMEM((2, half, slab_rows, LANES), bf16),
        dma((6,)),
        dma((6,)),
        dma((slots,)),
        dma((slots,)),
        dma((2,)),
        dma((2,)),
        dma((low_kinds,)),
        dma((low_kinds,)),
        dma((slots, sides)),
        dma((span,)),
        dma,
        dma((half,)),
        dma,
        dma,
    ]
    results = pl.pallas_call(
        functools.partial(block_kernel, n_rows, n_cols),
        out_shape=(
            shape(features.shape, bf16),
            shape(features.shape, bf16),
            shape((1, LANES), f32),
            shape(master.shape, f32),
            shape(master.shape, f32),
            shape(master.shape, f32),
            pltpu.VMEM(weights.shape, bf16),
        ),
        in_specs=[hbm] * 9,
        out_specs=[pl.BlockSpec(memory_space=pl.ANY)] * 6 + [vmem],
        scratch_shapes=scratch,
        compiler_params=pltpu.CompilerParams(
            collective_id=0, has_side_effects=True, vmem_limit_bytes=48 * 2**20
        ),
    )(*(pltpu.with_memory_space_constraint(x, pltpu.HBM) for x in (features, coords, valid_mask, neighbors, cotangent, weights, master, first_moment, second_moment)))
    results = pl.pallas_call(
        finish_kernel,
        out_shape=(
            shape(features.shape, bf16),
            shape(features.shape, bf16),
            shape((1, 1), f32),
            shape(master.shape, f32),
            shape(master.shape, f32),
            shape(master.shape, f32),
            shape(weights.shape, bf16),
        ),
        in_specs=[pl.BlockSpec(memory_space=pl.ANY)] * 7,
        out_specs=[hbm, hbm, vmem, hbm, hbm, hbm, hbm],
        scratch_shapes=[pltpu.VMEM((1, LANES), f32), dma((7,))],
        compiler_params=pltpu.CompilerParams(vmem_limit_bytes=8 * 2**20),
    )(*results)
    return results[0], results[1], results[2].reshape(()), *results[3:]


def solution(mesh):
    both = ("rows", "cols")
    rows_split, cols_split, flat_split = P(both, None), P(None, both), P(both)
    return jax.shard_map(
        functools.partial(shards, mesh.shape["rows"], mesh.shape["cols"]),
        mesh=mesh,
        in_specs=(
            rows_split, cols_split, flat_split, cols_split, rows_split, P(),
            flat_split, flat_split, flat_split,
        ),
        out_specs=(rows_split, rows_split, P(), flat_split, flat_split, flat_split, P()),
        check_vma=False,
    )
```

```python
import functools

import jax
import jax.numpy as jnp
from jax import lax
from jax.experimental import pallas as pl
from jax.experimental.pallas import tpu as pltpu
from jax.sharding import PartitionSpec as P

WIDTH = 256
GROUPS = 32
NEAREST = 16
PER_GROUP = WIDTH // GROUPS
LANES = 128
WINDOW = 256
PAIRS = NEAREST * LANES

SQUARE = WIDTH * WIDTH
OFF_ATT_IN = 5 * SQUARE
OFF_ATT_OUT = OFF_ATT_IN + WIDTH * GROUPS
OFF_TAIL = OFF_ATT_OUT + GROUPS * GROUPS
NORMS = 2 * WIDTH + 3 + GROUPS
TAIL_POS_OUT = 9
TAIL_GAINS = TAIL_POS_OUT + 3 * WIDTH
TAIL_SHIFTS = TAIL_GAINS + NORMS
TAIL_USED = TAIL_SHIFTS + NORMS
TAIL_PAD = 2048
SLICE = 2048
SLICE_ROWS = SLICE // LANES
LOW_ROWS = SLICE // WIDTH * 2 * GROUPS // LANES
DENSE_FROM = 3
CHUNK = 1024
POS_ROWS = 32

bn_eps = 1e-05
clip_norm = 0.01
learn_rate = 0.05
beta_one = 0.9
beta_two = 0.999
adam_eps = 1e-08
decay_rate = 0.01
step_count = 10
masked_logit = -1000000000.0

f32 = jnp.float32
bf16 = jnp.bfloat16
MESH = pl.DeviceIdType.MESH


def contract(a, b, left, right):
    return lax.dot_general(a, b, (((left,), (right,)), ((), ())), preferred_element_type=f32)


def nn(a, b):
    return contract(a, b, 1, 0)


def nt(a, b):
    return contract(a, b, 1, 1)


def tn(a, b):
    return contract(a, b, 0, 0)


def split(value, parts):
    pieces = []
    for _ in range(parts):
        piece = value.astype(bf16)
        pieces.append(piece)
        value = value - piece.astype(f32)
    return pieces


def silu_parts(value):
    gate = 0.5 * jnp.tanh(0.5 * value) + 0.5
    return value * gate, gate


def silu_slope(value, gate):
    return gate * (1.0 + value * (1.0 - gate))


def iota(shape, dim):
    return lax.broadcasted_iota(jnp.int32, shape, dim)


def loop(begin, end, body):
    if end - begin <= 31:
        for k in range(begin, end):
            body(k, 0)
    else:
        lax.fori_loop(begin, end, body, 0)


def row_to_col(row, count):
    wide = jnp.broadcast_to(row, (count, row.shape[1]))
    same = iota(wide.shape, 0) == iota(wide.shape, 1)
    return jnp.sum(jnp.where(same, wide, 0.0), axis=1, keepdims=True)


def col_to_row(col, offset):
    wide = jnp.broadcast_to(col, (col.shape[0], LANES))
    same = iota(wide.shape, 0) + offset == iota(wide.shape, 1)
    return jnp.sum(jnp.where(same, wide, 0.0), axis=0, keepdims=True)


def row_sum(value):
    return jnp.sum(value, axis=0, keepdims=True)


def lane_fold(value):
    total = value[:, 0:LANES]
    for k in range(1, value.shape[1] // LANES):
        total = total + value[:, k * LANES : (k + 1) * LANES]
    return total


def lane_sum(value):
    return jnp.sum(lane_fold(value), axis=1, keepdims=True)


def tiles(value):
    return jnp.concatenate([value] * NEAREST, axis=1)


def adam(param, moment, second, grad):
    moment_new = beta_one * moment + (1.0 - beta_one) * grad
    second_new = beta_two * second + (1.0 - beta_two) * grad * grad
    moment_hat = moment_new / (1.0 - beta_one**step_count)
    second_hat = second_new / (1.0 - beta_two**step_count)
    param_new = param - learn_rate * (
        moment_hat / (jnp.sqrt(second_hat) + adam_eps) + decay_rate * param
    )
    return param_new, moment_new, second_new


def peer(me, step, count):
    if count & (count - 1) == 0:
        return me ^ (count - step)
    return lax.rem(me + step, count)


def block_kernel(
    n_rows, n_cols,
    feat_h, coords_h, valid_h, nbrs_h, cot_h, weights_h, master_h, first_h, second_h,
    out_h, gfeat_h, gnorm_h, new_master_h, new_first_h, new_second_h, weights_out,
    feat, coords, valid, nbrs, cot, w_first, pos_first, weights, state, news, outs, norm_s, in_sem, out_sem,
    stat_send, stat_buf, stat_ssem, stat_rsem,
    tail1d, mats, onehot, vgat, att, wpre, uact, dyw, rel, pos, act, pmask, allow, dmix,
    ft_s, slope_a, slope_p, a1_s, z_s, h_s, h_ts, q_s, k_s, ba_s, o_s, o_ts, do_s, dv_s, sk_s, bd_s, ds_s, dw_s, xs, dz_s, dz16,
    mu_s, flat, pair_got, part16, got16, first_f, first_got, wide16, got_wide, low_f, low_got, low_sum, got_low, hat_s, sums, owned, tail_g, slab_f, shard_w, all_w,
    pair_ssem, pair_rsem, rs_ssem, rs_rsem, wd_ssem, wd_rsem, low_ssem, low_rsem, own_ssem, own_rsem, ag_ssem, ag_rsem, fw_ssem, fw_rsem,
):
    n = n_rows * n_cols
    half = n // 2
    row_id, col_id = lax.axis_index("rows"), lax.axis_index("cols")
    me = row_id * n_cols + col_id
    core = lax.rem(col_id, 2)
    chip = me // 2
    points = feat.shape[0]
    blocks = points // LANES
    starts = [min(max(LANES * b - (WINDOW - LANES) // 2, 0), points - WINDOW) for b in range(blocks)]
    total_len = weights.shape[0]
    shard_len = master_h.shape[0]
    shard_rows = -(-tail_g.shape[0] // LANES)
    per_matrix = SQUARE // SLICE // 2
    dense = DENSE_FROM * per_matrix
    sliced = dense + flat.shape[0]
    slots = got16.shape[0]
    low_kinds = got_low.shape[0]
    sides = own_ssem.shape[1]
    span = own_rsem.shape[0]

    def place(device):
        return (device // n_cols, lax.rem(device, n_cols))

    barrier = pltpu.get_barrier_semaphore()

    def greet(k, carry):
        pl.semaphore_signal(barrier, inc=1, device_id=place(peer(me, k, n)), device_id_type=MESH)
        return carry

    loop(1, n, greet)
    loads = []

    def load(source, target):
        copy = pltpu.make_async_copy(source, target, in_sem.at[len(loads)])
        copy.start()
        loads.append(copy)
        return copy

    stores = []

    def store(source, target):
        copy = pltpu.make_async_copy(source, target, out_sem.at[len(stores)])
        copy.start()
        stores.append(copy)

    early = [
        load(feat_h, feat),
        load(weights_h.at[pl.ds(0, SQUARE)], w_first),
        load(weights_h.at[pl.ds(OFF_TAIL, 1024)], pos_first),
        load(nbrs_h, nbrs),
        load(coords_h, coords),
        load(valid_h, valid),
    ]

    late = [load(weights_h, weights), load(cot_h, cot)]
    for source, target in ((master_h, 0), (first_h, 1), (second_h, 2)):
        late.append(load(source, state[target]))
    owned[...] = jnp.zeros(owned.shape, f32)
    for copy in early:
        copy.wait()

    sent = []

    def all_sum(index, message):
        rows = message.shape[0]
        stat_send[index, 0:rows] = message
        stat_buf[index, me, 0:rows] = message

        def post(k, carry):
            pltpu.make_async_remote_copy(
                src_ref=stat_send.at[index, pl.ds(0, rows)],
                dst_ref=stat_buf.at[index, me, pl.ds(0, rows)],
                send_sem=stat_ssem.at[index],
                recv_sem=stat_rsem.at[index],
                device_id=place(peer(me, k, n)),
                device_id_type=MESH,
            ).start()
            return carry

        loop(1, n, post)
        sent.append((index, rows))

        def collect():
            span = stat_buf.at[index, pl.ds(0, n - 1), pl.ds(0, rows)]
            pltpu.make_async_copy(span, span, stat_rsem.at[index]).wait()
            return jnp.sum(stat_buf[index, :, 0:rows], axis=0)

        return collect

    sibling = (row_id, col_id + 1 - 2 * core)
    def put_halves(target, value):
        rows = SLICE_ROWS // 2
        for k in range(2):
            part = value[:, k * LANES : (k + 1) * LANES]
            target[:, :, k * rows : (k + 1) * rows] = part.reshape(per_matrix, 2, rows, LANES)

    def whole_rows(piece):
        rows = SLICE_ROWS // 2
        return jnp.concatenate([piece[0:rows], piece[rows:]], axis=1).reshape(SLICE_ROWS, LANES)

    def put_matrix(m, grad):
        at = (m - DENSE_FROM) * per_matrix
        put_halves(flat.at[at : at + per_matrix], grad)

    def swap(group, source, target):
        copy = pltpu.make_async_remote_copy(
            src_ref=source.at[:, 1 - core],
            dst_ref=target,
            send_sem=pair_ssem.at[group],
            recv_sem=pair_rsem.at[group],
            device_id=sibling,
            device_id_type=MESH,
        )
        copy.start()
        return copy

    def to_chips(begin, count, send):
        if count == half and begin % half == 0:

            def post(k, carry):
                other = peer(chip, k, half)
                send(begin + other, other)
                return carry

            loop(1, half, post)
        else:

            def post_any(k, carry):
                index = begin + k
                other = lax.rem(index, half)

                @pl.when(other != chip)
                def _():
                    send(index, other)

                return carry

            loop(0, count, post_any)

    def send_dense(copy, begin, count):
        copy.wait()
        own = pl.ds(begin - dense, count)
        part16[own] = (flat[own, core] + pair_got[own]).astype(bf16)

        def send(index, other):
            pltpu.make_async_remote_copy(
                src_ref=part16.at[index - dense],
                dst_ref=got16.at[index // half, chip],
                send_sem=rs_ssem.at[index // half],
                recv_sem=rs_rsem.at[index // half],
                device_id=place(2 * other + core),
                device_id_type=MESH,
            ).start()

        at = begin
        while at < begin + count:
            step = min(half - at % half, begin + count - at)
            to_chips(at, step, send)
            at = at + step

    def send_wide(copy, which):
        copy.wait()
        for k, piece in enumerate(split(first_f[which, :, core] + first_got[which], 2)):
            wide16[which, :, k] = piece

        def send(index, other):
            pltpu.make_async_remote_copy(
                src_ref=wide16.at[which, index],
                dst_ref=got_wide.at[which, chip],
                send_sem=wd_ssem.at[which],
                recv_sem=wd_rsem.at[which],
                device_id=place(2 * other + core),
                device_id_type=MESH,
            ).start()

        to_chips(0, per_matrix, send)

    def send_low(copy):
        copy.wait()
        low_sum[...] = low_f[:, core] + low_got[...]
        for kind in range(low_kinds):

            def send(index, other, kind=kind):
                pltpu.make_async_remote_copy(
                    src_ref=low_sum.at[index - (1 + kind) * per_matrix],
                    dst_ref=got_low.at[kind, chip],
                    send_sem=low_ssem.at[kind],
                    recv_sem=low_rsem.at[kind],
                    device_id=place(2 * other + core),
                    device_id_type=MESH,
                ).start()

            to_chips((1 + kind) * per_matrix, per_matrix, send)

    def drain_stats(index, rows):
        span = stat_buf.at[index, pl.ds(0, n - 1), pl.ds(0, rows)]
        pltpu.make_async_copy(span, span, stat_ssem.at[index]).wait()

    w_in = w_first[...].reshape(WIDTH, WIDTH)
    mats[0] = w_in
    w_in = mats[0]
    pos_in = pos_first[...].reshape(1024 // LANES, LANES)[0:1].astype(f32)
    lane8 = iota((8, 1), 0)

    def pos_in_col(c):
        return jnp.where(lane8 < 3, row_to_col(pos_in[:, 3 * c : 3 * c + 8], 8), 0.0)

    valid_rows = valid[...].reshape(points // LANES, LANES).astype(f32)
    n_valid = jnp.sum(jnp.sum(valid_rows, axis=0, keepdims=True), axis=1, keepdims=True)
    point_mask = (iota((points, 1), 0).astype(f32) < n_valid).astype(f32)
    lane_mask = (iota((1, points), 1).astype(f32) < n_valid).astype(f32)

    a1 = nn(feat[...], w_in)
    a1_s[...] = a1
    masked = point_mask * a1
    sum_a, sqr_a = row_sum(masked), row_sum(masked * a1)

    weight = [[pos_in[:, 3 * c + d : 3 * c + d + 1] for d in range(3)] for c in range(3)]
    pos_one = [jnp.zeros((NEAREST, LANES), f32) for _ in range(3)]
    pos_two = [jnp.zeros((NEAREST, LANES), f32) for _ in range(3)]
    pairs_local = jnp.zeros((NEAREST, LANES), f32)
    for b in range(blocks):
        here = slice(b * LANES, (b + 1) * LANES)
        index = nbrs[:, here]
        tile, at = lax.shift_right_logical(index, 7), index & (LANES - 1)

        def fetch(c, t):
            row = jnp.broadcast_to(coords[c : c + 1, t * LANES : (t + 1) * LANES], index.shape)
            return jnp.take_along_axis(row, at, axis=1, mode="promise_in_bounds")

        r = []
        for c in range(3):
            near = fetch(c, b)
            if b > 0:
                near = jnp.where(tile < b, fetch(c, b - 1), near)
            if b < blocks - 1:
                near = jnp.where(tile > b, fetch(c, b + 1), near)
            r.append(near - coords[c : c + 1, here])
        pm = jnp.where(index.astype(f32) < n_valid, lane_mask[:, here], 0.0)
        pairs_local = pairs_local + pm
        for d in range(3):
            p = weight[0][d] * r[0] + weight[1][d] * r[1] + weight[2][d] * r[2]
            pos_one[d] = pos_one[d] + pm * p
            pos_two[d] = pos_two[d] + pm * p * p

    def total(value):
        return jnp.sum(row_sum(value), axis=1, keepdims=True)

    lane = iota((1, LANES), 1)
    last = jnp.where(lane == 16, n_valid, 0.0) + jnp.where(lane == 17, total(pairs_local), 0.0)
    for d in range(3):
        last = last + jnp.where(lane == d, total(pos_one[d]), 0.0)
        last = last + jnp.where(lane == 8 + d, total(pos_two[d]), 0.0)

    def fold(row):
        return jnp.concatenate([row[:, 0:LANES], row[:, LANES:WIDTH]], axis=0)

    def unfold(rows):
        return jnp.concatenate([rows[0:1], rows[1:2]], axis=1)

    pl.semaphore_wait(barrier, n - 1)
    collect_first = all_sum(0, jnp.concatenate([fold(sum_a), fold(sqr_a), last], axis=0))
    window_row = iota((WINDOW, LANES), 0)
    for b in range(blocks):
        for j in range(NEAREST):
            index = nbrs[j : j + 1, b * LANES : (b + 1) * LANES] - starts[b]
            onehot[b, 0:WINDOW, j * LANES : (j + 1) * LANES] = jnp.where(
                window_row == index, 1.0, 0.0
            ).astype(bf16)

    coords8 = jnp.concatenate([coords[...], jnp.zeros((5, points), f32)], axis=0)
    table = jnp.concatenate(
        split(coords8, 3) + [jnp.broadcast_to(lane_mask, (8, points)).astype(bf16)], axis=0
    )
    slot0 = (iota((1, PAIRS), 1) < LANES).astype(f32)
    pos_in_cols = [pos_in_col(c) for c in range(3)]
    for b in range(blocks):
        here = slice(b * LANES, (b + 1) * LANES)
        fetched = nn(table[:, starts[b] : starts[b] + WINDOW], onehot[b, 0:WINDOW])
        place_n = fetched[0:8] + fetched[8:16] + fetched[16:24]
        mask_n = fetched[24:32]
        r = place_n - tiles(coords8[:, here])
        pm = mask_n * tiles(lane_mask[:, here])
        p = pos_in_cols[0] * r[0:1] + pos_in_cols[1] * r[1:2] + pos_in_cols[2] * r[2:3]
        rel[b] = r
        pos[b] = p
        pmask[b] = pm
        allow[b] = jnp.maximum(mask_n, slot0)

    for copy in late:
        copy.wait()
    for m in range(1, 5):
        mats[m] = weights[pl.ds(m * SQUARE, SQUARE)].reshape(WIDTH, WIDTH)
    w_q, w_k, w_v, w_o = (mats[m] for m in range(1, 5))
    att_in = weights[pl.ds(OFF_ATT_IN, WIDTH * GROUPS)].reshape(WIDTH * GROUPS // LANES, LANES)
    att_in_f = att_in.astype(f32).reshape(WIDTH, GROUPS)
    att_in_t = att_in_f.T.astype(bf16)
    att_out_f = (
        weights[pl.ds(OFF_ATT_OUT, GROUPS * GROUPS)]
        .reshape(GROUPS * GROUPS // LANES, LANES)
        .astype(f32)
        .reshape(GROUPS, GROUPS)
    )
    att_out = att_out_f.astype(bf16)
    att_out_t = att_out_f.T.astype(bf16)
    tail1d[pl.ds(0, 1024)] = weights[pl.ds(OFF_TAIL, 1024)]
    rest = total_len - OFF_TAIL - 1024
    tail1d[pl.ds(1024, rest)] = weights[pl.ds(OFF_TAIL + 1024, rest)]
    tail = tail1d[pl.ds(0, TAIL_PAD)].reshape(TAIL_PAD // LANES, LANES).astype(f32)
    tail = jnp.concatenate([tail[k : k + 1] for k in range(TAIL_PAD // LANES)], axis=1)
    pos_rows = [tail[:, TAIL_POS_OUT + WIDTH * d : TAIL_POS_OUT + WIDTH * (d + 1)] for d in range(3)]
    def norm_pieces(start):
        ends = [0, WIDTH, WIDTH + 3, WIDTH + 3 + GROUPS, NORMS]
        return [tail[:, start + ends[k] : start + ends[k + 1]] for k in range(4)]

    gain_a, gain_p, gain_w, gain_o = norm_pieces(TAIL_GAINS)
    shift_a, shift_p, shift_w, shift_o = norm_pieces(TAIL_SHIFTS)

    def pad_col(row):
        wide = jnp.concatenate([row, jnp.zeros((1, 5), f32)], axis=1)
        return row_to_col(wide, 8)

    gain_p, shift_p = pad_col(gain_p), pad_col(shift_p)
    gain_w, shift_w = row_to_col(gain_w, GROUPS), row_to_col(shift_w, GROUPS)

    new_at = iota((WIDTH, WIDTH), 0)
    reorder = jnp.where(
        iota((WIDTH, WIDTH), 1) == new_at % GROUPS * PER_GROUP + new_at // GROUPS, 1.0, 0.0
    ).astype(bf16)
    w_o_new = nn(reorder, w_o)
    mats[4] = w_o_new.astype(bf16)
    mats[5] = w_o_new.T.astype(bf16)
    mats[6] = w_q.astype(f32).T.astype(bf16)
    mats[7] = w_k.astype(f32).T.astype(bf16)
    mats[8] = nt(reorder, w_v).astype(bf16)
    pos_mat = jnp.concatenate(pos_rows + [jnp.zeros((13, WIDTH), f32)], axis=0).astype(bf16)
    pos_cols = nt(reorder, pos_mat)
    pos_lanes = jnp.concatenate(
        [pos_cols[:, 0:8]] * 3 + [jnp.zeros((WIDTH, POS_ROWS - 24), f32)], axis=1
    ).astype(bf16)
    pos_cols = [pos_cols[:, d : d + 1] for d in range(3)]
    feat_f = feat[...].astype(f32)
    ft_s[...] = feat_f.T.astype(bf16)
    sum_f = row_sum(point_mask * feat_f)
    stats = collect_first()

    def pick(row, at):
        return jnp.sum(jnp.where(lane == at, row, 0.0), axis=1, keepdims=True)

    point_count, pair_count = pick(stats[4:5], 16), pick(stats[4:5], 17)
    inv_points, inv_pairs = 1.0 / point_count, 1.0 / pair_count

    def moments(total, square, inv):
        mean = total * inv
        return mean, lax.rsqrt(square * inv - mean * mean + bn_eps)

    mean_a, rs_a = moments(unfold(stats[0:2]), unfold(stats[2:4]), inv_points)
    mean_p, rs_p = moments(
        row_to_col(stats[4:5, 0:8], 8), row_to_col(stats[4:5, 8:16], 8), inv_pairs
    )

    h = silu_parts((a1_s[...] - mean_a) * rs_a * gain_a + shift_a)[0]
    h_s[...] = h.astype(bf16)
    h_t = h.T.astype(bf16)
    q_t = nn(mats[6], h_t).astype(bf16)
    k_t = nn(mats[7], h_t).astype(bf16)
    q_s[...] = q_t
    k_s[...] = k_t
    h_ts[...] = h_t
    q_att = nn(att_in_t, q_t)
    k_att = jnp.concatenate(split(nn(att_in_t, k_t), 3), axis=0)
    pos_att = nt(att_in_t, pos_mat)
    none = jnp.zeros((GROUPS, 8), f32)
    pos_ext = [piece.astype(f32) for piece in split(-pos_att[:, 0:8], 3)]
    pos_ext = jnp.concatenate(
        [
            jnp.concatenate([pos_ext[k]] * (3 - k) + [none] * (k + 1), axis=1) for k in range(3)
        ],
        axis=0,
    ).astype(bf16)
    back_att = jnp.concatenate([nn(att_in_t, mats[6]), nn(att_in_t, mats[7])], axis=0)
    back_split = split(back_att, 2)
    ba_s[...] = jnp.concatenate([back_split[0], back_split[0], back_split[1]], axis=0)

    sum_w = jnp.zeros((GROUPS, LANES), f32)
    sqr_w = jnp.zeros((GROUPS, LANES), f32)
    for b in range(blocks):
        here = slice(b * LANES, (b + 1) * LANES)
        active = silu_parts((pos[b] - mean_p) * rs_p * gain_p + shift_p)[0]
        act[b] = active
        pieces = [piece.astype(f32) for piece in split(active, 3)]
        onehot[b, WINDOW : WINDOW + POS_ROWS] = jnp.concatenate(
            pieces + [jnp.zeros((POS_ROWS - 24, PAIRS), f32)], axis=0
        ).astype(bf16)
        fetched = nn(
            jnp.concatenate([k_att[:, starts[b] : starts[b] + WINDOW], pos_ext], axis=1), onehot[b]
        )
        w = tiles(q_att[:, here]) - (
            fetched[0:GROUPS] + fetched[GROUPS : 2 * GROUPS] + fetched[2 * GROUPS : 3 * GROUPS]
        )
        wpre[b] = w
        mw = w * pmask[b, 0:1]
        sum_w = sum_w + lane_fold(mw)
        sqr_w = sqr_w + lane_fold(mw * w)

    def pair_row(one, two):
        one = jnp.sum(one, axis=1, keepdims=True)
        two = jnp.sum(two, axis=1, keepdims=True)
        return col_to_row(one, 0) + col_to_row(two, GROUPS)

    collect_w = all_sum(1, jnp.concatenate([pair_row(sum_w, sqr_w), fold(sum_f)], axis=0))
    v_t = nn(mats[8], h_ts[...]).astype(bf16)
    for b in range(blocks):
        vgat[b] = nn(
            jnp.concatenate([v_t[:, starts[b] : starts[b] + WINDOW], pos_lanes], axis=1), onehot[b]
        )
    stats = collect_w()
    mean_f = stats[1:3] * inv_points
    mean_w, rs_w = moments(
        row_to_col(stats[0:1, 0:GROUPS], GROUPS),
        row_to_col(stats[0:1, GROUPS : 2 * GROUPS], GROUPS),
        inv_pairs,
    )

    def each_channel(value):
        return jnp.concatenate([value] * PER_GROUP, axis=0)

    def over_channels(value):
        return functools.reduce(
            jnp.add, [value[c * GROUPS : (c + 1) * GROUPS] for c in range(PER_GROUP)]
        )

    def cols(j):
        return slice(j * LANES, (j + 1) * LANES)

    for b in range(blocks):
        here = slice(b * LANES, (b + 1) * LANES)
        u = silu_parts((wpre[b] - mean_w) * rs_w * gain_w + shift_w)[0].astype(bf16)
        uact[b] = u
        logit = jnp.where(allow[b, 0:1] > 0.5, nn(att_out_t, u), masked_logit)
        top = logit[:, cols(0)]
        for j in range(1, NEAREST):
            top = jnp.maximum(top, logit[:, cols(j)])
        weight = jnp.exp(logit - tiles(top))
        share = 1.0 / functools.reduce(jnp.add, [weight[:, cols(j)] for j in range(NEAREST)])
        att[b] = weight * tiles(share)
        mixed = jnp.zeros((WIDTH, LANES), f32)
        for j in range(NEAREST):
            mixed = mixed + each_channel(att[b, :, cols(j)]) * vgat[b, :, cols(j)]
        o_s[here, :] = mixed.T.astype(bf16)

    z = nn(o_s[...], mats[4])
    z_s[...] = z
    masked = point_mask * z
    collect_o = all_sum(2, jnp.concatenate([fold(row_sum(masked)), fold(row_sum(masked * z))], axis=0))
    for k in range(2):
        mu_s[k * LANES : (k + 1) * LANES] = jnp.broadcast_to(
            row_to_col(mean_f[k : k + 1], LANES), (LANES, LANES)
        )

    def put_first(which, value):
        put_halves(first_f.at[which], value)
        return swap(which, first_f.at[which], first_got.at[which])

    def from_feat(value):
        return nn(
            jnp.concatenate([ft_s[...]] * 2, axis=1), jnp.concatenate(split(value, 2), axis=0)
        )

    ahat = (a1_s[...] - mean_a) * rs_a
    a1_s[...] = ahat
    ahat_pair = put_first(0, from_feat(point_mask * ahat))
    for b in range(blocks):
        what = (wpre[b] - mean_w) * rs_w
        wpre[b] = what
        y = what * gain_w + shift_w
        dyw[b] = silu_slope(y, silu_parts(y)[1])
    send_wide(ahat_pair, 0)
    o_ts[...] = nn(o_s[...], reorder).T.astype(bf16)
    for b in range(blocks):
        here = slice(b * LANES, (b + 1) * LANES)
        enc = [jnp.zeros((GROUPS, LANES), f32) for _ in range(3)]
        for j in range(NEAREST):
            a = att[b, :, cols(j)]
            for d in range(3):
                enc[d] = enc[d] + a * act[b, d : d + 1, cols(j)]
        bd_s[:, here] = jnp.concatenate(enc, axis=0)
    stats = collect_o()
    mean_o, rs_o = moments(unfold(stats[0:2]), unfold(stats[2:4]), inv_points)

    zhat = (z_s[...] - mean_o) * rs_o
    z_s[...] = zhat
    y = feat[...].astype(f32) + zhat * gain_o + shift_o
    value, gate = silu_parts(y)
    outs[0] = (point_mask * value).astype(bf16)
    store(outs.at[0], out_h)
    dy = point_mask * cot[...].astype(f32) * silu_slope(y, gate)
    dz_s[...] = dy
    shift_grad_o, gain_grad_o = row_sum(dy), row_sum(dy * zhat)
    collect_o = all_sum(3, jnp.concatenate([fold(shift_grad_o), fold(gain_grad_o)], axis=0))
    for b in range(blocks):
        phat = (pos[b] - mean_p) * rs_p
        pos[b] = phat
        y = phat * gain_p + shift_p
        slope_p[b] = silu_slope(y, silu_parts(y)[1])
    y = a1_s[...] * gain_a + shift_a
    slope_a[...] = silu_slope(y, silu_parts(y)[1])
    pos_row = jnp.zeros((1, LANES), f32)
    for c in range(3):
        with_hat, alone = jnp.zeros((8, 1), f32), jnp.zeros((8, 1), f32)
        for b in range(blocks):
            masked = pmask[b] * rel[b, c : c + 1]
            with_hat = with_hat + lane_sum(masked * pos[b])
            alone = alone + lane_sum(masked)
        pos_row = pos_row + col_to_row(with_hat, 64 + 8 * c) + col_to_row(alone, 88 + 8 * c)
    stats = collect_o()
    one, two = unfold(stats[0:2]) * inv_points, unfold(stats[2:4]) * inv_points
    dz = (gain_o * rs_o * (dz_s[...] - point_mask * (one + z_s[...] * two))).astype(bf16)
    dz16[...] = dz
    do_s[...] = nn(dz, mats[5]).T

    sum_w = jnp.zeros((GROUPS, LANES), f32)
    sqr_w = jnp.zeros((GROUPS, LANES), f32)
    for b in range(blocks):
        here = slice(b * LANES, (b + 1) * LANES)
        do = do_s[:, here]
        da = []
        for j in range(NEAREST):
            da.append(over_channels(do * vgat[b, :, cols(j)]))
        mean_da = functools.reduce(jnp.add, [da[j] * att[b, :, cols(j)] for j in range(NEAREST)])
        ds = jnp.concatenate(
            [att[b, :, cols(j)] * (da[j] - mean_da) for j in range(NEAREST)], axis=1
        ).astype(bf16)
        ds_s[b] = ds
        dy = nn(att_out, ds) * dyw[b]
        dyw[b] = dy
        sum_w = sum_w + lane_fold(dy)
        sqr_w = sqr_w + lane_fold(dy * wpre[b])

    back_w = pair_row(sum_w, sqr_w)
    collect_w = all_sum(4, back_w + pos_row)
    put_matrix(4, nn(o_ts[...], dz16[...]))
    o_flat, v_flat = pl.ds(per_matrix, per_matrix), pl.ds(0, per_matrix)
    o_pair = swap(2, flat.at[o_flat], pair_got.at[o_flat])
    add_groups = jnp.where(
        iota((8, 3 * GROUPS), 1) // GROUPS == iota((8, 3 * GROUPS), 0), 1.0, 0.0
    ).astype(bf16)
    dv_s[...] = jnp.zeros(dv_s.shape, f32)
    for b in range(blocks):
        here = slice(b * LANES, (b + 1) * LANES)
        do = do_s[:, here]
        for j in range(NEAREST):
            xs[b, :, cols(j)] = (each_channel(att[b, :, cols(j)]) * do).astype(bf16)
        mix = [
            (tiles(over_channels(do * pos_cols[d])) * att[b]).astype(bf16) for d in range(3)
        ]
        dmix[b] = nn(add_groups, jnp.concatenate(mix, axis=0))
        dv_s[pl.ds(starts[b], WINDOW)] += nt(onehot[b, 0:WINDOW], xs[b])
    dv = dv_s[...].astype(bf16)
    dv_s[...] = nn(dv, mats[8])
    put_matrix(3, nn(h_ts[...], nn(dv, reorder).astype(bf16)))
    v_pair = swap(5, flat.at[v_flat], pair_got.at[v_flat])
    send_dense(o_pair, dense + per_matrix, per_matrix)
    send_dense(v_pair, dense, per_matrix)
    stats = collect_w()
    one = row_to_col(stats[:, 0:GROUPS], GROUPS) * inv_pairs
    two = row_to_col(stats[:, GROUPS : 2 * GROUPS], GROUPS) * inv_pairs
    pos_hat = [row_to_col(stats[:, 64 + 8 * c : 72 + 8 * c], 8) for c in range(3)]
    pos_alone = [row_to_col(stats[:, 88 + 8 * c : 96 + 8 * c], 8) for c in range(3)]

    sk_s[...] = jnp.zeros(sk_s.shape, f32)
    pos_att_rows = split(pos_att[:, 0:8].T, 3)
    pos_att_rows = jnp.concatenate(pos_att_rows, axis=0)
    dw_sums = []
    for b in range(blocks):
        dw = (gain_w * rs_w * (dyw[b] - pmask[b, 0:1] * (one + wpre[b] * two))).astype(bf16)
        sk_s[pl.ds(starts[b], WINDOW)] += nt(onehot[b, 0:WINDOW], dw)
        dw_sums.append(lane_slots(dw.astype(f32)))
        dw_s[b] = dw
    dq_att = jnp.concatenate(dw_sums, axis=1)
    both_att = jnp.concatenate([dq_att.T, -sk_s[...]], axis=1)
    both_split = split(both_att, 2)
    low = nn(
        jnp.concatenate([h_ts[...]] * 2, axis=1), jnp.concatenate(both_split, axis=0)
    )
    low_f[...] = low.reshape(per_matrix, 2, LOW_ROWS, LANES)
    low_pair = swap(3, low_f, low_got)
    dh = nn(jnp.concatenate(both_split + both_split[0:1], axis=1), ba_s[...]) + dv_s[...]
    dy = dh * slope_a[...]
    z_s[...] = dy
    shift_grad_a = row_sum(dy)
    away = jnp.concatenate(
        [mu_s[...] * shift_grad_a[:, k * LANES : (k + 1) * LANES] for k in range(2)], axis=1
    )
    first_pair = put_first(1, from_feat(dy) - away)
    along = [jnp.zeros((8, 1), f32) for _ in range(3)]
    sum_p = jnp.zeros((8, 1), f32)
    sqr_p = jnp.zeros((8, 1), f32)
    for b in range(blocks):
        back = nn(pos_att_rows, dw_s[b])
        d_act = dmix[b] + back[0:8] + back[8:16] + back[16:24]
        dy = d_act * slope_p[b]
        sum_p = sum_p + lane_sum(dy)
        sqr_p = sqr_p + lane_sum(dy * pos[b])
        for c in range(3):
            along[c] = along[c] + lane_sum(dy * rel[b, c : c + 1])
    gain_grad_a = row_sum(z_s[...] * a1_s[...])
    last = col_to_row(sum_p, 0) + col_to_row(sqr_p, 8)
    for c in range(3):
        last = last + col_to_row(along[c], 16 + 8 * c)
    collect_a = all_sum(
        5, jnp.concatenate([fold(shift_grad_a), fold(gain_grad_a), last], axis=0)
    )
    send_wide(first_pair, 1)
    send_low(low_pair)

    d_att_out = sum(nt(uact[b], ds_s[b]) for b in range(blocks))
    d_pos_att = sum(
        nt(jnp.concatenate(split(act[b], 3), axis=0), dw_s[b]) for b in range(blocks)
    )
    d_pos_att = d_pos_att[0:8] + d_pos_att[8:16] + d_pos_att[16:24]
    d_pos_split = split(d_pos_att, 3)
    d_att_in = sum(
        nn(q_s[...], piece[:, 0:GROUPS]) + nn(k_s[...], piece[:, GROUPS : 2 * GROUPS])
        for piece in both_split
    )
    d_att_in = d_att_in + sum(tn(pos_mat[0:8], piece) for piece in d_pos_split)
    d_pos_out = sum(nn(piece, att_in_t) for piece in d_pos_split)
    do_split = split(do_s[...], 2)
    bd_split = split(bd_s[...], 2)
    cross = nt(bd_split[0], do_split[0]) + nt(bd_split[0], do_split[1]) + nt(bd_split[1], do_split[0])
    own_group = iota((GROUPS, WIDTH), 1) % GROUPS == iota((GROUPS, WIDTH), 0)
    cross = [
        row_sum(jnp.where(own_group, cross[d * GROUPS : (d + 1) * GROUPS], 0.0)) for d in range(3)
    ]
    cross = jnp.concatenate(cross + [jnp.zeros((5, WIDTH), f32)], axis=0)
    d_pos_out = d_pos_out + sum(nn(piece, reorder) for piece in split(cross, 3))
    d_pos_rows = [d_pos_out[d : d + 1] for d in range(3)]
    pieces = [jnp.zeros((1, TAIL_POS_OUT), f32)] + d_pos_rows
    pieces = pieces + [
        gain_grad_a, col_to_row(sqr_p, 0)[:, 0:3], back_w[:, GROUPS : 2 * GROUPS], gain_grad_o,
        shift_grad_a, col_to_row(sum_p, 0)[:, 0:3], back_w[:, 0:GROUPS], shift_grad_o,
        jnp.zeros((1, TAIL_PAD - TAIL_USED), f32),
    ]
    small = 5 * per_matrix
    used_rows = OFF_TAIL // LANES + TAIL_PAD // LANES - 5 * SQUARE // LANES
    spare_rows = (sliced - small) * 2 * SLICE_ROWS - used_rows
    pieces_rows = [
        d_att_in.reshape(WIDTH * GROUPS // LANES, LANES),
        d_att_out.reshape(GROUPS * GROUPS // LANES, LANES),
        jnp.concatenate(pieces, axis=1).reshape(TAIL_PAD // LANES, LANES),
        jnp.zeros((spare_rows, LANES), f32),
    ]
    flat[small - dense : sliced - dense] = jnp.concatenate(pieces_rows, axis=0).reshape(
        sliced - small, 2, SLICE_ROWS, LANES
    )
    small_flat = pl.ds(small - dense, sliced - small)
    small_pair = swap(4, flat.at[small_flat], pair_got.at[small_flat])
    send_dense(small_pair, small, sliced - small)

    stats = collect_a()
    one, two = unfold(stats[0:2]) * inv_points, unfold(stats[2:4]) * inv_points
    def halves(row):
        return jnp.concatenate(
            [
                jnp.broadcast_to(row[:, k * LANES : (k + 1) * LANES], (SLICE_ROWS // 2, LANES))
                for k in range(2)
            ],
            axis=0,
        )

    scale_tile, two_tile = halves(gain_a * rs_a), halves(two)
    da1 = (gain_a * rs_a * (z_s[...] - point_mask * (one + a1_s[...] * two))).astype(bf16)
    outs[1] = (dz_s[...] + nt(da1, w_in)).astype(bf16)
    store(outs.at[1], gfeat_h)
    one = row_to_col(stats[4:5, 0:8], 8) * inv_pairs
    two = row_to_col(stats[4:5, 8:16], 8) * inv_pairs
    pos_in_row = jnp.zeros((1, LANES), f32)
    for c in range(3):
        moved = row_to_col(stats[4:5, 16 + 8 * c : 24 + 8 * c], 8)
        moved = gain_p * rs_p * (moved - one * pos_alone[c] - two * pos_hat[c])
        pos_in_row = pos_in_row + col_to_row(moved, 3 * c)

    begin = me * shard_len
    lead, skip = lax.rem(begin, CHUNK), lax.rem(begin, LANES)
    shard_at = pl.ds(lead // LANES, shard_rows)
    lanes_all = iota((shard_rows, LANES), 1)
    inside = iota((shard_rows, LANES), 0) * LANES + lanes_all < shard_len
    main = shard_len // 1024 * 1024
    parts = [pl.ds(at, size) for at, size in ((0, main), (main, shard_len - main)) if size]
    for k in range(3):
        for at in parts:
            tail_g[at] = state[k][at]
        rows = jnp.where(inside, tail_g[...].reshape(shard_rows, LANES), 0.0)
        turned = pltpu.roll(rows, skip, 1)
        above = pltpu.roll(turned, 1, 0)
        slab_f[k] = jnp.zeros(slab_f.shape[1:], f32)
        slab_f[k, shard_at, :] = jnp.where(lanes_all < skip, above, turned)

    def slice_of(slot):
        return 2 * (slot * half + chip) + core

    def when_in(slot, low, high, act_on):
        if (slot + 1) * n <= low or slot * n >= high:
            return
        if slot * n >= low and (slot + 1) * n <= high:
            act_on()
        else:
            number = slice_of(slot)
            pl.when((number >= low) & (number < high))(act_on)

    def others_sum(total, part):
        def add(k, total):
            return total + part(peer(chip, k, half))

        return lax.fori_loop(1, half, add, total, unroll=half <= 16)

    def take_wide(which):
        got = got_wide.at[which, pl.ds(0, half - 1)]
        pltpu.make_async_copy(got, got, wd_rsem.at[which]).wait()
        index = lax.rem(chip, per_matrix)

        def part(other):
            return got_wide[which, other, 0].astype(f32) + got_wide[which, other, 1].astype(f32)

        return others_sum(first_f[which, index, core] + first_got[which, index], part)

    def take_low(kind):
        got = got_low.at[kind, pl.ds(0, half - 1)]
        pltpu.make_async_copy(got, got, low_rsem.at[kind]).wait()
        index = lax.rem(chip, per_matrix)
        return others_sum(low_sum[index], lambda other: got_low[kind, other])

    def low_product(factor, which):
        factor = factor.reshape(SLICE // WIDTH, 2 * GROUPS)[:, which * GROUPS : (which + 1) * GROUPS]
        return sum(nn(piece, att_in_t) for piece in split(factor, 2)).reshape(SLICE_ROWS, LANES)

    squares = jnp.zeros((SLICE_ROWS, LANES), f32)
    matrix = SQUARE // SLICE
    for slot in range(slots):
        sums[slot] = jnp.zeros((SLICE_ROWS, LANES), f32)

    def take_dense(in_order, slot):
        index = slot * half + chip
        got = got16.at[slot, pl.ds(0, half - 1)]
        pltpu.make_async_copy(got, got, rs_rsem.at[slot]).wait()
        total = flat[index - dense, core] + pair_got[index - dense]
        total = others_sum(total, lambda other: got16[slot, other].astype(f32))
        sums[slot] = total if in_order else whole_rows(total)

    def take_hat():
        hat_s[...] = two_tile * take_wide(0)

    def first(slot):
        sums[slot] = whole_rows(scale_tile * (take_wide(1) - hat_s[...]))

    def add_pos_in(slot):
        at_row = iota((SLICE_ROWS, LANES), 0) == OFF_TAIL % SLICE // LANES
        sums[slot] += jnp.where(at_row, pos_in_row, 0.0)

    def each_slot(low, high, act_on):
        for slot in range(slots):
            when_in(slot, low, high, functools.partial(act_on, slot))

    each_slot(DENSE_FROM * matrix, 5 * matrix, functools.partial(take_dense, False))
    each_slot(0, matrix, lambda slot: take_hat())
    each_slot(0, matrix, first)
    for kind in range(low_kinds):
        kinds = range(2) if low_kinds == 1 else (kind,)

        def fill(kind=kind, kinds=kinds):
            factor = take_low(kind)
            for which in kinds:
                for slot in range(slots):

                    def product(slot=slot, which=which):
                        sums[slot] = low_product(factor, which)

                    when_in(slot, (1 + which) * matrix, (2 + which) * matrix, product)

        if low_kinds == 1:
            fill()
        else:
            when_in(0, (1 + kind) * matrix, (2 + kind) * matrix, fill)
    each_slot(5 * matrix, 2 * sliced, functools.partial(take_dense, True))
    each_slot(OFF_TAIL // SLICE, OFF_TAIL // SLICE + 1, add_pos_in)
    for slot in range(slots):
        squares = squares + sums[slot] * sums[slot]
    squares = total(squares)

    collect_norm = all_sum(6, jnp.where(lane == 0, squares, 0.0))

    def each_owner(slot, act_on):
        number = slice_of(slot)
        low = number * SLICE // shard_len
        high = jnp.minimum((number * SLICE + SLICE - 1) // shard_len, n - 1)
        for side in range(sides):
            owner = low + side

            @pl.when((number * SLICE < total_len) & (owner <= high))
            def _(owner=owner, side=side):
                act_on(owner, number - owner * shard_len // SLICE, side)

    def owned_rows(k):
        return owned.at[pl.ds(pl.multiple_of(k * SLICE_ROWS, SLICE_ROWS), SLICE_ROWS)]

    def own_copy(slot, owner, k, side):
        return pltpu.make_async_remote_copy(
            src_ref=sums.at[slot],
            dst_ref=owned_rows(k),
            send_sem=own_ssem.at[slot, side],
            recv_sem=own_rsem.at[k],
            device_id=place(owner),
            device_id_type=MESH,
        )

    for slot in range(slots):

        def hand_over(owner, k, side, slot=slot):
            @pl.when(owner != me)
            def _():
                own_copy(slot, owner, k, side).start()

            @pl.when(owner == me)
            def _():
                owned_rows(k)[...] = sums[slot]

        each_owner(slot, hand_over)

    first_slice = begin // SLICE
    last_slice = (begin + shard_len - 1) // SLICE
    for k in range(span):
        number = first_slice + k

        @pl.when((number <= last_slice) & (lax.rem(number, n) != me))
        def _(k=k):
            rows = owned.at[pl.ds(k * SLICE_ROWS, SLICE_ROWS)]
            pltpu.make_async_copy(rows, rows, own_rsem.at[k]).wait()

    slab_shape = slab_f.shape[1:]
    flat_at = iota(slab_shape, 0) * LANES + iota(slab_shape, 1) - lead
    grad = owned[pl.ds((begin - lead - first_slice * SLICE) // LANES, slab_shape[0]), :]
    grad = jnp.where((flat_at >= 0) & (flat_at < shard_len), grad, 0.0)

    stats = collect_norm()
    norm = jnp.sqrt(pick(stats, 0))
    grad = grad * jnp.minimum(1.0, clip_norm / norm)
    updated = adam(slab_f[0], slab_f[1], slab_f[2], grad)
    shard_w[...] = updated[0].astype(bf16)
    all_w[core, chip] = updated[0].astype(bf16)
    norm_s[...] = jnp.broadcast_to(norm, norm_s.shape)

    in_row = n_cols // 2
    row_chip = col_id // 2

    def send_slab(source, slab, row, chip_in_row):
        pltpu.make_async_remote_copy(
            src_ref=source,
            dst_ref=all_w.at[core, slab],
            send_sem=ag_ssem,
            recv_sem=ag_rsem.at[slab],
            device_id=(row, 2 * chip_in_row + core),
            device_id_type=MESH,
        ).start()

    def forward(other):
        pltpu.make_async_remote_copy(
            src_ref=all_w.at[core, other],
            dst_ref=all_w.at[core, other],
            send_sem=fw_ssem,
            recv_sem=fw_rsem,
            device_id=sibling,
            device_id_type=MESH,
        ).start()

    def arrived(other):
        pltpu.make_async_copy(shard_w, shard_w, ag_rsem.at[other]).wait()

    def send_along(k, carry):
        send_slab(shard_w, chip, peer(row_id, k, n_rows), row_chip)
        return carry

    def send_within(k, carry):
        send_slab(shard_w, chip, row_id, peer(row_chip, k, in_row))
        return carry

    loop(1, n_rows, send_along)
    loop(1, in_row, send_within)
    forward(chip)
    store(norm_s, gnorm_h)
    for k in range(3):
        slab_f[k] = updated[k]
        turned = pltpu.roll(slab_f[k, shard_at, :], lax.rem(LANES - skip, LANES), 1)
        below = pltpu.roll(turned, shard_rows - 1, 0)
        tail_g[...] = jnp.where(lanes_all < LANES - skip, turned, below).reshape(shard_rows * LANES)
        for at in parts:
            news[k][at] = tail_g[at]
    for source, target in ((0, new_master_h), (1, new_first_h), (2, new_second_h)):
        store(news[source], target)

    for index, rows in sent:
        drain_stats(index, rows)

    def drain(low, high, slices, sem):
        if high - low == half:
            rest = slices.at[pl.ds(0, half - 1)]
            pltpu.make_async_copy(rest, rest, sem).wait()
        else:
            inside = (chip >= low) & (chip < high)

            def wait_one(k, carry):
                pltpu.make_async_copy(slices.at[0], slices.at[0], sem).wait()
                return carry

            lax.fori_loop(0, high - low - inside.astype(jnp.int32), wait_one, 0)

    for which in range(2):
        drain(0, per_matrix, got_wide.at[which], wd_ssem.at[which])
    for kind in range(low_kinds):
        low_at = (1 + kind) * per_matrix % half
        drain(low_at, low_at + per_matrix, got_low.at[kind], low_ssem.at[kind])
    for slot in range(slots):
        low_at = max(dense - slot * half, 0)
        high_at = min(sliced - slot * half, half)
        if high_at > low_at:
            drain(low_at, high_at, got16.at[slot], rs_ssem.at[slot])

        def own_drain(owner, k, side, slot=slot):
            @pl.when(owner != me)
            def _():
                own_copy(slot, owner, k, side).wait_send()

        each_owner(slot, own_drain)
    for copy in stores:
        copy.wait()

    def spread_row(k, carry):
        other = peer(row_id, n_rows - k, n_rows) * in_row + row_chip
        arrived(other)

        def send_on(i, carry):
            send_slab(all_w.at[core, other], other, row_id, peer(row_chip, i, in_row))
            return carry

        loop(1, in_row, send_on)
        forward(other)
        return carry

    loop(1, n_rows, spread_row)

    def pass_on(k, carry):
        step = k // (in_row - 1)
        row = jnp.where(step == 0, row_id, peer(row_id, n_rows - step, n_rows))
        other = row * in_row + peer(row_chip, in_row - 1 - lax.rem(k, in_row - 1), in_row)
        arrived(other)
        forward(other)
        return carry

    loop(0, n_rows * (in_row - 1), pass_on)
    pltpu.make_async_copy(all_w.at[core], all_w.at[core], fw_rsem).wait()
    rows = CHUNK // LANES

    def chunk(c):
        value = None
        last_owner = min((c * CHUNK + CHUNK - 1) // shard_len, n - 1)
        for owner in range(c * CHUNK // shard_len, last_owner + 1):
            k = c - owner * shard_len // CHUNK
            part = all_w[owner % 2, owner // 2, rows * k : rows * (k + 1)].astype(f32)
            value = part if value is None else value + part
        return value

    whole = total_len // (2 * CHUNK)
    for c in range(whole):
        both = jnp.concatenate([chunk(2 * c), chunk(2 * c + 1)], axis=0)
        weights_out[pl.ds(2 * CHUNK * c, 2 * CHUNK)] = both.astype(bf16).reshape(2 * CHUNK)
    left = total_len - whole * 2 * CHUNK
    if left:
        parts = [chunk(2 * whole)]
        parts.append(chunk(2 * whole + 1) if left > CHUNK else jnp.zeros((rows, LANES), f32))
        both = jnp.concatenate(parts, axis=0).astype(bf16).reshape(2 * CHUNK)
        weights_out[pl.ds(2 * CHUNK * whole, left)] = both[0:left]

    pltpu.make_async_copy(all_w.at[core], all_w.at[core], fw_ssem).wait()
    rest = all_w.at[core, pl.ds(0, half - 1)]
    pltpu.make_async_copy(rest, rest, ag_ssem).wait()


def finish_kernel(
    out_t, gfeat_t, gnorm_t, master_t, first_t, second_t, weights_t,
    out_h, gfeat_h, gnorm, master_h, first_h, second_h, weights_h,
    norm_s, sem,
):
    copies = [
        pltpu.make_async_copy(source, target, sem.at[k])
        for k, (source, target) in enumerate(
            (
                (weights_t, weights_h),
                (out_t, out_h),
                (gfeat_t, gfeat_h),
                (master_t, master_h),
                (first_t, first_h),
                (second_t, second_h),
                (gnorm_t, norm_s),
            )
        )
    ]
    for copy in copies:
        copy.start()
    copies[-1].wait()
    gnorm[...] = norm_s[0:1, 0:1]
    for copy in copies[:-1]:
        copy.wait()


def lane_slots(value):
    return functools.reduce(
        jnp.add, [value[:, j * LANES : (j + 1) * LANES] for j in range(NEAREST)]
    )


def shards(
    n_rows, n_cols,
    features, coords, valid_mask, neighbors, cotangent, weights, master, first_moment, second_moment,
):
    n = n_rows * n_cols
    half = n // 2
    points = features.shape[0]
    blocks = points // LANES
    shard_len = master.shape[0]
    total_len = weights.shape[0]

    def up(value, unit):
        return -(-value // unit) * unit

    shard_rows = up(-(-shard_len // LANES) + 1, 8)
    slab_rows = up(shard_rows + CHUNK // LANES, 16)
    sliced = up(-(-total_len // SLICE), 2) // 2
    slots = -(-sliced // half)
    per_matrix = SQUARE // SLICE // 2
    dense_pairs = sliced - DENSE_FROM * per_matrix
    low_kinds = 1 if per_matrix % half == 0 else 2
    sides = (SLICE + shard_len - 2) // shard_len + 1
    span = (SLICE + shard_len - 2) // SLICE + 1
    hbm = pl.BlockSpec(memory_space=pltpu.HBM)
    vmem = pl.BlockSpec(memory_space=pltpu.VMEM)
    dma = pltpu.SemaphoreType.DMA
    shape = jax.ShapeDtypeStruct

    def pairs(rows, dtype=f32):
        return pltpu.VMEM((blocks, rows, PAIRS), dtype)

    def shard():
        return [pltpu.VMEM(master.shape, f32) for _ in range(3)]

    scratch = [
        pltpu.VMEM(features.shape, bf16),
        pltpu.VMEM(coords.shape, f32),
        pltpu.VMEM(valid_mask.shape, jnp.int32),
        pltpu.VMEM(neighbors.shape, jnp.int32),
        pltpu.VMEM(features.shape, bf16),
        pltpu.VMEM((SQUARE,), bf16),
        pltpu.VMEM((1024,), bf16),
        pltpu.VMEM(weights.shape, bf16),
        shard(),
        shard(),
        pltpu.VMEM((2, *features.shape), bf16),
        pltpu.VMEM((1, LANES), f32),
        dma((11,)),
        dma((7,)),
        pltpu.VMEM((7, 8, LANES), f32),
        pltpu.VMEM((7, n, 8, LANES), f32),
        dma((7,)),
        dma((7,)),
        pltpu.VMEM((TAIL_PAD,), bf16),
        pltpu.VMEM((9, WIDTH, WIDTH), bf16),
        pairs(WINDOW + POS_ROWS, bf16),
        pairs(WIDTH),
        pairs(GROUPS),
        pairs(GROUPS),
        pairs(GROUPS, bf16),
        pairs(GROUPS),
        pairs(8),
        pairs(8),
        pairs(8),
        pairs(8),
        pairs(8),
        pairs(8),
        pltpu.VMEM((WIDTH, points), bf16),
        pltpu.VMEM((points, WIDTH), f32),
        pairs(8),
        pltpu.VMEM((points, WIDTH), f32),
        pltpu.VMEM((points, WIDTH), f32),
        pltpu.VMEM((points, WIDTH), bf16),
        pltpu.VMEM((WIDTH, points), bf16),
        pltpu.VMEM((WIDTH, points), bf16),
        pltpu.VMEM((WIDTH, points), bf16),
        pltpu.VMEM((6 * GROUPS, WIDTH), bf16),
        pltpu.VMEM((points, WIDTH), bf16),
        pltpu.VMEM((WIDTH, points), bf16),
        pltpu.VMEM((WIDTH, points), f32),
        pltpu.VMEM((points, WIDTH), f32),
        pltpu.VMEM((points, GROUPS), f32),
        pltpu.VMEM((3 * GROUPS, points), f32),
        pairs(GROUPS, bf16),
        pairs(GROUPS, bf16),
        pairs(WIDTH, bf16),
        pltpu.VMEM((points, WIDTH), f32),
        pltpu.VMEM((points, WIDTH), bf16),
        pltpu.VMEM((WIDTH, LANES), f32),
        pltpu.VMEM((dense_pairs, 2, SLICE_ROWS, LANES), f32),
        pltpu.VMEM((dense_pairs, SLICE_ROWS, LANES), f32),
        pltpu.VMEM((dense_pairs, SLICE_ROWS, LANES), bf16),
        pltpu.VMEM((slots, half, SLICE_ROWS, LANES), bf16),
        pltpu.VMEM((2, per_matrix, 2, SLICE_ROWS, LANES), f32),
        pltpu.VMEM((2, per_matrix, SLICE_ROWS, LANES), f32),
        pltpu.VMEM((2, per_matrix, 2, SLICE_ROWS, LANES), bf16),
        pltpu.VMEM((2, half, 2, SLICE_ROWS, LANES), bf16),
        pltpu.VMEM((per_matrix, 2, LOW_ROWS, LANES), f32),
        pltpu.VMEM((per_matrix, LOW_ROWS, LANES), f32),
        pltpu.VMEM((per_matrix, LOW_ROWS, LANES), f32),
        pltpu.VMEM((low_kinds, half, LOW_ROWS, LANES), f32),
        pltpu.VMEM((SLICE_ROWS, LANES), f32),
        pltpu.VMEM((slots, SLICE_ROWS, LANES), f32),
        pltpu.VMEM((up(max(span * SLICE_ROWS, CHUNK // LANES + slab_rows), SLICE_ROWS), LANES), f32),
        pltpu.VMEM((shard_rows * LANES,), f32),
        pltpu.VMEM((3, slab_rows, LANES), f32),
        pltpu.VMEM((slab_rows, LANES), bf16),
        pltpu.VMEM((2, half, slab_rows, LANES), bf16),
        dma((6,)),
        dma((6,)),
        dma((slots,)),
        dma((slots,)),
        dma((2,)),
        dma((2,)),
        dma((low_kinds,)),
        dma((low_kinds,)),
        dma((slots, sides)),
        dma((span,)),
        dma,
        dma((half,)),
        dma,
        dma,
    ]
    results = pl.pallas_call(
        functools.partial(block_kernel, n_rows, n_cols),
        out_shape=(
            shape(features.shape, bf16),
            shape(features.shape, bf16),
            shape((1, LANES), f32),
            shape(master.shape, f32),
            shape(master.shape, f32),
            shape(master.shape, f32),
            pltpu.VMEM(weights.shape, bf16),
        ),
        in_specs=[hbm] * 9,
        out_specs=[pl.BlockSpec(memory_space=pl.ANY)] * 6 + [vmem],
        scratch_shapes=scratch,
        compiler_params=pltpu.CompilerParams(
            collective_id=0, has_side_effects=True, vmem_limit_bytes=48 * 2**20
        ),
    )(*(pltpu.with_memory_space_constraint(x, pltpu.HBM) for x in (features, coords, valid_mask, neighbors, cotangent, weights, master, first_moment, second_moment)))
    results = pl.pallas_call(
        finish_kernel,
        out_shape=(
            shape(features.shape, bf16),
            shape(features.shape, bf16),
            shape((1, 1), f32),
            shape(master.shape, f32),
            shape(master.shape, f32),
            shape(master.shape, f32),
            shape(weights.shape, bf16),
        ),
        in_specs=[pl.BlockSpec(memory_space=pl.ANY)] * 7,
        out_specs=[hbm, hbm, vmem, hbm, hbm, hbm, hbm],
        scratch_shapes=[pltpu.VMEM((1, LANES), f32), dma((7,))],
        compiler_params=pltpu.CompilerParams(vmem_limit_bytes=8 * 2**20),
    )(*results)
    return results[0], results[1], results[2].reshape(()), *results[3:]


def solution(mesh):
    both = ("rows", "cols")
    rows_split, cols_split, flat_split = P(both, None), P(None, both), P(both)
    return jax.shard_map(
        functools.partial(shards, mesh.shape["rows"], mesh.shape["cols"]),
        mesh=mesh,
        in_specs=(
            rows_split, cols_split, flat_split, cols_split, rows_split, P(),
            flat_split, flat_split, flat_split,
        ),
        out_specs=(rows_split, rows_split, P(), flat_split, flat_split, flat_split, P()),
        check_vma=False,
    )
```

```python
import functools

import jax
import jax.numpy as jnp
from jax import lax
from jax.experimental import pallas as pl
from jax.experimental.pallas import tpu as pltpu
from jax.sharding import PartitionSpec as P

WIDTH = 256
GROUPS = 32
NEAREST = 16
PER_GROUP = WIDTH // GROUPS
LANES = 128
WINDOW = 256
PAIRS = NEAREST * LANES

SQUARE = WIDTH * WIDTH
OFF_ATT_IN = 5 * SQUARE
OFF_ATT_OUT = OFF_ATT_IN + WIDTH * GROUPS
OFF_TAIL = OFF_ATT_OUT + GROUPS * GROUPS
NORMS = 2 * WIDTH + 3 + GROUPS
TAIL_POS_OUT = 9
TAIL_GAINS = TAIL_POS_OUT + 3 * WIDTH
TAIL_SHIFTS = TAIL_GAINS + NORMS
TAIL_USED = TAIL_SHIFTS + NORMS
TAIL_PAD = 2048
SLICE = 2048
SLICE_ROWS = SLICE // LANES
LOW_ROWS = SLICE // WIDTH * 2 * GROUPS // LANES
DENSE_FROM = 3
CHUNK = 1024
POS_ROWS = 32

bn_eps = 1e-05
clip_norm = 0.01
learn_rate = 0.05
beta_one = 0.9
beta_two = 0.999
adam_eps = 1e-08
decay_rate = 0.01
step_count = 10
masked_logit = -1000000000.0

f32 = jnp.float32
bf16 = jnp.bfloat16
MESH = pl.DeviceIdType.MESH


def contract(a, b, left, right):
    return lax.dot_general(a, b, (((left,), (right,)), ((), ())), preferred_element_type=f32)


def nn(a, b):
    return contract(a, b, 1, 0)


def nt(a, b):
    return contract(a, b, 1, 1)


def tn(a, b):
    return contract(a, b, 0, 0)


def split(value, parts):
    pieces = []
    for _ in range(parts):
        piece = value.astype(bf16)
        pieces.append(piece)
        value = value - piece.astype(f32)
    return pieces


def silu_parts(value):
    gate = 0.5 * jnp.tanh(0.5 * value) + 0.5
    return value * gate, gate


def silu_slope(value, gate):
    return gate * (1.0 + value * (1.0 - gate))


def iota(shape, dim):
    return lax.broadcasted_iota(jnp.int32, shape, dim)


def loop(begin, end, body):
    if end - begin <= 31:
        for k in range(begin, end):
            body(k, 0)
    else:
        lax.fori_loop(begin, end, body, 0)


def row_to_col(row, count):
    wide = jnp.broadcast_to(row, (count, row.shape[1]))
    same = iota(wide.shape, 0) == iota(wide.shape, 1)
    return jnp.sum(jnp.where(same, wide, 0.0), axis=1, keepdims=True)


def col_to_row(col, offset):
    wide = jnp.broadcast_to(col, (col.shape[0], LANES))
    same = iota(wide.shape, 0) + offset == iota(wide.shape, 1)
    return jnp.sum(jnp.where(same, wide, 0.0), axis=0, keepdims=True)


def row_sum(value):
    return jnp.sum(value, axis=0, keepdims=True)


def lane_fold(value):
    total = value[:, 0:LANES]
    for k in range(1, value.shape[1] // LANES):
        total = total + value[:, k * LANES : (k + 1) * LANES]
    return total


def lane_sum(value):
    return jnp.sum(lane_fold(value), axis=1, keepdims=True)


def tiles(value):
    return jnp.concatenate([value] * NEAREST, axis=1)


def adam(param, moment, second, grad):
    moment_new = beta_one * moment + (1.0 - beta_one) * grad
    second_new = beta_two * second + (1.0 - beta_two) * grad * grad
    moment_hat = moment_new / (1.0 - beta_one**step_count)
    second_hat = second_new / (1.0 - beta_two**step_count)
    param_new = param - learn_rate * (
        moment_hat / (jnp.sqrt(second_hat) + adam_eps) + decay_rate * param
    )
    return param_new, moment_new, second_new


def peer(me, step, count):
    if count & (count - 1) == 0:
        return me ^ (count - step)
    return lax.rem(me + step, count)


def block_kernel(
    n_rows, n_cols,
    feat_h, coords_h, valid_h, nbrs_h, cot_h, weights_h, master_h, first_h, second_h,
    out_h, gfeat_h, gnorm_h, new_master_h, new_first_h, new_second_h, weights_out,
    feat, coords, valid, nbrs, cot, w_first, pos_first, weights, state, news, outs, norm_s, in_sem, out_sem,
    stat_send, stat_buf, stat_ssem, stat_rsem,
    tail1d, mats, onehot, vgat, att, wpre, uact, dyw, rel, pos, act, pmask, allow, dmix,
    ft_s, slope_a, slope_p, a1_s, z_s, h_s, h_ts, q_s, k_s, ba_s, o_s, o_ts, do_s, dv_s, sk_s, bd_s, ds_s, dw_s, xs, dz_s, dz16,
    mu_s, flat, pair_got, part16, got16, first_f, first_got, wide16, got_wide, low_f, low_got, low_sum, got_low, hat_s, sums, owned, tail_g, slab_f, shard_w, all_w,
    pair_ssem, pair_rsem, rs_ssem, rs_rsem, wd_ssem, wd_rsem, low_ssem, low_rsem, own_ssem, own_rsem, ag_ssem, ag_rsem, fw_ssem, fw_rsem,
):
    n = n_rows * n_cols
    half = n // 2
    row_id, col_id = lax.axis_index("rows"), lax.axis_index("cols")
    me = row_id * n_cols + col_id
    core = lax.rem(col_id, 2)
    chip = me // 2
    points = feat.shape[0]
    blocks = points // LANES
    starts = [min(max(LANES * b - (WINDOW - LANES) // 2, 0), points - WINDOW) for b in range(blocks)]
    total_len = weights.shape[0]
    shard_len = master_h.shape[0]
    shard_rows = -(-tail_g.shape[0] // LANES)
    per_matrix = SQUARE // SLICE // 2
    dense = DENSE_FROM * per_matrix
    sliced = dense + flat.shape[0]
    slots = got16.shape[0]
    low_kinds = got_low.shape[0]
    sides = own_ssem.shape[1]
    span = own_rsem.shape[0]

    def place(device):
        return (device // n_cols, lax.rem(device, n_cols))

    barrier = pltpu.get_barrier_semaphore()

    def greet(k, carry):
        pl.semaphore_signal(barrier, inc=1, device_id=place(peer(me, k, n)), device_id_type=MESH)
        return carry

    loop(1, n, greet)
    loads = []

    def load(source, target):
        copy = pltpu.make_async_copy(source, target, in_sem.at[len(loads)])
        copy.start()
        loads.append(copy)
        return copy

    stores = []

    def store(source, target):
        copy = pltpu.make_async_copy(source, target, out_sem.at[len(stores)])
        copy.start()
        stores.append(copy)

    early = [
        load(feat_h, feat),
        load(weights_h.at[pl.ds(0, SQUARE)], w_first),
        load(weights_h.at[pl.ds(OFF_TAIL, 1024)], pos_first),
        load(nbrs_h, nbrs),
        load(coords_h, coords),
        load(valid_h, valid),
    ]

    late = [load(weights_h, weights), load(cot_h, cot)]
    for source, target in ((master_h, 0), (first_h, 1), (second_h, 2)):
        late.append(load(source, state[target]))
    owned[...] = jnp.zeros(owned.shape, f32)
    for copy in early:
        copy.wait()

    sent = []

    def all_sum(index, message):
        rows = message.shape[0]
        stat_send[index, 0:rows] = message
        stat_buf[index, me, 0:rows] = message

        def post(k, carry):
            pltpu.make_async_remote_copy(
                src_ref=stat_send.at[index, pl.ds(0, rows)],
                dst_ref=stat_buf.at[index, me, pl.ds(0, rows)],
                send_sem=stat_ssem.at[index],
                recv_sem=stat_rsem.at[index],
                device_id=place(peer(me, k, n)),
                device_id_type=MESH,
            ).start()
            return carry

        loop(1, n, post)
        sent.append((index, rows))

        def collect():
            span = stat_buf.at[index, pl.ds(0, n - 1), pl.ds(0, rows)]
            pltpu.make_async_copy(span, span, stat_rsem.at[index]).wait()
            return jnp.sum(stat_buf[index, :, 0:rows], axis=0)

        return collect

    sibling = (row_id, col_id + 1 - 2 * core)
    def put_halves(target, value):
        rows = SLICE_ROWS // 2
        for k in range(2):
            part = value[:, k * LANES : (k + 1) * LANES]
            target[:, :, k * rows : (k + 1) * rows] = part.reshape(per_matrix, 2, rows, LANES)

    def whole_rows(piece):
        rows = SLICE_ROWS // 2
        return jnp.concatenate([piece[0:rows], piece[rows:]], axis=1).reshape(SLICE_ROWS, LANES)

    def put_matrix(m, grad):
        at = (m - DENSE_FROM) * per_matrix
        put_halves(flat.at[at : at + per_matrix], grad)

    def swap(group, source, target):
        copy = pltpu.make_async_remote_copy(
            src_ref=source.at[:, 1 - core],
            dst_ref=target,
            send_sem=pair_ssem.at[group],
            recv_sem=pair_rsem.at[group],
            device_id=sibling,
            device_id_type=MESH,
        )
        copy.start()
        return copy

    def to_chips(begin, count, send):
        if count == half and begin % half == 0:

            def post(k, carry):
                other = peer(chip, k, half)
                send(begin + other, other)
                return carry

            loop(1, half, post)
        else:

            def post_any(k, carry):
                index = begin + k
                other = lax.rem(index, half)

                @pl.when(other != chip)
                def _():
                    send(index, other)

                return carry

            loop(0, count, post_any)

    def send_dense(copy, begin, count):
        copy.wait()
        own = pl.ds(begin - dense, count)
        part16[own] = (flat[own, core] + pair_got[own]).astype(bf16)

        def send(index, other):
            pltpu.make_async_remote_copy(
                src_ref=part16.at[index - dense],
                dst_ref=got16.at[index // half, chip],
                send_sem=rs_ssem.at[index // half],
                recv_sem=rs_rsem.at[index // half],
                device_id=place(2 * other + core),
                device_id_type=MESH,
            ).start()

        at = begin
        while at < begin + count:
            step = min(half - at % half, begin + count - at)
            to_chips(at, step, send)
            at = at + step

    def send_wide(copy, which):
        copy.wait()
        for k, piece in enumerate(split(first_f[which, :, core] + first_got[which], 2)):
            wide16[which, :, k] = piece

        def send(index, other):
            pltpu.make_async_remote_copy(
                src_ref=wide16.at[which, index],
                dst_ref=got_wide.at[which, chip],
                send_sem=wd_ssem.at[which],
                recv_sem=wd_rsem.at[which],
                device_id=place(2 * other + core),
                device_id_type=MESH,
            ).start()

        to_chips(0, per_matrix, send)

    def send_low(copy):
        copy.wait()
        low_sum[...] = low_f[:, core] + low_got[...]
        for kind in range(low_kinds):

            def send(index, other, kind=kind):
                pltpu.make_async_remote_copy(
                    src_ref=low_sum.at[index - (1 + kind) * per_matrix],
                    dst_ref=got_low.at[kind, chip],
                    send_sem=low_ssem.at[kind],
                    recv_sem=low_rsem.at[kind],
                    device_id=place(2 * other + core),
                    device_id_type=MESH,
                ).start()

            to_chips((1 + kind) * per_matrix, per_matrix, send)

    def drain_stats(index, rows):
        span = stat_buf.at[index, pl.ds(0, n - 1), pl.ds(0, rows)]
        pltpu.make_async_copy(span, span, stat_ssem.at[index]).wait()

    w_in = w_first[...].reshape(WIDTH, WIDTH)
    mats[0] = w_in
    w_in = mats[0]
    pos_in = pos_first[...].reshape(1024 // LANES, LANES)[0:1].astype(f32)
    lane8 = iota((8, 1), 0)

    def pos_in_col(c):
        return jnp.where(lane8 < 3, row_to_col(pos_in[:, 3 * c : 3 * c + 8], 8), 0.0)

    valid_rows = valid[...].reshape(points // LANES, LANES).astype(f32)
    n_valid = jnp.sum(jnp.sum(valid_rows, axis=0, keepdims=True), axis=1, keepdims=True)
    point_mask = (iota((points, 1), 0).astype(f32) < n_valid).astype(f32)
    lane_mask = (iota((1, points), 1).astype(f32) < n_valid).astype(f32)

    a1 = nn(feat[...], w_in)
    a1_s[...] = a1
    masked = point_mask * a1
    sum_a, sqr_a = row_sum(masked), row_sum(masked * a1)

    weight = [[pos_in[:, 3 * c + d : 3 * c + d + 1] for d in range(3)] for c in range(3)]
    pos_one = [jnp.zeros((NEAREST, LANES), f32) for _ in range(3)]
    pos_two = [jnp.zeros((NEAREST, LANES), f32) for _ in range(3)]
    pairs_local = jnp.zeros((NEAREST, LANES), f32)
    for b in range(blocks):
        here = slice(b * LANES, (b + 1) * LANES)
        index = nbrs[:, here]
        tile, at = lax.shift_right_logical(index, 7), index & (LANES - 1)

        def fetch(c, t):
            row = jnp.broadcast_to(coords[c : c + 1, t * LANES : (t + 1) * LANES], index.shape)
            return jnp.take_along_axis(row, at, axis=1, mode="promise_in_bounds")

        r = []
        for c in range(3):
            near = fetch(c, b)
            if b > 0:
                near = jnp.where(tile < b, fetch(c, b - 1), near)
            if b < blocks - 1:
                near = jnp.where(tile > b, fetch(c, b + 1), near)
            r.append(near - coords[c : c + 1, here])
        pm = jnp.where(index.astype(f32) < n_valid, lane_mask[:, here], 0.0)
        pairs_local = pairs_local + pm
        for d in range(3):
            p = weight[0][d] * r[0] + weight[1][d] * r[1] + weight[2][d] * r[2]
            pos_one[d] = pos_one[d] + pm * p
            pos_two[d] = pos_two[d] + pm * p * p

    def total(value):
        return jnp.sum(row_sum(value), axis=1, keepdims=True)

    lane = iota((1, LANES), 1)
    last = jnp.where(lane == 16, n_valid, 0.0) + jnp.where(lane == 17, total(pairs_local), 0.0)
    for d in range(3):
        last = last + jnp.where(lane == d, total(pos_one[d]), 0.0)
        last = last + jnp.where(lane == 8 + d, total(pos_two[d]), 0.0)

    def fold(row):
        return jnp.concatenate([row[:, 0:LANES], row[:, LANES:WIDTH]], axis=0)

    def unfold(rows):
        return jnp.concatenate([rows[0:1], rows[1:2]], axis=1)

    pl.semaphore_wait(barrier, n - 1)
    collect_first = all_sum(0, jnp.concatenate([fold(sum_a), fold(sqr_a), last], axis=0))
    window_row = iota((WINDOW, LANES), 0)
    for b in range(blocks):
        for j in range(NEAREST):
            index = nbrs[j : j + 1, b * LANES : (b + 1) * LANES] - starts[b]
            onehot[b, 0:WINDOW, j * LANES : (j + 1) * LANES] = jnp.where(
                window_row == index, 1.0, 0.0
            ).astype(bf16)

    coords8 = jnp.concatenate([coords[...], jnp.zeros((5, points), f32)], axis=0)
    table = jnp.concatenate(
        split(coords8, 3) + [jnp.broadcast_to(lane_mask, (8, points)).astype(bf16)], axis=0
    )
    slot0 = (iota((1, PAIRS), 1) < LANES).astype(f32)
    pos_in_cols = [pos_in_col(c) for c in range(3)]
    for b in range(blocks):
        here = slice(b * LANES, (b + 1) * LANES)
        fetched = nn(table[:, starts[b] : starts[b] + WINDOW], onehot[b, 0:WINDOW])
        place_n = fetched[0:8] + fetched[8:16] + fetched[16:24]
        mask_n = fetched[24:32]
        r = place_n - tiles(coords8[:, here])
        pm = mask_n * tiles(lane_mask[:, here])
        p = pos_in_cols[0] * r[0:1] + pos_in_cols[1] * r[1:2] + pos_in_cols[2] * r[2:3]
        rel[b] = r
        pos[b] = p
        pmask[b] = pm
        allow[b] = jnp.maximum(mask_n, slot0)

    for copy in late:
        copy.wait()
    for m in range(1, 5):
        mats[m] = weights[pl.ds(m * SQUARE, SQUARE)].reshape(WIDTH, WIDTH)
    w_q, w_k, w_v, w_o = (mats[m] for m in range(1, 5))
    att_in = weights[pl.ds(OFF_ATT_IN, WIDTH * GROUPS)].reshape(WIDTH * GROUPS // LANES, LANES)
    att_in_f = att_in.astype(f32).reshape(WIDTH, GROUPS)
    att_in_t = att_in_f.T.astype(bf16)
    att_out_f = (
        weights[pl.ds(OFF_ATT_OUT, GROUPS * GROUPS)]
        .reshape(GROUPS * GROUPS // LANES, LANES)
        .astype(f32)
        .reshape(GROUPS, GROUPS)
    )
    att_out = att_out_f.astype(bf16)
    att_out_t = att_out_f.T.astype(bf16)
    tail1d[pl.ds(0, 1024)] = weights[pl.ds(OFF_TAIL, 1024)]
    rest = total_len - OFF_TAIL - 1024
    tail1d[pl.ds(1024, rest)] = weights[pl.ds(OFF_TAIL + 1024, rest)]
    tail = tail1d[pl.ds(0, TAIL_PAD)].reshape(TAIL_PAD // LANES, LANES).astype(f32)
    tail = jnp.concatenate([tail[k : k + 1] for k in range(TAIL_PAD // LANES)], axis=1)
    pos_rows = [tail[:, TAIL_POS_OUT + WIDTH * d : TAIL_POS_OUT + WIDTH * (d + 1)] for d in range(3)]
    def norm_pieces(start):
        ends = [0, WIDTH, WIDTH + 3, WIDTH + 3 + GROUPS, NORMS]
        return [tail[:, start + ends[k] : start + ends[k + 1]] for k in range(4)]

    gain_a, gain_p, gain_w, gain_o = norm_pieces(TAIL_GAINS)
    shift_a, shift_p, shift_w, shift_o = norm_pieces(TAIL_SHIFTS)

    def pad_col(row):
        wide = jnp.concatenate([row, jnp.zeros((1, 5), f32)], axis=1)
        return row_to_col(wide, 8)

    gain_p, shift_p = pad_col(gain_p), pad_col(shift_p)
    gain_w, shift_w = row_to_col(gain_w, GROUPS), row_to_col(shift_w, GROUPS)

    new_at = iota((WIDTH, WIDTH), 0)
    reorder = jnp.where(
        iota((WIDTH, WIDTH), 1) == new_at % GROUPS * PER_GROUP + new_at // GROUPS, 1.0, 0.0
    ).astype(bf16)
    w_o_new = nn(reorder, w_o)
    mats[4] = w_o_new.astype(bf16)
    mats[5] = w_o_new.T.astype(bf16)
    mats[6] = w_q.astype(f32).T.astype(bf16)
    mats[7] = w_k.astype(f32).T.astype(bf16)
    mats[8] = nt(reorder, w_v).astype(bf16)
    pos_mat = jnp.concatenate(pos_rows + [jnp.zeros((13, WIDTH), f32)], axis=0).astype(bf16)
    pos_cols = nt(reorder, pos_mat)
    pos_lanes = jnp.concatenate(
        [pos_cols[:, 0:8]] * 3 + [jnp.zeros((WIDTH, POS_ROWS - 24), f32)], axis=1
    ).astype(bf16)
    pos_cols = [pos_cols[:, d : d + 1] for d in range(3)]
    feat_f = feat[...].astype(f32)
    ft_s[...] = feat_f.T.astype(bf16)
    sum_f = row_sum(point_mask * feat_f)
    stats = collect_first()

    def pick(row, at):
        return jnp.sum(jnp.where(lane == at, row, 0.0), axis=1, keepdims=True)

    point_count, pair_count = pick(stats[4:5], 16), pick(stats[4:5], 17)
    inv_points, inv_pairs = 1.0 / point_count, 1.0 / pair_count

    def moments(total, square, inv):
        mean = total * inv
        return mean, lax.rsqrt(square * inv - mean * mean + bn_eps)

    mean_a, rs_a = moments(unfold(stats[0:2]), unfold(stats[2:4]), inv_points)
    mean_p, rs_p = moments(
        row_to_col(stats[4:5, 0:8], 8), row_to_col(stats[4:5, 8:16], 8), inv_pairs
    )

    h = silu_parts((a1_s[...] - mean_a) * rs_a * gain_a + shift_a)[0]
    h_s[...] = h.astype(bf16)
    h_t = h.T.astype(bf16)
    q_t = nn(mats[6], h_t).astype(bf16)
    k_t = nn(mats[7], h_t).astype(bf16)
    q_s[...] = q_t
    k_s[...] = k_t
    h_ts[...] = h_t
    q_att = nn(att_in_t, q_t)
    k_att = jnp.concatenate(split(nn(att_in_t, k_t), 3), axis=0)
    pos_att = nt(att_in_t, pos_mat)
    none = jnp.zeros((GROUPS, 8), f32)
    pos_ext = [piece.astype(f32) for piece in split(-pos_att[:, 0:8], 3)]
    pos_ext = jnp.concatenate(
        [
            jnp.concatenate([pos_ext[k]] * (3 - k) + [none] * (k + 1), axis=1) for k in range(3)
        ],
        axis=0,
    ).astype(bf16)
    back_att = jnp.concatenate([nn(att_in_t, mats[6]), nn(att_in_t, mats[7])], axis=0)
    back_split = split(back_att, 2)
    ba_s[...] = jnp.concatenate([back_split[0], back_split[0], back_split[1]], axis=0)

    sum_w = jnp.zeros((GROUPS, LANES), f32)
    sqr_w = jnp.zeros((GROUPS, LANES), f32)
    for b in range(blocks):
        here = slice(b * LANES, (b + 1) * LANES)
        active = silu_parts((pos[b] - mean_p) * rs_p * gain_p + shift_p)[0]
        act[b] = active
        pieces = [piece.astype(f32) for piece in split(active, 3)]
        onehot[b, WINDOW : WINDOW + POS_ROWS] = jnp.concatenate(
            pieces + [jnp.zeros((POS_ROWS - 24, PAIRS), f32)], axis=0
        ).astype(bf16)
        fetched = nn(
            jnp.concatenate([k_att[:, starts[b] : starts[b] + WINDOW], pos_ext], axis=1), onehot[b]
        )
        w = tiles(q_att[:, here]) - (
            fetched[0:GROUPS] + fetched[GROUPS : 2 * GROUPS] + fetched[2 * GROUPS : 3 * GROUPS]
        )
        wpre[b] = w
        mw = w * pmask[b, 0:1]
        sum_w = sum_w + lane_fold(mw)
        sqr_w = sqr_w + lane_fold(mw * w)

    def pair_row(one, two):
        one = jnp.sum(one, axis=1, keepdims=True)
        two = jnp.sum(two, axis=1, keepdims=True)
        return col_to_row(one, 0) + col_to_row(two, GROUPS)

    collect_w = all_sum(1, jnp.concatenate([pair_row(sum_w, sqr_w), fold(sum_f)], axis=0))
    v_t = nn(mats[8], h_ts[...]).astype(bf16)
    for b in range(blocks):
        vgat[b] = nn(
            jnp.concatenate([v_t[:, starts[b] : starts[b] + WINDOW], pos_lanes], axis=1), onehot[b]
        )
    stats = collect_w()
    mean_f = stats[1:3] * inv_points
    mean_w, rs_w = moments(
        row_to_col(stats[0:1, 0:GROUPS], GROUPS),
        row_to_col(stats[0:1, GROUPS : 2 * GROUPS], GROUPS),
        inv_pairs,
    )

    def each_channel(value):
        return jnp.concatenate([value] * PER_GROUP, axis=0)

    def over_channels(value):
        return functools.reduce(
            jnp.add, [value[c * GROUPS : (c + 1) * GROUPS] for c in range(PER_GROUP)]
        )

    def cols(j):
        return slice(j * LANES, (j + 1) * LANES)

    for b in range(blocks):
        here = slice(b * LANES, (b + 1) * LANES)
        u = silu_parts((wpre[b] - mean_w) * rs_w * gain_w + shift_w)[0].astype(bf16)
        uact[b] = u
        logit = jnp.where(allow[b, 0:1] > 0.5, nn(att_out_t, u), masked_logit)
        top = logit[:, cols(0)]
        for j in range(1, NEAREST):
            top = jnp.maximum(top, logit[:, cols(j)])
        weight = jnp.exp(logit - tiles(top))
        share = 1.0 / functools.reduce(jnp.add, [weight[:, cols(j)] for j in range(NEAREST)])
        att[b] = weight * tiles(share)
        mixed = jnp.zeros((WIDTH, LANES), f32)
        for j in range(NEAREST):
            mixed = mixed + each_channel(att[b, :, cols(j)]) * vgat[b, :, cols(j)]
        o_s[here, :] = mixed.T.astype(bf16)

    z = nn(o_s[...], mats[4])
    z_s[...] = z
    masked = point_mask * z
    collect_o = all_sum(2, jnp.concatenate([fold(row_sum(masked)), fold(row_sum(masked * z))], axis=0))
    for k in range(2):
        mu_s[k * LANES : (k + 1) * LANES] = jnp.broadcast_to(
            row_to_col(mean_f[k : k + 1], LANES), (LANES, LANES)
        )

    def put_first(which, value):
        put_halves(first_f.at[which], value)
        return swap(which, first_f.at[which], first_got.at[which])

    def from_feat(value):
        return nn(
            jnp.concatenate([ft_s[...]] * 2, axis=1), jnp.concatenate(split(value, 2), axis=0)
        )

    ahat = (a1_s[...] - mean_a) * rs_a
    a1_s[...] = ahat
    ahat_pair = put_first(0, from_feat(point_mask * ahat))
    for b in range(blocks):
        what = (wpre[b] - mean_w) * rs_w
        wpre[b] = what
        y = what * gain_w + shift_w
        dyw[b] = silu_slope(y, silu_parts(y)[1])
    send_wide(ahat_pair, 0)
    o_ts[...] = nn(o_s[...], reorder).T.astype(bf16)
    for b in range(blocks):
        here = slice(b * LANES, (b + 1) * LANES)
        enc = [jnp.zeros((GROUPS, LANES), f32) for _ in range(3)]
        for j in range(NEAREST):
            a = att[b, :, cols(j)]
            for d in range(3):
                enc[d] = enc[d] + a * act[b, d : d + 1, cols(j)]
        bd_s[:, here] = jnp.concatenate(enc, axis=0)
    stats = collect_o()
    mean_o, rs_o = moments(unfold(stats[0:2]), unfold(stats[2:4]), inv_points)

    zhat = (z_s[...] - mean_o) * rs_o
    z_s[...] = zhat
    y = feat[...].astype(f32) + zhat * gain_o + shift_o
    value, gate = silu_parts(y)
    outs[0] = (point_mask * value).astype(bf16)
    store(outs.at[0], out_h)
    dy = point_mask * cot[...].astype(f32) * silu_slope(y, gate)
    dz_s[...] = dy
    shift_grad_o, gain_grad_o = row_sum(dy), row_sum(dy * zhat)
    collect_o = all_sum(3, jnp.concatenate([fold(shift_grad_o), fold(gain_grad_o)], axis=0))
    for b in range(blocks):
        phat = (pos[b] - mean_p) * rs_p
        pos[b] = phat
        y = phat * gain_p + shift_p
        slope_p[b] = silu_slope(y, silu_parts(y)[1])
    y = a1_s[...] * gain_a + shift_a
    slope_a[...] = silu_slope(y, silu_parts(y)[1])
    pos_row = jnp.zeros((1, LANES), f32)
    for c in range(3):
        with_hat, alone = jnp.zeros((8, 1), f32), jnp.zeros((8, 1), f32)
        for b in range(blocks):
            masked = pmask[b] * rel[b, c : c + 1]
            with_hat = with_hat + lane_sum(masked * pos[b])
            alone = alone + lane_sum(masked)
        pos_row = pos_row + col_to_row(with_hat, 64 + 8 * c) + col_to_row(alone, 88 + 8 * c)
    stats = collect_o()
    one, two = unfold(stats[0:2]) * inv_points, unfold(stats[2:4]) * inv_points
    dz = (gain_o * rs_o * (dz_s[...] - point_mask * (one + z_s[...] * two))).astype(bf16)
    dz16[...] = dz
    do_s[...] = nn(dz, mats[5]).T

    sum_w = jnp.zeros((GROUPS, LANES), f32)
    sqr_w = jnp.zeros((GROUPS, LANES), f32)
    for b in range(blocks):
        here = slice(b * LANES, (b + 1) * LANES)
        do = do_s[:, here]
        da = []
        for j in range(NEAREST):
            da.append(over_channels(do * vgat[b, :, cols(j)]))
        mean_da = functools.reduce(jnp.add, [da[j] * att[b, :, cols(j)] for j in range(NEAREST)])
        ds = jnp.concatenate(
            [att[b, :, cols(j)] * (da[j] - mean_da) for j in range(NEAREST)], axis=1
        ).astype(bf16)
        ds_s[b] = ds
        dy = nn(att_out, ds) * dyw[b]
        dyw[b] = dy
        sum_w = sum_w + lane_fold(dy)
        sqr_w = sqr_w + lane_fold(dy * wpre[b])

    back_w = pair_row(sum_w, sqr_w)
    collect_w = all_sum(4, back_w + pos_row)
    put_matrix(4, nn(o_ts[...], dz16[...]))
    o_flat, v_flat = pl.ds(per_matrix, per_matrix), pl.ds(0, per_matrix)
    o_pair = swap(2, flat.at[o_flat], pair_got.at[o_flat])
    add_groups = jnp.where(
        iota((8, 3 * GROUPS), 1) // GROUPS == iota((8, 3 * GROUPS), 0), 1.0, 0.0
    ).astype(bf16)
    dv_s[...] = jnp.zeros(dv_s.shape, f32)
    for b in range(blocks):
        here = slice(b * LANES, (b + 1) * LANES)
        do = do_s[:, here]
        for j in range(NEAREST):
            xs[b, :, cols(j)] = (each_channel(att[b, :, cols(j)]) * do).astype(bf16)
        mix = [
            (tiles(over_channels(do * pos_cols[d])) * att[b]).astype(bf16) for d in range(3)
        ]
        dmix[b] = nn(add_groups, jnp.concatenate(mix, axis=0))
        dv_s[pl.ds(starts[b], WINDOW)] += nt(onehot[b, 0:WINDOW], xs[b])
    dv = dv_s[...].astype(bf16)
    dv_s[...] = nn(dv, mats[8])
    put_matrix(3, nn(h_ts[...], nn(dv, reorder).astype(bf16)))
    v_pair = swap(5, flat.at[v_flat], pair_got.at[v_flat])
    send_dense(o_pair, dense + per_matrix, per_matrix)
    send_dense(v_pair, dense, per_matrix)
    stats = collect_w()
    one = row_to_col(stats[:, 0:GROUPS], GROUPS) * inv_pairs
    two = row_to_col(stats[:, GROUPS : 2 * GROUPS], GROUPS) * inv_pairs
    pos_hat = [row_to_col(stats[:, 64 + 8 * c : 72 + 8 * c], 8) for c in range(3)]
    pos_alone = [row_to_col(stats[:, 88 + 8 * c : 96 + 8 * c], 8) for c in range(3)]

    sk_s[...] = jnp.zeros(sk_s.shape, f32)
    pos_att_rows = split(pos_att[:, 0:8].T, 3)
    pos_att_rows = jnp.concatenate(pos_att_rows, axis=0)
    dw_sums = []
    for b in range(blocks):
        dw = (gain_w * rs_w * (dyw[b] - pmask[b, 0:1] * (one + wpre[b] * two))).astype(bf16)
        sk_s[pl.ds(starts[b], WINDOW)] += nt(onehot[b, 0:WINDOW], dw)
        dw_sums.append(lane_slots(dw.astype(f32)))
        dw_s[b] = dw
    dq_att = jnp.concatenate(dw_sums, axis=1)
    both_att = jnp.concatenate([dq_att.T, -sk_s[...]], axis=1)
    both_split = split(both_att, 2)
    dh = nn(jnp.concatenate(both_split + both_split[0:1], axis=1), ba_s[...]) + dv_s[...]
    dy = dh * slope_a[...]
    z_s[...] = dy
    shift_grad_a = row_sum(dy)
    away = jnp.concatenate(
        [mu_s[...] * shift_grad_a[:, k * LANES : (k + 1) * LANES] for k in range(2)], axis=1
    )
    first_pair = put_first(1, from_feat(dy) - away)
    low = nn(
        jnp.concatenate([h_ts[...]] * 2, axis=1), jnp.concatenate(both_split, axis=0)
    )
    low_f[...] = low.reshape(per_matrix, 2, LOW_ROWS, LANES)
    low_pair = swap(3, low_f, low_got)
    along = [jnp.zeros((8, 1), f32) for _ in range(3)]
    sum_p = jnp.zeros((8, 1), f32)
    sqr_p = jnp.zeros((8, 1), f32)
    for b in range(blocks):
        back = nn(pos_att_rows, dw_s[b])
        d_act = dmix[b] + back[0:8] + back[8:16] + back[16:24]
        dy = d_act * slope_p[b]
        sum_p = sum_p + lane_sum(dy)
        sqr_p = sqr_p + lane_sum(dy * pos[b])
        for c in range(3):
            along[c] = along[c] + lane_sum(dy * rel[b, c : c + 1])
    gain_grad_a = row_sum(z_s[...] * a1_s[...])
    last = col_to_row(sum_p, 0) + col_to_row(sqr_p, 8)
    for c in range(3):
        last = last + col_to_row(along[c], 16 + 8 * c)
    collect_a = all_sum(
        5, jnp.concatenate([fold(shift_grad_a), fold(gain_grad_a), last], axis=0)
    )
    send_wide(first_pair, 1)
    send_low(low_pair)

    d_att_out = sum(nt(uact[b], ds_s[b]) for b in range(blocks))
    d_pos_att = sum(
        nt(jnp.concatenate(split(act[b], 3), axis=0), dw_s[b]) for b in range(blocks)
    )
    d_pos_att = d_pos_att[0:8] + d_pos_att[8:16] + d_pos_att[16:24]
    d_pos_split = split(d_pos_att, 3)
    d_att_in = sum(
        nn(q_s[...], piece[:, 0:GROUPS]) + nn(k_s[...], piece[:, GROUPS : 2 * GROUPS])
        for piece in both_split
    )
    d_att_in = d_att_in + sum(tn(pos_mat[0:8], piece) for piece in d_pos_split)
    d_pos_out = sum(nn(piece, att_in_t) for piece in d_pos_split)
    do_split = split(do_s[...], 2)
    bd_split = split(bd_s[...], 2)
    cross = nt(bd_split[0], do_split[0]) + nt(bd_split[0], do_split[1]) + nt(bd_split[1], do_split[0])
    own_group = iota((GROUPS, WIDTH), 1) % GROUPS == iota((GROUPS, WIDTH), 0)
    cross = [
        row_sum(jnp.where(own_group, cross[d * GROUPS : (d + 1) * GROUPS], 0.0)) for d in range(3)
    ]
    cross = jnp.concatenate(cross + [jnp.zeros((5, WIDTH), f32)], axis=0)
    d_pos_out = d_pos_out + sum(nn(piece, reorder) for piece in split(cross, 3))
    d_pos_rows = [d_pos_out[d : d + 1] for d in range(3)]
    pieces = [jnp.zeros((1, TAIL_POS_OUT), f32)] + d_pos_rows
    pieces = pieces + [
        gain_grad_a, col_to_row(sqr_p, 0)[:, 0:3], back_w[:, GROUPS : 2 * GROUPS], gain_grad_o,
        shift_grad_a, col_to_row(sum_p, 0)[:, 0:3], back_w[:, 0:GROUPS], shift_grad_o,
        jnp.zeros((1, TAIL_PAD - TAIL_USED), f32),
    ]
    small = 5 * per_matrix
    used_rows = OFF_TAIL // LANES + TAIL_PAD // LANES - 5 * SQUARE // LANES
    spare_rows = (sliced - small) * 2 * SLICE_ROWS - used_rows
    pieces_rows = [
        d_att_in.reshape(WIDTH * GROUPS // LANES, LANES),
        d_att_out.reshape(GROUPS * GROUPS // LANES, LANES),
        jnp.concatenate(pieces, axis=1).reshape(TAIL_PAD // LANES, LANES),
        jnp.zeros((spare_rows, LANES), f32),
    ]
    flat[small - dense : sliced - dense] = jnp.concatenate(pieces_rows, axis=0).reshape(
        sliced - small, 2, SLICE_ROWS, LANES
    )
    small_flat = pl.ds(small - dense, sliced - small)
    small_pair = swap(4, flat.at[small_flat], pair_got.at[small_flat])
    send_dense(small_pair, small, sliced - small)

    begin = me * shard_len
    lead, skip = lax.rem(begin, CHUNK), lax.rem(begin, LANES)
    shard_at = pl.ds(lead // LANES, shard_rows)
    lanes_all = iota((shard_rows, LANES), 1)
    inside = iota((shard_rows, LANES), 0) * LANES + lanes_all < shard_len
    main = shard_len // 1024 * 1024
    parts = [pl.ds(at, size) for at, size in ((0, main), (main, shard_len - main)) if size]
    for k in range(3):
        for at in parts:
            tail_g[at] = state[k][at]
        rows = jnp.where(inside, tail_g[...].reshape(shard_rows, LANES), 0.0)
        turned = pltpu.roll(rows, skip, 1)
        above = pltpu.roll(turned, 1, 0)
        slab_f[k] = jnp.zeros(slab_f.shape[1:], f32)
        slab_f[k, shard_at, :] = jnp.where(lanes_all < skip, above, turned)

    stats = collect_a()
    one_a, two_a = unfold(stats[0:2]) * inv_points, unfold(stats[2:4]) * inv_points
    def halves(row):
        return jnp.concatenate(
            [
                jnp.broadcast_to(row[:, k * LANES : (k + 1) * LANES], (SLICE_ROWS // 2, LANES))
                for k in range(2)
            ],
            axis=0,
        )

    scale_tile, two_tile = halves(gain_a * rs_a), halves(two_a)
    one = row_to_col(stats[4:5, 0:8], 8) * inv_pairs
    two = row_to_col(stats[4:5, 8:16], 8) * inv_pairs
    pos_in_row = jnp.zeros((1, LANES), f32)
    for c in range(3):
        moved = row_to_col(stats[4:5, 16 + 8 * c : 24 + 8 * c], 8)
        moved = gain_p * rs_p * (moved - one * pos_alone[c] - two * pos_hat[c])
        pos_in_row = pos_in_row + col_to_row(moved, 3 * c)

    def slice_of(slot):
        return 2 * (slot * half + chip) + core

    def when_in(slot, low, high, act_on):
        if (slot + 1) * n <= low or slot * n >= high:
            return
        if slot * n >= low and (slot + 1) * n <= high:
            act_on()
        else:
            number = slice_of(slot)
            pl.when((number >= low) & (number < high))(act_on)

    def others_sum(total, part):
        def add(k, total):
            return total + part(peer(chip, k, half))

        return lax.fori_loop(1, half, add, total, unroll=half <= 16)

    def take_wide(which):
        got = got_wide.at[which, pl.ds(0, half - 1)]
        pltpu.make_async_copy(got, got, wd_rsem.at[which]).wait()
        index = lax.rem(chip, per_matrix)

        def part(other):
            return got_wide[which, other, 0].astype(f32) + got_wide[which, other, 1].astype(f32)

        return others_sum(first_f[which, index, core] + first_got[which, index], part)

    def take_low(kind):
        got = got_low.at[kind, pl.ds(0, half - 1)]
        pltpu.make_async_copy(got, got, low_rsem.at[kind]).wait()
        index = lax.rem(chip, per_matrix)
        return others_sum(low_sum[index], lambda other: got_low[kind, other])

    def low_product(factor, which):
        factor = factor.reshape(SLICE // WIDTH, 2 * GROUPS)[:, which * GROUPS : (which + 1) * GROUPS]
        return sum(nn(piece, att_in_t) for piece in split(factor, 2)).reshape(SLICE_ROWS, LANES)

    squares = jnp.zeros((SLICE_ROWS, LANES), f32)
    matrix = SQUARE // SLICE
    for slot in range(slots):
        sums[slot] = jnp.zeros((SLICE_ROWS, LANES), f32)

    def take_dense(in_order, slot):
        index = slot * half + chip
        got = got16.at[slot, pl.ds(0, half - 1)]
        pltpu.make_async_copy(got, got, rs_rsem.at[slot]).wait()
        total = flat[index - dense, core] + pair_got[index - dense]
        total = others_sum(total, lambda other: got16[slot, other].astype(f32))
        sums[slot] = total if in_order else whole_rows(total)

    def take_hat():
        hat_s[...] = two_tile * take_wide(0)

    def first(slot):
        sums[slot] = whole_rows(scale_tile * (take_wide(1) - hat_s[...]))

    def add_pos_in(slot):
        at_row = iota((SLICE_ROWS, LANES), 0) == OFF_TAIL % SLICE // LANES
        sums[slot] += jnp.where(at_row, pos_in_row, 0.0)

    def each_slot(low, high, act_on):
        for slot in range(slots):
            when_in(slot, low, high, functools.partial(act_on, slot))

    each_slot(DENSE_FROM * matrix, 5 * matrix, functools.partial(take_dense, False))
    each_slot(0, matrix, lambda slot: take_hat())
    each_slot(0, matrix, first)
    for kind in range(low_kinds):
        kinds = range(2) if low_kinds == 1 else (kind,)

        def fill(kind=kind, kinds=kinds):
            factor = take_low(kind)
            for which in kinds:
                for slot in range(slots):

                    def product(slot=slot, which=which):
                        sums[slot] = low_product(factor, which)

                    when_in(slot, (1 + which) * matrix, (2 + which) * matrix, product)

        if low_kinds == 1:
            fill()
        else:
            when_in(0, (1 + kind) * matrix, (2 + kind) * matrix, fill)
    each_slot(5 * matrix, 2 * sliced, functools.partial(take_dense, True))
    each_slot(OFF_TAIL // SLICE, OFF_TAIL // SLICE + 1, add_pos_in)
    for slot in range(slots):
        squares = squares + sums[slot] * sums[slot]
    squares = total(squares)

    collect_norm = all_sum(6, jnp.where(lane == 0, squares, 0.0))

    def each_owner(slot, act_on):
        number = slice_of(slot)
        low = number * SLICE // shard_len
        high = jnp.minimum((number * SLICE + SLICE - 1) // shard_len, n - 1)
        for side in range(sides):
            owner = low + side

            @pl.when((number * SLICE < total_len) & (owner <= high))
            def _(owner=owner, side=side):
                act_on(owner, number - owner * shard_len // SLICE, side)

    def owned_rows(k):
        return owned.at[pl.ds(pl.multiple_of(k * SLICE_ROWS, SLICE_ROWS), SLICE_ROWS)]

    def own_copy(slot, owner, k, side):
        return pltpu.make_async_remote_copy(
            src_ref=sums.at[slot],
            dst_ref=owned_rows(k),
            send_sem=own_ssem.at[slot, side],
            recv_sem=own_rsem.at[k],
            device_id=place(owner),
            device_id_type=MESH,
        )

    for slot in range(slots):

        def hand_over(owner, k, side, slot=slot):
            @pl.when(owner != me)
            def _():
                own_copy(slot, owner, k, side).start()

            @pl.when(owner == me)
            def _():
                owned_rows(k)[...] = sums[slot]

        each_owner(slot, hand_over)

    first_slice = begin // SLICE
    last_slice = (begin + shard_len - 1) // SLICE
    for k in range(span):
        number = first_slice + k

        @pl.when((number <= last_slice) & (lax.rem(number, n) != me))
        def _(k=k):
            rows = owned.at[pl.ds(k * SLICE_ROWS, SLICE_ROWS)]
            pltpu.make_async_copy(rows, rows, own_rsem.at[k]).wait()

    slab_shape = slab_f.shape[1:]
    flat_at = iota(slab_shape, 0) * LANES + iota(slab_shape, 1) - lead
    grad = owned[pl.ds((begin - lead - first_slice * SLICE) // LANES, slab_shape[0]), :]
    grad = jnp.where((flat_at >= 0) & (flat_at < shard_len), grad, 0.0)

    stats = collect_norm()
    norm = jnp.sqrt(pick(stats, 0))
    grad = grad * jnp.minimum(1.0, clip_norm / norm)
    updated = adam(slab_f[0], slab_f[1], slab_f[2], grad)
    shard_w[...] = updated[0].astype(bf16)
    all_w[core, chip] = updated[0].astype(bf16)
    norm_s[...] = jnp.broadcast_to(norm, norm_s.shape)

    in_row = n_cols // 2
    row_chip = col_id // 2

    def send_slab(source, slab, row, chip_in_row):
        pltpu.make_async_remote_copy(
            src_ref=source,
            dst_ref=all_w.at[core, slab],
            send_sem=ag_ssem,
            recv_sem=ag_rsem.at[slab],
            device_id=(row, 2 * chip_in_row + core),
            device_id_type=MESH,
        ).start()

    def forward(other):
        pltpu.make_async_remote_copy(
            src_ref=all_w.at[core, other],
            dst_ref=all_w.at[core, other],
            send_sem=fw_ssem,
            recv_sem=fw_rsem,
            device_id=sibling,
            device_id_type=MESH,
        ).start()

    def arrived(other):
        pltpu.make_async_copy(shard_w, shard_w, ag_rsem.at[other]).wait()

    def send_along(k, carry):
        send_slab(shard_w, chip, peer(row_id, k, n_rows), row_chip)
        return carry

    def send_within(k, carry):
        send_slab(shard_w, chip, row_id, peer(row_chip, k, in_row))
        return carry

    loop(1, n_rows, send_along)
    loop(1, in_row, send_within)
    forward(chip)
    store(norm_s, gnorm_h)
    for k in range(3):
        slab_f[k] = updated[k]
        turned = pltpu.roll(slab_f[k, shard_at, :], lax.rem(LANES - skip, LANES), 1)
        below = pltpu.roll(turned, shard_rows - 1, 0)
        tail_g[...] = jnp.where(lanes_all < LANES - skip, turned, below).reshape(shard_rows * LANES)
        for at in parts:
            news[k][at] = tail_g[at]
    for source, target in ((0, new_master_h), (1, new_first_h), (2, new_second_h)):
        store(news[source], target)

    da1 = (gain_a * rs_a * (z_s[...] - point_mask * (one_a + a1_s[...] * two_a))).astype(bf16)
    outs[1] = (dz_s[...] + nt(da1, w_in)).astype(bf16)
    store(outs.at[1], gfeat_h)
    for index, rows in sent:
        drain_stats(index, rows)

    def drain(low, high, slices, sem):
        if high - low == half:
            rest = slices.at[pl.ds(0, half - 1)]
            pltpu.make_async_copy(rest, rest, sem).wait()
        else:
            inside = (chip >= low) & (chip < high)

            def wait_one(k, carry):
                pltpu.make_async_copy(slices.at[0], slices.at[0], sem).wait()
                return carry

            lax.fori_loop(0, high - low - inside.astype(jnp.int32), wait_one, 0)

    for which in range(2):
        drain(0, per_matrix, got_wide.at[which], wd_ssem.at[which])
    for kind in range(low_kinds):
        low_at = (1 + kind) * per_matrix % half
        drain(low_at, low_at + per_matrix, got_low.at[kind], low_ssem.at[kind])
    for slot in range(slots):
        low_at = max(dense - slot * half, 0)
        high_at = min(sliced - slot * half, half)
        if high_at > low_at:
            drain(low_at, high_at, got16.at[slot], rs_ssem.at[slot])

        def own_drain(owner, k, side, slot=slot):
            @pl.when(owner != me)
            def _():
                own_copy(slot, owner, k, side).wait_send()

        each_owner(slot, own_drain)
    for copy in stores:
        copy.wait()

    def spread_row(k, carry):
        other = peer(row_id, n_rows - k, n_rows) * in_row + row_chip
        arrived(other)

        def send_on(i, carry):
            send_slab(all_w.at[core, other], other, row_id, peer(row_chip, i, in_row))
            return carry

        loop(1, in_row, send_on)
        forward(other)
        return carry

    loop(1, n_rows, spread_row)

    def pass_on(k, carry):
        step = k // (in_row - 1)
        row = jnp.where(step == 0, row_id, peer(row_id, n_rows - step, n_rows))
        other = row * in_row + peer(row_chip, in_row - 1 - lax.rem(k, in_row - 1), in_row)
        arrived(other)
        forward(other)
        return carry

    loop(0, n_rows * (in_row - 1), pass_on)
    pltpu.make_async_copy(all_w.at[core], all_w.at[core], fw_rsem).wait()
    rows = CHUNK // LANES

    def chunk(c):
        value = None
        last_owner = min((c * CHUNK + CHUNK - 1) // shard_len, n - 1)
        for owner in range(c * CHUNK // shard_len, last_owner + 1):
            k = c - owner * shard_len // CHUNK
            part = all_w[owner % 2, owner // 2, rows * k : rows * (k + 1)].astype(f32)
            value = part if value is None else value + part
        return value

    whole = total_len // (2 * CHUNK)
    for c in range(whole):
        both = jnp.concatenate([chunk(2 * c), chunk(2 * c + 1)], axis=0)
        weights_out[pl.ds(2 * CHUNK * c, 2 * CHUNK)] = both.astype(bf16).reshape(2 * CHUNK)
    left = total_len - whole * 2 * CHUNK
    if left:
        parts = [chunk(2 * whole)]
        parts.append(chunk(2 * whole + 1) if left > CHUNK else jnp.zeros((rows, LANES), f32))
        both = jnp.concatenate(parts, axis=0).astype(bf16).reshape(2 * CHUNK)
        weights_out[pl.ds(2 * CHUNK * whole, left)] = both[0:left]

    pltpu.make_async_copy(all_w.at[core], all_w.at[core], fw_ssem).wait()
    rest = all_w.at[core, pl.ds(0, half - 1)]
    pltpu.make_async_copy(rest, rest, ag_ssem).wait()


def finish_kernel(
    out_t, gfeat_t, gnorm_t, master_t, first_t, second_t, weights_t,
    out_h, gfeat_h, gnorm_h, master_h, first_h, second_h, weights_h,
    norm_s, gnorm, sem,
):
    copies = [
        pltpu.make_async_copy(source, target, sem.at[k])
        for k, (source, target) in enumerate(
            (
                (weights_t, weights_h),
                (out_t, out_h),
                (gfeat_t, gfeat_h),
                (master_t, master_h),
                (first_t, first_h),
                (second_t, second_h),
                (gnorm_t, norm_s),
            )
        )
    ]
    for copy in copies:
        copy.start()
    copies[-1].wait()
    gnorm[...] = norm_s[0:1, 0:1]
    copies[-1] = pltpu.make_async_copy(gnorm, gnorm_h, sem.at[len(copies)])
    copies[-1].start()
    for copy in copies:
        copy.wait()


def lane_slots(value):
    return functools.reduce(
        jnp.add, [value[:, j * LANES : (j + 1) * LANES] for j in range(NEAREST)]
    )


def shards(
    n_rows, n_cols,
    features, coords, valid_mask, neighbors, cotangent, weights, master, first_moment, second_moment,
):
    n = n_rows * n_cols
    half = n // 2
    points = features.shape[0]
    blocks = points // LANES
    shard_len = master.shape[0]
    total_len = weights.shape[0]

    def up(value, unit):
        return -(-value // unit) * unit

    shard_rows = up(-(-shard_len // LANES) + 1, 8)
    slab_rows = up(shard_rows + CHUNK // LANES, 16)
    sliced = up(-(-total_len // SLICE), 2) // 2
    slots = -(-sliced // half)
    per_matrix = SQUARE // SLICE // 2
    dense_pairs = sliced - DENSE_FROM * per_matrix
    low_kinds = 1 if per_matrix % half == 0 else 2
    sides = (SLICE + shard_len - 2) // shard_len + 1
    span = (SLICE + shard_len - 2) // SLICE + 1
    hbm = pl.BlockSpec(memory_space=pltpu.HBM)
    vmem = pl.BlockSpec(memory_space=pltpu.VMEM)
    dma = pltpu.SemaphoreType.DMA
    shape = jax.ShapeDtypeStruct

    def pairs(rows, dtype=f32):
        return pltpu.VMEM((blocks, rows, PAIRS), dtype)

    def shard():
        return [pltpu.VMEM(master.shape, f32) for _ in range(3)]

    scratch = [
        pltpu.VMEM(features.shape, bf16),
        pltpu.VMEM(coords.shape, f32),
        pltpu.VMEM(valid_mask.shape, jnp.int32),
        pltpu.VMEM(neighbors.shape, jnp.int32),
        pltpu.VMEM(features.shape, bf16),
        pltpu.VMEM((SQUARE,), bf16),
        pltpu.VMEM((1024,), bf16),
        pltpu.VMEM(weights.shape, bf16),
        shard(),
        shard(),
        pltpu.VMEM((2, *features.shape), bf16),
        pltpu.VMEM((1, LANES), f32),
        dma((11,)),
        dma((7,)),
        pltpu.VMEM((7, 8, LANES), f32),
        pltpu.VMEM((7, n, 8, LANES), f32),
        dma((7,)),
        dma((7,)),
        pltpu.VMEM((TAIL_PAD,), bf16),
        pltpu.VMEM((9, WIDTH, WIDTH), bf16),
        pairs(WINDOW + POS_ROWS, bf16),
        pairs(WIDTH),
        pairs(GROUPS),
        pairs(GROUPS),
        pairs(GROUPS, bf16),
        pairs(GROUPS),
        pairs(8),
        pairs(8),
        pairs(8),
        pairs(8),
        pairs(8),
        pairs(8),
        pltpu.VMEM((WIDTH, points), bf16),
        pltpu.VMEM((points, WIDTH), f32),
        pairs(8),
        pltpu.VMEM((points, WIDTH), f32),
        pltpu.VMEM((points, WIDTH), f32),
        pltpu.VMEM((points, WIDTH), bf16),
        pltpu.VMEM((WIDTH, points), bf16),
        pltpu.VMEM((WIDTH, points), bf16),
        pltpu.VMEM((WIDTH, points), bf16),
        pltpu.VMEM((6 * GROUPS, WIDTH), bf16),
        pltpu.VMEM((points, WIDTH), bf16),
        pltpu.VMEM((WIDTH, points), bf16),
        pltpu.VMEM((WIDTH, points), f32),
        pltpu.VMEM((points, WIDTH), f32),
        pltpu.VMEM((points, GROUPS), f32),
        pltpu.VMEM((3 * GROUPS, points), f32),
        pairs(GROUPS, bf16),
        pairs(GROUPS, bf16),
        pairs(WIDTH, bf16),
        pltpu.VMEM((points, WIDTH), f32),
        pltpu.VMEM((points, WIDTH), bf16),
        pltpu.VMEM((WIDTH, LANES), f32),
        pltpu.VMEM((dense_pairs, 2, SLICE_ROWS, LANES), f32),
        pltpu.VMEM((dense_pairs, SLICE_ROWS, LANES), f32),
        pltpu.VMEM((dense_pairs, SLICE_ROWS, LANES), bf16),
        pltpu.VMEM((slots, half, SLICE_ROWS, LANES), bf16),
        pltpu.VMEM((2, per_matrix, 2, SLICE_ROWS, LANES), f32),
        pltpu.VMEM((2, per_matrix, SLICE_ROWS, LANES), f32),
        pltpu.VMEM((2, per_matrix, 2, SLICE_ROWS, LANES), bf16),
        pltpu.VMEM((2, half, 2, SLICE_ROWS, LANES), bf16),
        pltpu.VMEM((per_matrix, 2, LOW_ROWS, LANES), f32),
        pltpu.VMEM((per_matrix, LOW_ROWS, LANES), f32),
        pltpu.VMEM((per_matrix, LOW_ROWS, LANES), f32),
        pltpu.VMEM((low_kinds, half, LOW_ROWS, LANES), f32),
        pltpu.VMEM((SLICE_ROWS, LANES), f32),
        pltpu.VMEM((slots, SLICE_ROWS, LANES), f32),
        pltpu.VMEM((up(max(span * SLICE_ROWS, CHUNK // LANES + slab_rows), SLICE_ROWS), LANES), f32),
        pltpu.VMEM((shard_rows * LANES,), f32),
        pltpu.VMEM((3, slab_rows, LANES), f32),
        pltpu.VMEM((slab_rows, LANES), bf16),
        pltpu.VMEM((2, half, slab_rows, LANES), bf16),
        dma((6,)),
        dma((6,)),
        dma((slots,)),
        dma((slots,)),
        dma((2,)),
        dma((2,)),
        dma((low_kinds,)),
        dma((low_kinds,)),
        dma((slots, sides)),
        dma((span,)),
        dma,
        dma((half,)),
        dma,
        dma,
    ]
    results = pl.pallas_call(
        functools.partial(block_kernel, n_rows, n_cols),
        out_shape=(
            shape(features.shape, bf16),
            shape(features.shape, bf16),
            shape((1, LANES), f32),
            shape(master.shape, f32),
            shape(master.shape, f32),
            shape(master.shape, f32),
            pltpu.VMEM(weights.shape, bf16),
        ),
        in_specs=[hbm] * 9,
        out_specs=[pl.BlockSpec(memory_space=pl.ANY)] * 6 + [vmem],
        scratch_shapes=scratch,
        compiler_params=pltpu.CompilerParams(
            collective_id=0, has_side_effects=True, vmem_limit_bytes=48 * 2**20
        ),
    )(*(pltpu.with_memory_space_constraint(x, pltpu.HBM) for x in (features, coords, valid_mask, neighbors, cotangent, weights, master, first_moment, second_moment)))
    results = pl.pallas_call(
        finish_kernel,
        out_shape=(
            shape(features.shape, bf16),
            shape(features.shape, bf16),
            shape((1, 1), f32),
            shape(master.shape, f32),
            shape(master.shape, f32),
            shape(master.shape, f32),
            shape(weights.shape, bf16),
        ),
        in_specs=[pl.BlockSpec(memory_space=pl.ANY)] * 7,
        out_specs=[hbm] * 7,
        scratch_shapes=[pltpu.VMEM((1, LANES), f32), pltpu.VMEM((1, 1), f32), dma((8,))],
        compiler_params=pltpu.CompilerParams(vmem_limit_bytes=8 * 2**20),
    )(*results)
    return results[0], results[1], results[2].reshape(()), *results[3:]


def solution(mesh):
    both = ("rows", "cols")
    rows_split, cols_split, flat_split = P(both, None), P(None, both), P(both)
    return jax.shard_map(
        functools.partial(shards, mesh.shape["rows"], mesh.shape["cols"]),
        mesh=mesh,
        in_specs=(
            rows_split, cols_split, flat_split, cols_split, rows_split, P(),
            flat_split, flat_split, flat_split,
        ),
        out_specs=(rows_split, rows_split, P(), flat_split, flat_split, flat_split, P()),
        check_vma=False,
    )
```

```python
import functools

import jax
import jax.numpy as jnp
from jax import lax
from jax.experimental import pallas as pl
from jax.experimental.pallas import tpu as pltpu
from jax.sharding import PartitionSpec as P

WIDTH = 256
GROUPS = 32
NEAREST = 16
PER_GROUP = WIDTH // GROUPS
LANES = 128
WINDOW = 256
PAIRS = NEAREST * LANES

SQUARE = WIDTH * WIDTH
OFF_ATT_IN = 5 * SQUARE
OFF_ATT_OUT = OFF_ATT_IN + WIDTH * GROUPS
OFF_TAIL = OFF_ATT_OUT + GROUPS * GROUPS
NORMS = 2 * WIDTH + 3 + GROUPS
TAIL_POS_OUT = 9
TAIL_GAINS = TAIL_POS_OUT + 3 * WIDTH
TAIL_SHIFTS = TAIL_GAINS + NORMS
TAIL_USED = TAIL_SHIFTS + NORMS
TAIL_PAD = 2048
SLICE = 2048
SLICE_ROWS = SLICE // LANES
LOW_ROWS = SLICE // WIDTH * 2 * GROUPS // LANES
DENSE_FROM = 3
CHUNK = 1024
POS_ROWS = 32

bn_eps = 1e-05
clip_norm = 0.01
learn_rate = 0.05
beta_one = 0.9
beta_two = 0.999
adam_eps = 1e-08
decay_rate = 0.01
step_count = 10
masked_logit = -1000000000.0

f32 = jnp.float32
bf16 = jnp.bfloat16
MESH = pl.DeviceIdType.MESH


def contract(a, b, left, right):
    return lax.dot_general(a, b, (((left,), (right,)), ((), ())), preferred_element_type=f32)


def nn(a, b):
    return contract(a, b, 1, 0)


def nt(a, b):
    return contract(a, b, 1, 1)


def tn(a, b):
    return contract(a, b, 0, 0)


def split(value, parts):
    pieces = []
    for _ in range(parts):
        piece = value.astype(bf16)
        pieces.append(piece)
        value = value - piece.astype(f32)
    return pieces


def silu_parts(value):
    gate = 0.5 * jnp.tanh(0.5 * value) + 0.5
    return value * gate, gate


def silu_slope(value, gate):
    return gate * (1.0 + value * (1.0 - gate))


def iota(shape, dim):
    return lax.broadcasted_iota(jnp.int32, shape, dim)


def loop(begin, end, body):
    if end - begin <= 31:
        for k in range(begin, end):
            body(k, 0)
    else:
        lax.fori_loop(begin, end, body, 0)


def row_to_col(row, count):
    wide = jnp.broadcast_to(row, (count, row.shape[1]))
    same = iota(wide.shape, 0) == iota(wide.shape, 1)
    return jnp.sum(jnp.where(same, wide, 0.0), axis=1, keepdims=True)


def col_to_row(col, offset):
    wide = jnp.broadcast_to(col, (col.shape[0], LANES))
    same = iota(wide.shape, 0) + offset == iota(wide.shape, 1)
    return jnp.sum(jnp.where(same, wide, 0.0), axis=0, keepdims=True)


def row_sum(value):
    return jnp.sum(value, axis=0, keepdims=True)


def lane_fold(value):
    total = value[:, 0:LANES]
    for k in range(1, value.shape[1] // LANES):
        total = total + value[:, k * LANES : (k + 1) * LANES]
    return total


def lane_sum(value):
    return jnp.sum(lane_fold(value), axis=1, keepdims=True)


def tiles(value):
    return jnp.concatenate([value] * NEAREST, axis=1)


def adam(param, moment, second, grad):
    moment_new = beta_one * moment + (1.0 - beta_one) * grad
    second_new = beta_two * second + (1.0 - beta_two) * grad * grad
    moment_hat = moment_new / (1.0 - beta_one**step_count)
    second_hat = second_new / (1.0 - beta_two**step_count)
    param_new = param - learn_rate * (
        moment_hat / (jnp.sqrt(second_hat) + adam_eps) + decay_rate * param
    )
    return param_new, moment_new, second_new


def peer(me, step, count):
    if count & (count - 1) == 0:
        return me ^ (count - step)
    return lax.rem(me + step, count)


def block_kernel(
    n_rows, n_cols,
    feat_h, coords_h, valid_h, nbrs_h, cot_h, weights_h, master_h, first_h, second_h,
    out_h, gfeat_h, gnorm_h, new_master_h, new_first_h, new_second_h, weights_out,
    feat, coords, valid, nbrs, cot, w_first, pos_first, weights, state, news, outs, norm_s, in_sem, out_sem,
    stat_send, stat_buf, stat_ssem, stat_rsem,
    tail1d, mats, onehot, vgat, att, wpre, uact, dyw, rel, pos, act, pmask, allow, dmix,
    ft_s, slope_a, slope_p, a1_s, z_s, h_s, h_ts, q_s, k_s, ba_s, o_s, o_ts, do_s, dv_s, sk_s, bd_s, ds_s, dw_s, xs, dz_s, dz16,
    mu_s, flat, pair_got, part16, got16, first_f, first_got, wide16, got_wide, low_f, low_got, low_sum, got_low, hat_s, sums, owned, tail_g, slab_f, shard_w, all_w,
    pair_ssem, pair_rsem, rs_ssem, rs_rsem, wd_ssem, wd_rsem, low_ssem, low_rsem, own_ssem, own_rsem, ag_ssem, ag_rsem, fw_ssem, fw_rsem,
):
    n = n_rows * n_cols
    half = n // 2
    row_id, col_id = lax.axis_index("rows"), lax.axis_index("cols")
    me = row_id * n_cols + col_id
    core = lax.rem(col_id, 2)
    chip = me // 2
    points = feat.shape[0]
    blocks = points // LANES
    starts = [min(max(LANES * b - (WINDOW - LANES) // 2, 0), points - WINDOW) for b in range(blocks)]
    total_len = weights.shape[0]
    shard_len = master_h.shape[0]
    shard_rows = -(-tail_g.shape[0] // LANES)
    per_matrix = SQUARE // SLICE // 2
    dense = DENSE_FROM * per_matrix
    sliced = dense + flat.shape[0]
    slots = got16.shape[0]
    low_kinds = got_low.shape[0]
    sides = own_ssem.shape[1]
    span = own_rsem.shape[0]

    def place(device):
        return (device // n_cols, lax.rem(device, n_cols))

    barrier = pltpu.get_barrier_semaphore()

    def greet(k, carry):
        pl.semaphore_signal(barrier, inc=1, device_id=place(peer(me, k, n)), device_id_type=MESH)
        return carry

    loop(1, n, greet)
    loads = []

    def load(source, target):
        copy = pltpu.make_async_copy(source, target, in_sem.at[len(loads)])
        copy.start()
        loads.append(copy)
        return copy

    stores = []

    def store(source, target):
        copy = pltpu.make_async_copy(source, target, out_sem.at[len(stores)])
        copy.start()
        stores.append(copy)

    early = [
        load(feat_h, feat),
        load(weights_h.at[pl.ds(0, SQUARE)], w_first),
        load(weights_h.at[pl.ds(OFF_ATT_OUT, SLICE)], pos_first),
        load(nbrs_h, nbrs),
        load(coords_h, coords),
        load(valid_h, valid),
    ]

    late = [load(weights_h, weights), load(cot_h, cot)]
    for source, target in ((master_h, 0), (first_h, 1), (second_h, 2)):
        late.append(load(source, state[target]))
    owned[...] = jnp.zeros(owned.shape, f32)
    for copy in early:
        copy.wait()

    sent = []

    def all_sum(index, message):
        rows = message.shape[0]
        stat_send[index, 0:rows] = message
        stat_buf[index, me, 0:rows] = message

        def post(k, carry):
            pltpu.make_async_remote_copy(
                src_ref=stat_send.at[index, pl.ds(0, rows)],
                dst_ref=stat_buf.at[index, me, pl.ds(0, rows)],
                send_sem=stat_ssem.at[index],
                recv_sem=stat_rsem.at[index],
                device_id=place(peer(me, k, n)),
                device_id_type=MESH,
            ).start()
            return carry

        loop(1, n, post)
        sent.append((index, rows))

        def collect():
            span = stat_buf.at[index, pl.ds(0, n - 1), pl.ds(0, rows)]
            pltpu.make_async_copy(span, span, stat_rsem.at[index]).wait()
            return jnp.sum(stat_buf[index, :, 0:rows], axis=0)

        return collect

    sibling = (row_id, col_id + 1 - 2 * core)
    def put_halves(target, value):
        rows = SLICE_ROWS // 2
        for k in range(2):
            part = value[:, k * LANES : (k + 1) * LANES]
            target[:, :, k * rows : (k + 1) * rows] = part.reshape(per_matrix, 2, rows, LANES)

    def whole_rows(piece):
        rows = SLICE_ROWS // 2
        return jnp.concatenate([piece[0:rows], piece[rows:]], axis=1).reshape(SLICE_ROWS, LANES)

    def put_matrix(m, grad):
        at = (m - DENSE_FROM) * per_matrix
        put_halves(flat.at[at : at + per_matrix], grad)

    def swap(group, source, target):
        copy = pltpu.make_async_remote_copy(
            src_ref=source.at[:, 1 - core],
            dst_ref=target,
            send_sem=pair_ssem.at[group],
            recv_sem=pair_rsem.at[group],
            device_id=sibling,
            device_id_type=MESH,
        )
        copy.start()
        return copy

    def to_chips(begin, count, send):
        if count == half and begin % half == 0:

            def post(k, carry):
                other = peer(chip, k, half)
                send(begin + other, other)
                return carry

            loop(1, half, post)
        else:

            def post_any(k, carry):
                index = begin + k
                other = lax.rem(index, half)

                @pl.when(other != chip)
                def _():
                    send(index, other)

                return carry

            loop(0, count, post_any)

    def send_dense(copy, begin, count):
        copy.wait()
        own = pl.ds(begin - dense, count)
        part16[own] = (flat[own, core] + pair_got[own]).astype(bf16)

        def send(index, other):
            pltpu.make_async_remote_copy(
                src_ref=part16.at[index - dense],
                dst_ref=got16.at[index // half, chip],
                send_sem=rs_ssem.at[index // half],
                recv_sem=rs_rsem.at[index // half],
                device_id=place(2 * other + core),
                device_id_type=MESH,
            ).start()

        at = begin
        while at < begin + count:
            step = min(half - at % half, begin + count - at)
            to_chips(at, step, send)
            at = at + step

    def send_wide(copy, which):
        copy.wait()
        for k, piece in enumerate(split(first_f[which, :, core] + first_got[which], 2)):
            wide16[which, :, k] = piece

        def send(index, other):
            pltpu.make_async_remote_copy(
                src_ref=wide16.at[which, index],
                dst_ref=got_wide.at[which, chip],
                send_sem=wd_ssem.at[which],
                recv_sem=wd_rsem.at[which],
                device_id=place(2 * other + core),
                device_id_type=MESH,
            ).start()

        to_chips(0, per_matrix, send)

    def send_low(copy):
        copy.wait()
        low_sum[...] = low_f[:, core] + low_got[...]
        for kind in range(low_kinds):

            def send(index, other, kind=kind):
                pltpu.make_async_remote_copy(
                    src_ref=low_sum.at[index - (1 + kind) * per_matrix],
                    dst_ref=got_low.at[kind, chip],
                    send_sem=low_ssem.at[kind],
                    recv_sem=low_rsem.at[kind],
                    device_id=place(2 * other + core),
                    device_id_type=MESH,
                ).start()

            to_chips((1 + kind) * per_matrix, per_matrix, send)

    def drain_stats(index, rows):
        span = stat_buf.at[index, pl.ds(0, n - 1), pl.ds(0, rows)]
        pltpu.make_async_copy(span, span, stat_ssem.at[index]).wait()

    w_in = w_first[...].reshape(WIDTH, WIDTH)
    mats[0] = w_in
    w_in = mats[0]
    at = (OFF_TAIL - OFF_ATT_OUT) // LANES
    pos_in = pos_first[...].reshape(SLICE_ROWS, LANES).astype(f32)[at : at + 1]
    lane8 = iota((8, 1), 0)

    def pos_in_col(c):
        return jnp.where(lane8 < 3, row_to_col(pos_in[:, 3 * c : 3 * c + 8], 8), 0.0)

    valid_rows = valid[...].reshape(points // LANES, LANES).astype(f32)
    n_valid = jnp.sum(jnp.sum(valid_rows, axis=0, keepdims=True), axis=1, keepdims=True)
    point_mask = (iota((points, 1), 0).astype(f32) < n_valid).astype(f32)
    lane_mask = (iota((1, points), 1).astype(f32) < n_valid).astype(f32)

    a1 = nn(feat[...], w_in)
    a1_s[...] = a1
    masked = point_mask * a1
    sum_a, sqr_a = row_sum(masked), row_sum(masked * a1)

    weight = [[pos_in[:, 3 * c + d : 3 * c + d + 1] for d in range(3)] for c in range(3)]
    pos_one = [jnp.zeros((NEAREST, LANES), f32) for _ in range(3)]
    pos_two = [jnp.zeros((NEAREST, LANES), f32) for _ in range(3)]
    pairs_local = jnp.zeros((NEAREST, LANES), f32)
    for b in range(blocks):
        here = slice(b * LANES, (b + 1) * LANES)
        index = nbrs[:, here]
        tile, at = lax.shift_right_logical(index, 7), index & (LANES - 1)

        def fetch(c, t):
            row = jnp.broadcast_to(coords[c : c + 1, t * LANES : (t + 1) * LANES], index.shape)
            return jnp.take_along_axis(row, at, axis=1, mode="promise_in_bounds")

        r = []
        for c in range(3):
            near = fetch(c, b)
            if b > 0:
                near = jnp.where(tile < b, fetch(c, b - 1), near)
            if b < blocks - 1:
                near = jnp.where(tile > b, fetch(c, b + 1), near)
            r.append(near - coords[c : c + 1, here])
        pm = jnp.where(index.astype(f32) < n_valid, lane_mask[:, here], 0.0)
        pairs_local = pairs_local + pm
        for d in range(3):
            p = weight[0][d] * r[0] + weight[1][d] * r[1] + weight[2][d] * r[2]
            pos_one[d] = pos_one[d] + pm * p
            pos_two[d] = pos_two[d] + pm * p * p

    def total(value):
        return jnp.sum(row_sum(value), axis=1, keepdims=True)

    lane = iota((1, LANES), 1)
    last = jnp.where(lane == 16, n_valid, 0.0) + jnp.where(lane == 17, total(pairs_local), 0.0)
    for d in range(3):
        last = last + jnp.where(lane == d, total(pos_one[d]), 0.0)
        last = last + jnp.where(lane == 8 + d, total(pos_two[d]), 0.0)

    def fold(row):
        return jnp.concatenate([row[:, 0:LANES], row[:, LANES:WIDTH]], axis=0)

    def unfold(rows):
        return jnp.concatenate([rows[0:1], rows[1:2]], axis=1)

    pl.semaphore_wait(barrier, n - 1)
    collect_first = all_sum(0, jnp.concatenate([fold(sum_a), fold(sqr_a), last], axis=0))
    window_row = iota((WINDOW, LANES), 0)
    for b in range(blocks):
        for j in range(NEAREST):
            index = nbrs[j : j + 1, b * LANES : (b + 1) * LANES] - starts[b]
            onehot[b, 0:WINDOW, j * LANES : (j + 1) * LANES] = jnp.where(
                window_row == index, 1.0, 0.0
            ).astype(bf16)

    coords8 = jnp.concatenate([coords[...], jnp.zeros((5, points), f32)], axis=0)
    table = jnp.concatenate(
        split(coords8, 3) + [jnp.broadcast_to(lane_mask, (8, points)).astype(bf16)], axis=0
    )
    slot0 = (iota((1, PAIRS), 1) < LANES).astype(f32)
    pos_in_cols = [pos_in_col(c) for c in range(3)]
    for b in range(blocks):
        here = slice(b * LANES, (b + 1) * LANES)
        fetched = nn(table[:, starts[b] : starts[b] + WINDOW], onehot[b, 0:WINDOW])
        place_n = fetched[0:8] + fetched[8:16] + fetched[16:24]
        mask_n = fetched[24:32]
        r = place_n - tiles(coords8[:, here])
        pm = mask_n * tiles(lane_mask[:, here])
        p = pos_in_cols[0] * r[0:1] + pos_in_cols[1] * r[1:2] + pos_in_cols[2] * r[2:3]
        rel[b] = r
        pos[b] = p
        pmask[b] = pm
        allow[b] = jnp.maximum(mask_n, slot0)

    for copy in late:
        copy.wait()
    for m in range(1, 5):
        mats[m] = weights[pl.ds(m * SQUARE, SQUARE)].reshape(WIDTH, WIDTH)
    w_q, w_k, w_v, w_o = (mats[m] for m in range(1, 5))
    att_in = weights[pl.ds(OFF_ATT_IN, WIDTH * GROUPS)].reshape(WIDTH * GROUPS // LANES, LANES)
    att_in_f = att_in.astype(f32).reshape(WIDTH, GROUPS)
    att_in_t = att_in_f.T.astype(bf16)
    att_out_f = (
        weights[pl.ds(OFF_ATT_OUT, GROUPS * GROUPS)]
        .reshape(GROUPS * GROUPS // LANES, LANES)
        .astype(f32)
        .reshape(GROUPS, GROUPS)
    )
    att_out = att_out_f.astype(bf16)
    att_out_t = att_out_f.T.astype(bf16)
    tail1d[pl.ds(0, 1024)] = weights[pl.ds(OFF_TAIL, 1024)]
    rest = total_len - OFF_TAIL - 1024
    tail1d[pl.ds(1024, rest)] = weights[pl.ds(OFF_TAIL + 1024, rest)]
    tail = tail1d[pl.ds(0, TAIL_PAD)].reshape(TAIL_PAD // LANES, LANES).astype(f32)
    tail = jnp.concatenate([tail[k : k + 1] for k in range(TAIL_PAD // LANES)], axis=1)
    pos_rows = [tail[:, TAIL_POS_OUT + WIDTH * d : TAIL_POS_OUT + WIDTH * (d + 1)] for d in range(3)]
    def norm_pieces(start):
        ends = [0, WIDTH, WIDTH + 3, WIDTH + 3 + GROUPS, NORMS]
        return [tail[:, start + ends[k] : start + ends[k + 1]] for k in range(4)]

    gain_a, gain_p, gain_w, gain_o = norm_pieces(TAIL_GAINS)
    shift_a, shift_p, shift_w, shift_o = norm_pieces(TAIL_SHIFTS)

    def pad_col(row):
        wide = jnp.concatenate([row, jnp.zeros((1, 5), f32)], axis=1)
        return row_to_col(wide, 8)

    gain_p, shift_p = pad_col(gain_p), pad_col(shift_p)
    gain_w, shift_w = row_to_col(gain_w, GROUPS), row_to_col(shift_w, GROUPS)

    new_at = iota((WIDTH, WIDTH), 0)
    reorder = jnp.where(
        iota((WIDTH, WIDTH), 1) == new_at % GROUPS * PER_GROUP + new_at // GROUPS, 1.0, 0.0
    ).astype(bf16)
    w_o_new = nn(reorder, w_o)
    mats[4] = w_o_new.astype(bf16)
    mats[5] = w_o_new.T.astype(bf16)
    mats[6] = w_q.astype(f32).T.astype(bf16)
    mats[7] = w_k.astype(f32).T.astype(bf16)
    mats[8] = nt(reorder, w_v).astype(bf16)
    pos_mat = jnp.concatenate(pos_rows + [jnp.zeros((13, WIDTH), f32)], axis=0).astype(bf16)
    pos_cols = nt(reorder, pos_mat)
    pos_lanes = jnp.concatenate(
        [pos_cols[:, 0:8]] * 3 + [jnp.zeros((WIDTH, POS_ROWS - 24), f32)], axis=1
    ).astype(bf16)
    pos_cols = [pos_cols[:, d : d + 1] for d in range(3)]
    feat_f = feat[...].astype(f32)
    ft_s[...] = feat_f.T.astype(bf16)
    sum_f = row_sum(point_mask * feat_f)
    stats = collect_first()

    def pick(row, at):
        return jnp.sum(jnp.where(lane == at, row, 0.0), axis=1, keepdims=True)

    point_count, pair_count = pick(stats[4:5], 16), pick(stats[4:5], 17)
    inv_points, inv_pairs = 1.0 / point_count, 1.0 / pair_count

    def moments(total, square, inv):
        mean = total * inv
        return mean, lax.rsqrt(square * inv - mean * mean + bn_eps)

    mean_a, rs_a = moments(unfold(stats[0:2]), unfold(stats[2:4]), inv_points)
    mean_p, rs_p = moments(
        row_to_col(stats[4:5, 0:8], 8), row_to_col(stats[4:5, 8:16], 8), inv_pairs
    )

    h = silu_parts((a1_s[...] - mean_a) * rs_a * gain_a + shift_a)[0]
    h_s[...] = h.astype(bf16)
    h_t = h.T.astype(bf16)
    q_t = nn(mats[6], h_t).astype(bf16)
    k_t = nn(mats[7], h_t).astype(bf16)
    q_s[...] = q_t
    k_s[...] = k_t
    h_ts[...] = h_t
    pos_att = nt(att_in_t, pos_mat)
    enc_lanes = -jnp.concatenate(pos_rows + [jnp.zeros((5, WIDTH), f32)], axis=0).T
    enc_lanes = jnp.concatenate(
        [enc_lanes] * 3 + [jnp.zeros((WIDTH, POS_ROWS - 24), f32)], axis=1
    ).astype(bf16)
    back_att = jnp.concatenate([nn(att_in_t, mats[6]), nn(att_in_t, mats[7])], axis=0)
    back_split = split(back_att, 2)
    ba_s[...] = jnp.concatenate([back_split[0], back_split[0], back_split[1]], axis=0)

    sum_w = jnp.zeros((GROUPS, LANES), f32)
    sqr_w = jnp.zeros((GROUPS, LANES), f32)
    for b in range(blocks):
        here = slice(b * LANES, (b + 1) * LANES)
        active = silu_parts((pos[b] - mean_p) * rs_p * gain_p + shift_p)[0]
        act[b] = active
        pieces = [piece.astype(f32) for piece in split(active, 3)]
        onehot[b, WINDOW : WINDOW + POS_ROWS] = jnp.concatenate(
            pieces + [jnp.zeros((POS_ROWS - 24, PAIRS), f32)], axis=0
        ).astype(bf16)
        vgat[b] = nn(
            jnp.concatenate([k_s[:, starts[b] : starts[b] + WINDOW], enc_lanes], axis=1), onehot[b]
        )
        here_q = q_s[:, here].astype(f32)
        for j in range(NEAREST):
            at = slice(j * LANES, (j + 1) * LANES)
            xs[b, :, at] = (here_q - vgat[b, :, at]).astype(bf16)
        w = nn(att_in_t, xs[b])
        wpre[b] = w
        mw = w * pmask[b, 0:1]
        sum_w = sum_w + lane_fold(mw)
        sqr_w = sqr_w + lane_fold(mw * w)

    def pair_row(one, two):
        one = jnp.sum(one, axis=1, keepdims=True)
        two = jnp.sum(two, axis=1, keepdims=True)
        return col_to_row(one, 0) + col_to_row(two, GROUPS)

    collect_w = all_sum(1, jnp.concatenate([pair_row(sum_w, sqr_w), fold(sum_f)], axis=0))
    v_t = nn(mats[8], h_ts[...]).astype(bf16)
    for b in range(blocks):
        vgat[b] = nn(
            jnp.concatenate([v_t[:, starts[b] : starts[b] + WINDOW], pos_lanes], axis=1), onehot[b]
        )
    stats = collect_w()
    mean_f = stats[1:3] * inv_points
    mean_w, rs_w = moments(
        row_to_col(stats[0:1, 0:GROUPS], GROUPS),
        row_to_col(stats[0:1, GROUPS : 2 * GROUPS], GROUPS),
        inv_pairs,
    )

    def each_channel(value):
        return jnp.concatenate([value] * PER_GROUP, axis=0)

    def over_channels(value):
        return functools.reduce(
            jnp.add, [value[c * GROUPS : (c + 1) * GROUPS] for c in range(PER_GROUP)]
        )

    def cols(j):
        return slice(j * LANES, (j + 1) * LANES)

    for b in range(blocks):
        here = slice(b * LANES, (b + 1) * LANES)
        u = silu_parts((wpre[b] - mean_w) * rs_w * gain_w + shift_w)[0].astype(bf16)
        uact[b] = u
        logit = jnp.where(allow[b, 0:1] > 0.5, nn(att_out_t, u), masked_logit)
        top = logit[:, cols(0)]
        for j in range(1, NEAREST):
            top = jnp.maximum(top, logit[:, cols(j)])
        weight = jnp.exp(logit - tiles(top))
        share = 1.0 / functools.reduce(jnp.add, [weight[:, cols(j)] for j in range(NEAREST)])
        att[b] = weight * tiles(share)
        mixed = jnp.zeros((WIDTH, LANES), f32)
        for j in range(NEAREST):
            mixed = mixed + each_channel(att[b, :, cols(j)]) * vgat[b, :, cols(j)]
        o_s[here, :] = mixed.T.astype(bf16)

    z = nn(o_s[...], mats[4])
    z_s[...] = z
    masked = point_mask * z
    collect_o = all_sum(2, jnp.concatenate([fold(row_sum(masked)), fold(row_sum(masked * z))], axis=0))
    for k in range(2):
        mu_s[k * LANES : (k + 1) * LANES] = jnp.broadcast_to(
            row_to_col(mean_f[k : k + 1], LANES), (LANES, LANES)
        )

    def put_first(which, value):
        put_halves(first_f.at[which], value)
        return swap(which, first_f.at[which], first_got.at[which])

    def from_feat(value):
        return nn(
            jnp.concatenate([ft_s[...]] * 2, axis=1), jnp.concatenate(split(value, 2), axis=0)
        )

    ahat = (a1_s[...] - mean_a) * rs_a
    a1_s[...] = ahat
    ahat_pair = put_first(0, from_feat(point_mask * ahat))
    for b in range(blocks):
        what = (wpre[b] - mean_w) * rs_w
        wpre[b] = what
        y = what * gain_w + shift_w
        dyw[b] = silu_slope(y, silu_parts(y)[1])
    send_wide(ahat_pair, 0)
    o_ts[...] = nn(o_s[...], reorder).T.astype(bf16)
    for b in range(blocks):
        here = slice(b * LANES, (b + 1) * LANES)
        enc = [jnp.zeros((GROUPS, LANES), f32) for _ in range(3)]
        for j in range(NEAREST):
            a = att[b, :, cols(j)]
            for d in range(3):
                enc[d] = enc[d] + a * act[b, d : d + 1, cols(j)]
        bd_s[:, here] = jnp.concatenate(enc, axis=0)
    stats = collect_o()
    mean_o, rs_o = moments(unfold(stats[0:2]), unfold(stats[2:4]), inv_points)

    zhat = (z_s[...] - mean_o) * rs_o
    z_s[...] = zhat
    y = feat[...].astype(f32) + zhat * gain_o + shift_o
    value, gate = silu_parts(y)
    outs[0] = (point_mask * value).astype(bf16)
    store(outs.at[0], out_h)
    dy = point_mask * cot[...].astype(f32) * silu_slope(y, gate)
    dz_s[...] = dy
    shift_grad_o, gain_grad_o = row_sum(dy), row_sum(dy * zhat)
    collect_o = all_sum(3, jnp.concatenate([fold(shift_grad_o), fold(gain_grad_o)], axis=0))
    for b in range(blocks):
        phat = (pos[b] - mean_p) * rs_p
        pos[b] = phat
        y = phat * gain_p + shift_p
        slope_p[b] = silu_slope(y, silu_parts(y)[1])
    y = a1_s[...] * gain_a + shift_a
    slope_a[...] = silu_slope(y, silu_parts(y)[1])
    pos_row = jnp.zeros((1, LANES), f32)
    for c in range(3):
        with_hat, alone = jnp.zeros((8, 1), f32), jnp.zeros((8, 1), f32)
        for b in range(blocks):
            masked = pmask[b] * rel[b, c : c + 1]
            with_hat = with_hat + lane_sum(masked * pos[b])
            alone = alone + lane_sum(masked)
        pos_row = pos_row + col_to_row(with_hat, 64 + 8 * c) + col_to_row(alone, 88 + 8 * c)
    stats = collect_o()
    one, two = unfold(stats[0:2]) * inv_points, unfold(stats[2:4]) * inv_points
    dz = (gain_o * rs_o * (dz_s[...] - point_mask * (one + z_s[...] * two))).astype(bf16)
    dz16[...] = dz
    do_s[...] = nn(dz, mats[5]).T

    sum_w = jnp.zeros((GROUPS, LANES), f32)
    sqr_w = jnp.zeros((GROUPS, LANES), f32)
    for b in range(blocks):
        here = slice(b * LANES, (b + 1) * LANES)
        do = do_s[:, here]
        da = []
        for j in range(NEAREST):
            da.append(over_channels(do * vgat[b, :, cols(j)]))
        mean_da = functools.reduce(jnp.add, [da[j] * att[b, :, cols(j)] for j in range(NEAREST)])
        ds = jnp.concatenate(
            [att[b, :, cols(j)] * (da[j] - mean_da) for j in range(NEAREST)], axis=1
        ).astype(bf16)
        ds_s[b] = ds
        dy = nn(att_out, ds) * dyw[b]
        dyw[b] = dy
        sum_w = sum_w + lane_fold(dy)
        sqr_w = sqr_w + lane_fold(dy * wpre[b])

    back_w = pair_row(sum_w, sqr_w)
    collect_w = all_sum(4, back_w + pos_row)
    put_matrix(4, nn(o_ts[...], dz16[...]))
    o_flat, v_flat = pl.ds(per_matrix, per_matrix), pl.ds(0, per_matrix)
    o_pair = swap(2, flat.at[o_flat], pair_got.at[o_flat])
    add_groups = jnp.where(
        iota((8, 3 * GROUPS), 1) // GROUPS == iota((8, 3 * GROUPS), 0), 1.0, 0.0
    ).astype(bf16)
    dv_s[...] = jnp.zeros(dv_s.shape, f32)
    for b in range(blocks):
        here = slice(b * LANES, (b + 1) * LANES)
        do = do_s[:, here]
        for j in range(NEAREST):
            xs[b, :, cols(j)] = (each_channel(att[b, :, cols(j)]) * do).astype(bf16)
        mix = [
            (tiles(over_channels(do * pos_cols[d])) * att[b]).astype(bf16) for d in range(3)
        ]
        dmix[b] = nn(add_groups, jnp.concatenate(mix, axis=0))
        dv_s[pl.ds(starts[b], WINDOW)] += nt(onehot[b, 0:WINDOW], xs[b])
    dv = dv_s[...].astype(bf16)
    dv_s[...] = nn(dv, mats[8])
    put_matrix(3, nn(h_ts[...], nn(dv, reorder).astype(bf16)))
    v_pair = swap(5, flat.at[v_flat], pair_got.at[v_flat])
    send_dense(o_pair, dense + per_matrix, per_matrix)
    send_dense(v_pair, dense, per_matrix)
    stats = collect_w()
    one = row_to_col(stats[:, 0:GROUPS], GROUPS) * inv_pairs
    two = row_to_col(stats[:, GROUPS : 2 * GROUPS], GROUPS) * inv_pairs
    pos_hat = [row_to_col(stats[:, 64 + 8 * c : 72 + 8 * c], 8) for c in range(3)]
    pos_alone = [row_to_col(stats[:, 88 + 8 * c : 96 + 8 * c], 8) for c in range(3)]

    sk_s[...] = jnp.zeros(sk_s.shape, f32)
    pos_att_rows = split(pos_att[:, 0:8].T, 3)
    pos_att_rows = jnp.concatenate(pos_att_rows, axis=0)
    dw_sums = []
    for b in range(blocks):
        dw = (gain_w * rs_w * (dyw[b] - pmask[b, 0:1] * (one + wpre[b] * two))).astype(bf16)
        sk_s[pl.ds(starts[b], WINDOW)] += nt(onehot[b, 0:WINDOW], dw)
        dw_sums.append(lane_slots(dw.astype(f32)))
        dw_s[b] = dw
    dq_att = jnp.concatenate(dw_sums, axis=1)
    both_att = jnp.concatenate([dq_att.T, -sk_s[...]], axis=1)
    both_split = split(both_att, 2)
    dh = nn(jnp.concatenate(both_split + both_split[0:1], axis=1), ba_s[...]) + dv_s[...]
    dy = dh * slope_a[...]
    z_s[...] = dy
    shift_grad_a = row_sum(dy)
    away = jnp.concatenate(
        [mu_s[...] * shift_grad_a[:, k * LANES : (k + 1) * LANES] for k in range(2)], axis=1
    )
    first_pair = put_first(1, from_feat(dy) - away)
    low = nn(
        jnp.concatenate([h_ts[...]] * 2, axis=1), jnp.concatenate(both_split, axis=0)
    )
    low_f[...] = low.reshape(per_matrix, 2, LOW_ROWS, LANES)
    low_pair = swap(3, low_f, low_got)
    along = [jnp.zeros((8, 1), f32) for _ in range(3)]
    sum_p = jnp.zeros((8, 1), f32)
    sqr_p = jnp.zeros((8, 1), f32)
    for b in range(blocks):
        back = nn(pos_att_rows, dw_s[b])
        d_act = dmix[b] + back[0:8] + back[8:16] + back[16:24]
        dy = d_act * slope_p[b]
        sum_p = sum_p + lane_sum(dy)
        sqr_p = sqr_p + lane_sum(dy * pos[b])
        for c in range(3):
            along[c] = along[c] + lane_sum(dy * rel[b, c : c + 1])
    gain_grad_a = row_sum(z_s[...] * a1_s[...])
    last = col_to_row(sum_p, 0) + col_to_row(sqr_p, 8)
    for c in range(3):
        last = last + col_to_row(along[c], 16 + 8 * c)
    collect_a = all_sum(
        5, jnp.concatenate([fold(shift_grad_a), fold(gain_grad_a), last], axis=0)
    )
    send_wide(first_pair, 1)
    send_low(low_pair)

    d_att_out = sum(nt(uact[b], ds_s[b]) for b in range(blocks))
    d_pos_att = sum(
        nt(jnp.concatenate(split(act[b], 3), axis=0), dw_s[b]) for b in range(blocks)
    )
    d_pos_att = d_pos_att[0:8] + d_pos_att[8:16] + d_pos_att[16:24]
    d_pos_split = split(d_pos_att, 3)
    d_att_in = sum(
        nn(q_s[...], piece[:, 0:GROUPS]) + nn(k_s[...], piece[:, GROUPS : 2 * GROUPS])
        for piece in both_split
    )
    d_att_in = d_att_in + sum(tn(pos_mat[0:8], piece) for piece in d_pos_split)
    d_pos_out = sum(nn(piece, att_in_t) for piece in d_pos_split)
    do_split = split(do_s[...], 2)
    bd_split = split(bd_s[...], 2)
    cross = nt(bd_split[0], do_split[0]) + nt(bd_split[0], do_split[1]) + nt(bd_split[1], do_split[0])
    own_group = iota((GROUPS, WIDTH), 1) % GROUPS == iota((GROUPS, WIDTH), 0)
    cross = [
        row_sum(jnp.where(own_group, cross[d * GROUPS : (d + 1) * GROUPS], 0.0)) for d in range(3)
    ]
    cross = jnp.concatenate(cross + [jnp.zeros((5, WIDTH), f32)], axis=0)
    d_pos_out = d_pos_out + sum(nn(piece, reorder) for piece in split(cross, 3))
    d_pos_rows = [d_pos_out[d : d + 1] for d in range(3)]
    pieces = [jnp.zeros((1, TAIL_POS_OUT), f32)] + d_pos_rows
    pieces = pieces + [
        gain_grad_a, col_to_row(sqr_p, 0)[:, 0:3], back_w[:, GROUPS : 2 * GROUPS], gain_grad_o,
        shift_grad_a, col_to_row(sum_p, 0)[:, 0:3], back_w[:, 0:GROUPS], shift_grad_o,
        jnp.zeros((1, TAIL_PAD - TAIL_USED), f32),
    ]
    small = 5 * per_matrix
    used_rows = OFF_TAIL // LANES + TAIL_PAD // LANES - 5 * SQUARE // LANES
    spare_rows = (sliced - small) * 2 * SLICE_ROWS - used_rows
    pieces_rows = [
        d_att_in.reshape(WIDTH * GROUPS // LANES, LANES),
        d_att_out.reshape(GROUPS * GROUPS // LANES, LANES),
        jnp.concatenate(pieces, axis=1).reshape(TAIL_PAD // LANES, LANES),
        jnp.zeros((spare_rows, LANES), f32),
    ]
    flat[small - dense : sliced - dense] = jnp.concatenate(pieces_rows, axis=0).reshape(
        sliced - small, 2, SLICE_ROWS, LANES
    )
    small_flat = pl.ds(small - dense, sliced - small)
    small_pair = swap(4, flat.at[small_flat], pair_got.at[small_flat])
    send_dense(small_pair, small, sliced - small)

    begin = me * shard_len
    lead, skip = lax.rem(begin, CHUNK), lax.rem(begin, LANES)
    shard_at = pl.ds(lead // LANES, shard_rows)
    lanes_all = iota((shard_rows, LANES), 1)
    inside = iota((shard_rows, LANES), 0) * LANES + lanes_all < shard_len
    main = shard_len // 1024 * 1024
    parts = [pl.ds(at, size) for at, size in ((0, main), (main, shard_len - main)) if size]
    for k in range(3):
        for at in parts:
            tail_g[at] = state[k][at]
        rows = jnp.where(inside, tail_g[...].reshape(shard_rows, LANES), 0.0)
        turned = pltpu.roll(rows, skip, 1)
        above = pltpu.roll(turned, 1, 0)
        slab_f[k] = jnp.zeros(slab_f.shape[1:], f32)
        slab_f[k, shard_at, :] = jnp.where(lanes_all < skip, above, turned)

    stats = collect_a()
    one_a, two_a = unfold(stats[0:2]) * inv_points, unfold(stats[2:4]) * inv_points
    def halves(row):
        return jnp.concatenate(
            [
                jnp.broadcast_to(row[:, k * LANES : (k + 1) * LANES], (SLICE_ROWS // 2, LANES))
                for k in range(2)
            ],
            axis=0,
        )

    scale_tile, two_tile = halves(gain_a * rs_a), halves(two_a)
    one = row_to_col(stats[4:5, 0:8], 8) * inv_pairs
    two = row_to_col(stats[4:5, 8:16], 8) * inv_pairs
    pos_in_row = jnp.zeros((1, LANES), f32)
    for c in range(3):
        moved = row_to_col(stats[4:5, 16 + 8 * c : 24 + 8 * c], 8)
        moved = gain_p * rs_p * (moved - one * pos_alone[c] - two * pos_hat[c])
        pos_in_row = pos_in_row + col_to_row(moved, 3 * c)

    def slice_of(slot):
        return 2 * (slot * half + chip) + core

    def when_in(slot, low, high, act_on):
        if (slot + 1) * n <= low or slot * n >= high:
            return
        if slot * n >= low and (slot + 1) * n <= high:
            act_on()
        else:
            number = slice_of(slot)
            pl.when((number >= low) & (number < high))(act_on)

    def others_sum(total, part):
        def add(k, total):
            return total + part(peer(chip, k, half))

        return lax.fori_loop(1, half, add, total, unroll=half <= 16)

    def take_wide(which):
        got = got_wide.at[which, pl.ds(0, half - 1)]
        pltpu.make_async_copy(got, got, wd_rsem.at[which]).wait()
        index = lax.rem(chip, per_matrix)

        def part(other):
            return got_wide[which, other, 0].astype(f32) + got_wide[which, other, 1].astype(f32)

        return others_sum(first_f[which, index, core] + first_got[which, index], part)

    def take_low(kind):
        got = got_low.at[kind, pl.ds(0, half - 1)]
        pltpu.make_async_copy(got, got, low_rsem.at[kind]).wait()
        index = lax.rem(chip, per_matrix)
        return others_sum(low_sum[index], lambda other: got_low[kind, other])

    def low_product(factor, which):
        factor = factor.reshape(SLICE // WIDTH, 2 * GROUPS)[:, which * GROUPS : (which + 1) * GROUPS]
        return sum(nn(piece, att_in_t) for piece in split(factor, 2)).reshape(SLICE_ROWS, LANES)

    squares = jnp.zeros((SLICE_ROWS, LANES), f32)
    matrix = SQUARE // SLICE
    for slot in range(slots):
        sums[slot] = jnp.zeros((SLICE_ROWS, LANES), f32)

    def take_dense(in_order, slot):
        index = slot * half + chip
        got = got16.at[slot, pl.ds(0, half - 1)]
        pltpu.make_async_copy(got, got, rs_rsem.at[slot]).wait()
        total = flat[index - dense, core] + pair_got[index - dense]
        total = others_sum(total, lambda other: got16[slot, other].astype(f32))
        sums[slot] = total if in_order else whole_rows(total)

    def take_hat():
        hat_s[...] = two_tile * take_wide(0)

    def first(slot):
        sums[slot] = whole_rows(scale_tile * (take_wide(1) - hat_s[...]))

    def add_pos_in(slot):
        at_row = iota((SLICE_ROWS, LANES), 0) == OFF_TAIL % SLICE // LANES
        sums[slot] += jnp.where(at_row, pos_in_row, 0.0)

    def each_slot(low, high, act_on):
        for slot in range(slots):
            when_in(slot, low, high, functools.partial(act_on, slot))

    each_slot(DENSE_FROM * matrix, 5 * matrix, functools.partial(take_dense, False))
    each_slot(0, matrix, lambda slot: take_hat())
    each_slot(0, matrix, first)
    for kind in range(low_kinds):
        kinds = range(2) if low_kinds == 1 else (kind,)

        def fill(kind=kind, kinds=kinds):
            factor = take_low(kind)
            for which in kinds:
                for slot in range(slots):

                    def product(slot=slot, which=which):
                        sums[slot] = low_product(factor, which)

                    when_in(slot, (1 + which) * matrix, (2 + which) * matrix, product)

        if low_kinds == 1:
            fill()
        else:
            when_in(0, (1 + kind) * matrix, (2 + kind) * matrix, fill)
    each_slot(5 * matrix, 2 * sliced, functools.partial(take_dense, True))
    each_slot(OFF_TAIL // SLICE, OFF_TAIL // SLICE + 1, add_pos_in)
    for slot in range(slots):
        squares = squares + sums[slot] * sums[slot]
    squares = total(squares)

    collect_norm = all_sum(6, jnp.where(lane == 0, squares, 0.0))

    def each_owner(slot, act_on):
        number = slice_of(slot)
        low = number * SLICE // shard_len
        high = jnp.minimum((number * SLICE + SLICE - 1) // shard_len, n - 1)
        for side in range(sides):
            owner = low + side

            @pl.when((number * SLICE < total_len) & (owner <= high))
            def _(owner=owner, side=side):
                act_on(owner, number - owner * shard_len // SLICE, side)

    def owned_rows(k):
        return owned.at[pl.ds(pl.multiple_of(k * SLICE_ROWS, SLICE_ROWS), SLICE_ROWS)]

    def own_copy(slot, owner, k, side):
        return pltpu.make_async_remote_copy(
            src_ref=sums.at[slot],
            dst_ref=owned_rows(k),
            send_sem=own_ssem.at[slot, side],
            recv_sem=own_rsem.at[k],
            device_id=place(owner),
            device_id_type=MESH,
        )

    for slot in range(slots):

        def hand_over(owner, k, side, slot=slot):
            @pl.when(owner != me)
            def _():
                own_copy(slot, owner, k, side).start()

            @pl.when(owner == me)
            def _():
                owned_rows(k)[...] = sums[slot]

        each_owner(slot, hand_over)

    first_slice = begin // SLICE
    last_slice = (begin + shard_len - 1) // SLICE
    for k in range(span):
        number = first_slice + k

        @pl.when((number <= last_slice) & (lax.rem(number, n) != me))
        def _(k=k):
            rows = owned.at[pl.ds(k * SLICE_ROWS, SLICE_ROWS)]
            pltpu.make_async_copy(rows, rows, own_rsem.at[k]).wait()

    slab_shape = slab_f.shape[1:]
    flat_at = iota(slab_shape, 0) * LANES + iota(slab_shape, 1) - lead
    grad = owned[pl.ds((begin - lead - first_slice * SLICE) // LANES, slab_shape[0]), :]
    grad = jnp.where((flat_at >= 0) & (flat_at < shard_len), grad, 0.0)

    stats = collect_norm()
    norm = jnp.sqrt(pick(stats, 0))
    grad = grad * jnp.minimum(1.0, clip_norm / norm)
    updated = adam(slab_f[0], slab_f[1], slab_f[2], grad)
    shard_w[...] = updated[0].astype(bf16)
    all_w[core, chip] = updated[0].astype(bf16)
    norm_s[...] = jnp.broadcast_to(norm, norm_s.shape)

    in_row = n_cols // 2
    row_chip = col_id // 2

    def send_slab(source, slab, row, chip_in_row):
        pltpu.make_async_remote_copy(
            src_ref=source,
            dst_ref=all_w.at[core, slab],
            send_sem=ag_ssem,
            recv_sem=ag_rsem.at[slab],
            device_id=(row, 2 * chip_in_row + core),
            device_id_type=MESH,
        ).start()

    def forward(other):
        pltpu.make_async_remote_copy(
            src_ref=all_w.at[core, other],
            dst_ref=all_w.at[core, other],
            send_sem=fw_ssem,
            recv_sem=fw_rsem,
            device_id=sibling,
            device_id_type=MESH,
        ).start()

    def arrived(other):
        pltpu.make_async_copy(shard_w, shard_w, ag_rsem.at[other]).wait()

    def send_along(k, carry):
        send_slab(shard_w, chip, peer(row_id, k, n_rows), row_chip)
        return carry

    def send_within(k, carry):
        send_slab(shard_w, chip, row_id, peer(row_chip, k, in_row))
        return carry

    loop(1, n_rows, send_along)
    loop(1, in_row, send_within)
    forward(chip)
    store(norm_s, gnorm_h)
    for k in range(3):
        slab_f[k] = updated[k]
        turned = pltpu.roll(slab_f[k, shard_at, :], lax.rem(LANES - skip, LANES), 1)
        below = pltpu.roll(turned, shard_rows - 1, 0)
        tail_g[...] = jnp.where(lanes_all < LANES - skip, turned, below).reshape(shard_rows * LANES)
        for at in parts:
            news[k][at] = tail_g[at]
    for source, target in ((0, new_master_h), (1, new_first_h), (2, new_second_h)):
        store(news[source], target)

    da1 = (gain_a * rs_a * (z_s[...] - point_mask * (one_a + a1_s[...] * two_a))).astype(bf16)
    outs[1] = (dz_s[...] + nt(da1, w_in)).astype(bf16)
    store(outs.at[1], gfeat_h)
    for index, rows in sent:
        drain_stats(index, rows)

    def drain(low, high, slices, sem):
        if high - low == half:
            rest = slices.at[pl.ds(0, half - 1)]
            pltpu.make_async_copy(rest, rest, sem).wait()
        else:
            inside = (chip >= low) & (chip < high)

            def wait_one(k, carry):
                pltpu.make_async_copy(slices.at[0], slices.at[0], sem).wait()
                return carry

            lax.fori_loop(0, high - low - inside.astype(jnp.int32), wait_one, 0)

    for which in range(2):
        drain(0, per_matrix, got_wide.at[which], wd_ssem.at[which])
    for kind in range(low_kinds):
        low_at = (1 + kind) * per_matrix % half
        drain(low_at, low_at + per_matrix, got_low.at[kind], low_ssem.at[kind])
    for slot in range(slots):
        low_at = max(dense - slot * half, 0)
        high_at = min(sliced - slot * half, half)
        if high_at > low_at:
            drain(low_at, high_at, got16.at[slot], rs_ssem.at[slot])

        def own_drain(owner, k, side, slot=slot):
            @pl.when(owner != me)
            def _():
                own_copy(slot, owner, k, side).wait_send()

        each_owner(slot, own_drain)
    for copy in stores:
        copy.wait()

    def spread_row(k, carry):
        other = peer(row_id, n_rows - k, n_rows) * in_row + row_chip
        arrived(other)

        def send_on(i, carry):
            send_slab(all_w.at[core, other], other, row_id, peer(row_chip, i, in_row))
            return carry

        loop(1, in_row, send_on)
        forward(other)
        return carry

    loop(1, n_rows, spread_row)

    def pass_on(k, carry):
        step = k // (in_row - 1)
        row = jnp.where(step == 0, row_id, peer(row_id, n_rows - step, n_rows))
        other = row * in_row + peer(row_chip, in_row - 1 - lax.rem(k, in_row - 1), in_row)
        arrived(other)
        forward(other)
        return carry

    loop(0, n_rows * (in_row - 1), pass_on)
    pltpu.make_async_copy(all_w.at[core], all_w.at[core], fw_rsem).wait()
    rows = CHUNK // LANES

    def chunk(c):
        value = None
        last_owner = min((c * CHUNK + CHUNK - 1) // shard_len, n - 1)
        for owner in range(c * CHUNK // shard_len, last_owner + 1):
            k = c - owner * shard_len // CHUNK
            part = all_w[owner % 2, owner // 2, rows * k : rows * (k + 1)].astype(f32)
            value = part if value is None else value + part
        return value

    whole = total_len // (2 * CHUNK)
    for c in range(whole):
        both = jnp.concatenate([chunk(2 * c), chunk(2 * c + 1)], axis=0)
        weights_out[pl.ds(2 * CHUNK * c, 2 * CHUNK)] = both.astype(bf16).reshape(2 * CHUNK)
    left = total_len - whole * 2 * CHUNK
    if left:
        parts = [chunk(2 * whole)]
        parts.append(chunk(2 * whole + 1) if left > CHUNK else jnp.zeros((rows, LANES), f32))
        both = jnp.concatenate(parts, axis=0).astype(bf16).reshape(2 * CHUNK)
        weights_out[pl.ds(2 * CHUNK * whole, left)] = both[0:left]

    pltpu.make_async_copy(all_w.at[core], all_w.at[core], fw_ssem).wait()
    rest = all_w.at[core, pl.ds(0, half - 1)]
    pltpu.make_async_copy(rest, rest, ag_ssem).wait()


def finish_kernel(
    out_t, gfeat_t, gnorm_t, master_t, first_t, second_t, weights_t,
    out_h, gfeat_h, gnorm_h, master_h, first_h, second_h, weights_h,
    norm_s, gnorm, sem,
):
    copies = [
        pltpu.make_async_copy(source, target, sem.at[k])
        for k, (source, target) in enumerate(
            (
                (weights_t, weights_h),
                (out_t, out_h),
                (gfeat_t, gfeat_h),
                (master_t, master_h),
                (first_t, first_h),
                (second_t, second_h),
                (gnorm_t, norm_s),
            )
        )
    ]
    for copy in copies:
        copy.start()
    copies[-1].wait()
    gnorm[...] = norm_s[0:1, 0:1]
    copies[-1] = pltpu.make_async_copy(gnorm, gnorm_h, sem.at[len(copies)])
    copies[-1].start()
    for copy in copies:
        copy.wait()


def lane_slots(value):
    return functools.reduce(
        jnp.add, [value[:, j * LANES : (j + 1) * LANES] for j in range(NEAREST)]
    )


def shards(
    n_rows, n_cols,
    features, coords, valid_mask, neighbors, cotangent, weights, master, first_moment, second_moment,
):
    n = n_rows * n_cols
    half = n // 2
    points = features.shape[0]
    blocks = points // LANES
    shard_len = master.shape[0]
    total_len = weights.shape[0]

    def up(value, unit):
        return -(-value // unit) * unit

    shard_rows = up(-(-shard_len // LANES) + 1, 8)
    slab_rows = up(shard_rows + CHUNK // LANES, 16)
    sliced = up(-(-total_len // SLICE), 2) // 2
    slots = -(-sliced // half)
    per_matrix = SQUARE // SLICE // 2
    dense_pairs = sliced - DENSE_FROM * per_matrix
    low_kinds = 1 if per_matrix % half == 0 else 2
    sides = (SLICE + shard_len - 2) // shard_len + 1
    span = (SLICE + shard_len - 2) // SLICE + 1
    hbm = pl.BlockSpec(memory_space=pltpu.HBM)
    vmem = pl.BlockSpec(memory_space=pltpu.VMEM)
    dma = pltpu.SemaphoreType.DMA
    shape = jax.ShapeDtypeStruct

    def pairs(rows, dtype=f32):
        return pltpu.VMEM((blocks, rows, PAIRS), dtype)

    def shard():
        return [pltpu.VMEM(master.shape, f32) for _ in range(3)]

    scratch = [
        pltpu.VMEM(features.shape, bf16),
        pltpu.VMEM(coords.shape, f32),
        pltpu.VMEM(valid_mask.shape, jnp.int32),
        pltpu.VMEM(neighbors.shape, jnp.int32),
        pltpu.VMEM(features.shape, bf16),
        pltpu.VMEM((SQUARE,), bf16),
        pltpu.VMEM((SLICE,), bf16),
        pltpu.VMEM(weights.shape, bf16),
        shard(),
        shard(),
        pltpu.VMEM((2, *features.shape), bf16),
        pltpu.VMEM((1, LANES), f32),
        dma((11,)),
        dma((7,)),
        pltpu.VMEM((7, 8, LANES), f32),
        pltpu.VMEM((7, n, 8, LANES), f32),
        dma((7,)),
        dma((7,)),
        pltpu.VMEM((TAIL_PAD,), bf16),
        pltpu.VMEM((9, WIDTH, WIDTH), bf16),
        pairs(WINDOW + POS_ROWS, bf16),
        pairs(WIDTH),
        pairs(GROUPS),
        pairs(GROUPS),
        pairs(GROUPS, bf16),
        pairs(GROUPS),
        pairs(8),
        pairs(8),
        pairs(8),
        pairs(8),
        pairs(8),
        pairs(8),
        pltpu.VMEM((WIDTH, points), bf16),
        pltpu.VMEM((points, WIDTH), f32),
        pairs(8),
        pltpu.VMEM((points, WIDTH), f32),
        pltpu.VMEM((points, WIDTH), f32),
        pltpu.VMEM((points, WIDTH), bf16),
        pltpu.VMEM((WIDTH, points), bf16),
        pltpu.VMEM((WIDTH, points), bf16),
        pltpu.VMEM((WIDTH, points), bf16),
        pltpu.VMEM((6 * GROUPS, WIDTH), bf16),
        pltpu.VMEM((points, WIDTH), bf16),
        pltpu.VMEM((WIDTH, points), bf16),
        pltpu.VMEM((WIDTH, points), f32),
        pltpu.VMEM((points, WIDTH), f32),
        pltpu.VMEM((points, GROUPS), f32),
        pltpu.VMEM((3 * GROUPS, points), f32),
        pairs(GROUPS, bf16),
        pairs(GROUPS, bf16),
        pairs(WIDTH, bf16),
        pltpu.VMEM((points, WIDTH), f32),
        pltpu.VMEM((points, WIDTH), bf16),
        pltpu.VMEM((WIDTH, LANES), f32),
        pltpu.VMEM((dense_pairs, 2, SLICE_ROWS, LANES), f32),
        pltpu.VMEM((dense_pairs, SLICE_ROWS, LANES), f32),
        pltpu.VMEM((dense_pairs, SLICE_ROWS, LANES), bf16),
        pltpu.VMEM((slots, half, SLICE_ROWS, LANES), bf16),
        pltpu.VMEM((2, per_matrix, 2, SLICE_ROWS, LANES), f32),
        pltpu.VMEM((2, per_matrix, SLICE_ROWS, LANES), f32),
        pltpu.VMEM((2, per_matrix, 2, SLICE_ROWS, LANES), bf16),
        pltpu.VMEM((2, half, 2, SLICE_ROWS, LANES), bf16),
        pltpu.VMEM((per_matrix, 2, LOW_ROWS, LANES), f32),
        pltpu.VMEM((per_matrix, LOW_ROWS, LANES), f32),
        pltpu.VMEM((per_matrix, LOW_ROWS, LANES), f32),
        pltpu.VMEM((low_kinds, half, LOW_ROWS, LANES), f32),
        pltpu.VMEM((SLICE_ROWS, LANES), f32),
        pltpu.VMEM((slots, SLICE_ROWS, LANES), f32),
        pltpu.VMEM((up(max(span * SLICE_ROWS, CHUNK // LANES + slab_rows), SLICE_ROWS), LANES), f32),
        pltpu.VMEM((shard_rows * LANES,), f32),
        pltpu.VMEM((3, slab_rows, LANES), f32),
        pltpu.VMEM((slab_rows, LANES), bf16),
        pltpu.VMEM((2, half, slab_rows, LANES), bf16),
        dma((6,)),
        dma((6,)),
        dma((slots,)),
        dma((slots,)),
        dma((2,)),
        dma((2,)),
        dma((low_kinds,)),
        dma((low_kinds,)),
        dma((slots, sides)),
        dma((span,)),
        dma,
        dma((half,)),
        dma,
        dma,
    ]
    results = pl.pallas_call(
        functools.partial(block_kernel, n_rows, n_cols),
        out_shape=(
            shape(features.shape, bf16),
            shape(features.shape, bf16),
            shape((1, LANES), f32),
            shape(master.shape, f32),
            shape(master.shape, f32),
            shape(master.shape, f32),
            pltpu.VMEM(weights.shape, bf16),
        ),
        in_specs=[hbm] * 9,
        out_specs=[pl.BlockSpec(memory_space=pl.ANY)] * 6 + [vmem],
        scratch_shapes=scratch,
        compiler_params=pltpu.CompilerParams(
            collective_id=0, has_side_effects=True, vmem_limit_bytes=48 * 2**20
        ),
    )(*(pltpu.with_memory_space_constraint(x, pltpu.HBM) for x in (features, coords, valid_mask, neighbors, cotangent, weights, master, first_moment, second_moment)))
    results = pl.pallas_call(
        finish_kernel,
        out_shape=(
            shape(features.shape, bf16),
            shape(features.shape, bf16),
            shape((1, 1), f32),
            shape(master.shape, f32),
            shape(master.shape, f32),
            shape(master.shape, f32),
            shape(weights.shape, bf16),
        ),
        in_specs=[pl.BlockSpec(memory_space=pl.ANY)] * 7,
        out_specs=[hbm] * 7,
        scratch_shapes=[pltpu.VMEM((1, LANES), f32), pltpu.VMEM((1, 1), f32), dma((8,))],
        compiler_params=pltpu.CompilerParams(vmem_limit_bytes=8 * 2**20),
    )(*results)
    return results[0], results[1], results[2].reshape(()), *results[3:]


def solution(mesh):
    both = ("rows", "cols")
    rows_split, cols_split, flat_split = P(both, None), P(None, both), P(both)
    return jax.shard_map(
        functools.partial(shards, mesh.shape["rows"], mesh.shape["cols"]),
        mesh=mesh,
        in_specs=(
            rows_split, cols_split, flat_split, cols_split, rows_split, P(),
            flat_split, flat_split, flat_split,
        ),
        out_specs=(rows_split, rows_split, P(), flat_split, flat_split, flat_split, P()),
        check_vma=False,
    )
```
